32 devices in a mesh: expert: 16 (over z, y, x), shard: 2 (over core).
Axes of the slice: x: 2, y: 2, z: 4, core: 2. Of those that a mesh axis runs over, the one named last changes fastest.
Arguments:
- tokens: bfloat16 [4096, 2048], P(('expert', 'shard')), may hold values from -6 to 6
- segment_ids: int32 [4096], P('expert'), may hold values from 0 to 2, as said below
- routes: int32 [4096, 6], P(('expert', 'shard')), may hold values from 0 to 15, all different within a row; in each aligned block of 128 rows (0 to 127, 128 to 255, ...) at most 64 rows name the same one
- cotangent: bfloat16 [4096, 2048], P(('expert', 'shard')), may hold values from -6 to 6
- gain_attn: bfloat16 [2048], P('shard'), may hold values from 0.5 to 1.5
- gain_query: bfloat16 [1536], P('shard'), may hold values from 0.5 to 1.5
- gain_latent: bfloat16 [512], P('shard'), may hold values from 0.5 to 1.5
- gain_ffn: bfloat16 [2048], P('shard'), may hold values from 0.5 to 1.5
- w_qa: bfloat16 [2048, 1536], P('shard'), may hold values from -0.125 to 0.125
- w_qb: bfloat16 [1536, 3072], P('shard'), may hold values from -0.15625 to 0.15625
- w_kva: bfloat16 [2048, 576], P('shard'), may hold values from -0.125 to 0.125
- w_kvb: bfloat16 [512, 4096], P('shard'), may hold values from -0.25 to 0.25
- w_out: bfloat16 [2048, 2048], P('shard'), may hold values from -0.5 to 0.5
- w_router: bfloat16 [2048, 16], P('shard'), may hold values from -0.06591797 to 0.06591797
- shared_gate: bfloat16 [2048, 2816], P(None, 'shard'), may hold values from -0.125 to 0.125
- shared_up: bfloat16 [2048, 2816], P(None, 'shard'), may hold values from -0.125 to 0.125
- shared_down: bfloat16 [2816, 2048], P('shard'), may hold values from -0.109375 to 0.109375
- expert_gate: bfloat16 [16, 2048, 1408], P('expert', None, 'shard'), may hold values from -0.125 to 0.125
- expert_up: bfloat16 [16, 2048, 1408], P('expert', None, 'shard'), may hold values from -0.125 to 0.125
- expert_down: bfloat16 [16, 1408, 2048], P('expert', 'shard'), may hold values from -0.15625 to 0.15625
Outputs:
- result: float32 [4096, 2048], P(('expert', 'shard'))
- grad_tokens: float32 [4096, 2048], P(('expert', 'shard'))
- grad_gain_attn: float32 [2048], P('shard')
- grad_gain_query: float32 [1536], P('shard')
- grad_gain_latent: float32 [512], P('shard')
- grad_gain_ffn: float32 [2048], P('shard')
- grad_w_qa: float32 [2048, 1536], P('shard')
- grad_w_qb: float32 [1536, 3072], P('shard')
- grad_w_kva: float32 [2048, 576], P('shard')
- grad_w_kvb: float32 [512, 4096], P('shard')
- grad_w_out: float32 [2048, 2048], P('shard')
- grad_w_router: float32 [2048, 16], P('shard')
- grad_shared_gate: float32 [2048, 2816], P(None, 'shard')
- grad_shared_up: float32 [2048, 2816], P(None, 'shard')
- grad_shared_down: float32 [2816, 2048], P('shard')
- grad_expert_gate: float32 [16, 2048, 1408], P('expert', None, 'shard')
- grad_expert_up: float32 [16, 2048, 1408], P('expert', None, 'shard')
- grad_expert_down: float32 [16, 1408, 2048], P('expert', 'shard')
The draws below stay inside these ranges and needn't reach their ends.
Inputs may be any that keep to these rules, and one draw needn't show every extreme that they name: `segment_ids`: each group of 256 consecutive tokens holds three sequences numbered 0, 1, 2 in order; sequence 1 starts within the group's first 128 tokens and ends within its last 128. `routes`: each token names 6 different experts; among the 128 tokens of one device no expert is named by more than 64 tokens, a bound that some block reaches.
All inputs are finite; a program needn't handle non-finite values.
Results may differ from the reference program's by a relative error of at most 0.025.
Values may be sent and summed in bfloat16 or wider, within the bound.
No kernel may reach another device: no remote copies, remote signals or barrier semaphores. Data moves between devices by JAX's collectives and lax.ppermute only.
A program may use at most 448 MiB of HBM per device.

```python
import math
import jax
import jax.numpy as jnp
import numpy as np
from jax import lax

MODEL_WIDTH = 2048
H = 16
DN = 128
DR = 64
DV = 128
QR = 1536
KR = 512
FE = 1408
TOP = 6
TOK_DEV = 128
FS = 2816
EXPERTS = 16
GROUP_TOK = 256
TOKENS = 4096
CAP = 64


def draw_segment_ids(key, part):
    key = jax.random.fold_in(key, 11)
    first_key, second_key = jax.random.split(key)
    groups = TOKENS // GROUP_TOK
    leading = jax.random.randint(first_key, (groups, 1), 1, TOK_DEV)
    trailing = jax.random.randint(second_key, (groups, 1), 1, TOK_DEV)
    index = jnp.arange(GROUP_TOK, dtype=jnp.int32)[None, :]
    segments = (index >= leading).astype(jnp.int32) + (index >= GROUP_TOK - trailing).astype(jnp.int32)
    return segments.reshape(TOKENS)


def shard_levels(rng, extent, cuts, low, top_value):
    factor_of = 1.0
    for axis_at, blocks in cuts:
        heights = jax.random.uniform(jax.random.fold_in(jax.random.fold_in(rng, 6), axis_at), (blocks,), jnp.float32, low / len(cuts), top_value / len(cuts))
        factor_of = factor_of * jnp.repeat(jnp.exp(heights), extent[axis_at] // blocks).reshape((-1,) + (1,) * (len(extent) - 1 - axis_at))
    return factor_of


def assign_block(stream_key, own, number, rows, number_of, top, reach, slope):
    ranking = jax.random.permutation(stream_key, number_of)
    heavy_load, ordinary = load_shares(number_of, rows * top, reach, slope, True), load_shares(number_of, rows * top, reach, slope, False)
    places = jnp.arange(number_of)

    def named(tallies, turn):
        used = int((tallies > 0).sum())
        fixed = max(1, used // 4)
        passed = fixed + (places - fixed + turn * (used - fixed)) % max(1, number_of - fixed)
        return jnp.zeros((number_of,), jnp.int32).at[ranking[jnp.where(places < fixed, places, passed)]].set(jnp.asarray(tallies, jnp.int32))

    tallies = jnp.where(number % 4 == 0, named(heavy_load, number // 4), named(ordinary, number - number // 4 - 1))
    mixed = jax.random.permutation(jax.random.fold_in(own, 3), number_of)
    donor, receiver = mixed[0:number_of // 2 * 2:2], mixed[1:number_of // 2 * 2:2]
    slack = jnp.minimum(tallies[donor] - 1, reach - tallies[receiver]) // 2
    slack = jnp.where((donor == ranking[0]) | (receiver == ranking[0]) | (tallies[receiver] == 0), 0, jnp.maximum(slack, 0))
    passed = jax.random.randint(jax.random.fold_in(own, 4), (number_of // 2,), 0, 1 << 20) % (slack + 1)
    tallies = tallies.at[donor].add(-passed).at[receiver].add(passed)
    labels = jnp.searchsorted(jnp.cumsum(tallies), jnp.arange(rows * top), side="right").astype(jnp.int32)
    listing = labels.reshape(top, rows).T
    listing = listing[jax.random.permutation(jax.random.fold_in(own, 1), rows)]
    turn = jax.random.randint(jax.random.fold_in(own, 2), (rows, 1), 0, top)
    return jnp.take_along_axis(listing, (jnp.arange(top)[None, :] + turn) % top, axis=1)


def load_shares(amount, total, limit, skew, full):
    portions = [(1 << 20) // math.isqrt(rank ** skew) + 1 for rank in range(1, amount + 1)]
    largest = limit if full else min(limit, max(-(-total // amount), total * portions[0] // sum(portions)))
    least = 1 if total - largest >= amount - 1 else 0
    holding, surplus = [largest] + [least] * (amount - 1), total - largest - least * (amount - 1)
    while surplus > 0:
        candidates = [i for i in range(1, amount) if holding[i] < largest] or [i for i in range(1, amount) if holding[i] < limit]
        mass, budget = sum([portions[i] for i in candidates]), surplus
        for i in candidates:
            more = min(limit - holding[i], max(1, budget * portions[i] // mass), surplus)
            holding[i] = holding[i] + more
            surplus = surplus - more
    return np.array(holding)


def scatter_about(stream_key, shape, deviation, most, cuts=(), kind=jnp.bfloat16):
    values = jax.random.normal(stream_key, shape, jnp.float32) * deviation
    if len(cuts) > 0:
        values = shard_levels(stream_key, shape, cuts, -0.22, 0.18) * values
    return jnp.clip(values, min=-most, max=most).astype(kind)


def setup_inputs(seed: int = 0) -> dict:
    seeds = jax.random.split(jax.random.key(seed), 21)
    tokens = scatter_about(seeds[0], (TOKENS, MODEL_WIDTH), 1.0, 6.0, ((0, 32),))
    segment_ids = draw_segment_ids(jax.random.fold_in(seeds[20], 71), 0)
    routes_keys = jax.random.split(jax.random.fold_in(seeds[2], 1), TOKENS // TOK_DEV)
    routes_turns = jax.random.permutation(jax.random.fold_in(seeds[2], 3), TOKENS // TOK_DEV)
    routes = jax.vmap(lambda own, number: assign_block(jax.random.fold_in(seeds[2], 2), own, number, TOK_DEV, EXPERTS, TOP, CAP, 1))(routes_keys, routes_turns).reshape((TOKENS, TOP))
    cotangent = scatter_about(seeds[3], (TOKENS, MODEL_WIDTH), 1.0, 6.0, ((0, 32),))
    gain_attn = jnp.clip(1.0 + 0.1 * jax.random.normal(seeds[4], (MODEL_WIDTH,), jnp.float32), 0.5, 1.5).astype(jnp.bfloat16)
    gain_query = jnp.clip(1.0 + 0.1 * jax.random.normal(seeds[5], (QR,), jnp.float32), 0.5, 1.5).astype(jnp.bfloat16)
    gain_latent = jnp.clip(1.0 + 0.1 * jax.random.normal(seeds[6], (KR,), jnp.float32), 0.5, 1.5).astype(jnp.bfloat16)
    gain_ffn = jnp.clip(1.0 + 0.1 * jax.random.normal(seeds[7], (MODEL_WIDTH,), jnp.float32), 0.5, 1.5).astype(jnp.bfloat16)
    w_qa = scatter_about(seeds[8], (MODEL_WIDTH, QR), MODEL_WIDTH ** -0.5, 0.125, ((0, 2),))
    w_qb = scatter_about(seeds[9], (QR, H * (DN + DR)), QR ** -0.5, 0.15625, ((0, 2),))
    w_kva = scatter_about(seeds[10], (MODEL_WIDTH, KR + DR), MODEL_WIDTH ** -0.5, 0.125, ((0, 2),))
    w_kvb = scatter_about(seeds[11], (KR, H * (DN + DV)), KR ** -0.5, 0.25, ((0, 2),))
    w_out = scatter_about(seeds[12], (H * DV, MODEL_WIDTH), (H * DV // 16) ** -0.5, 0.5, ((0, 2),))
    w_router = scatter_about(seeds[13], (MODEL_WIDTH, EXPERTS), 0.011, 0.06591797, ((0, 2),))
    shared_gate = scatter_about(seeds[14], (MODEL_WIDTH, FS), MODEL_WIDTH ** -0.5, 0.125, ((1, 2),))
    shared_up = scatter_about(seeds[15], (MODEL_WIDTH, FS), MODEL_WIDTH ** -0.5, 0.125, ((1, 2),))
    shared_down = scatter_about(seeds[16], (FS, MODEL_WIDTH), FS ** -0.5, 0.109375, ((0, 2),))
    expert_gate = scatter_about(seeds[17], (EXPERTS, MODEL_WIDTH, FE), MODEL_WIDTH ** -0.5, 0.125, ((0, 16), (2, 2)))
    expert_up = scatter_about(seeds[18], (EXPERTS, MODEL_WIDTH, FE), MODEL_WIDTH ** -0.5, 0.125, ((0, 16), (2, 2)))
    expert_down = scatter_about(seeds[19], (EXPERTS, FE, MODEL_WIDTH), FE ** -0.5, 0.15625, ((0, 16), (1, 2)))
    return dict(tokens=tokens, segment_ids=segment_ids, routes=routes, cotangent=cotangent, gain_attn=gain_attn, gain_query=gain_query, gain_latent=gain_latent, gain_ffn=gain_ffn, w_qa=w_qa, w_qb=w_qb, w_kva=w_kva, w_kvb=w_kvb, w_out=w_out, w_router=w_router, shared_gate=shared_gate, shared_up=shared_up, shared_down=shared_down, expert_gate=expert_gate, expert_up=expert_up, expert_down=expert_down)


norm_eps = 1e-06
rope_base = 50000.0
route_scale = 2.446
masked_score = -1e+30
highest = lax.Precision.HIGHEST

@jax.custom_vjp
def low(v):
    return lax.optimization_barrier(v.astype(jnp.bfloat16)).astype(jnp.float32)

@jax.custom_vjp
def low_back(v):
    return v

def low_keep(v):
    return (low(v), None)

def low_pass(kept, grad):
    return (grad,)

def back_keep(v):
    return (v, None)

def back_low(kept, grad):
    return (low(grad),)
low.defvjp(low_keep, low_pass)
low_back.defvjp(back_keep, back_low)

def matmul(left, right):
    return jnp.dot(left, right, precision=highest)

def normed(values, gain):
    scale = lax.rsqrt(lax.optimization_barrier(jnp.mean(values * values, axis=-1, keepdims=True)) + norm_eps)
    return values * scale * gain

def seq_positions(segments):
    token_count = segments.shape[0]
    index = jnp.arange(token_count, dtype=jnp.int32)
    change = jnp.concatenate([jnp.ones((1,), bool), segments[1:] != segments[:-1]])
    starts = lax.cummax(jnp.where(change, index, 0), axis=0)
    return index - starts

def rope_tables(positions, half):
    freq = rope_base ** (-jnp.arange(half, dtype=jnp.float32) / half)
    angles = positions.astype(jnp.float32)[:, None] * freq[None, :]
    return (jnp.cos(angles), jnp.sin(angles))

def rotate(values, cosine, sine):
    half = values.shape[-1] // 2
    first = values[..., :half]
    second = values[..., half:]
    return jnp.concatenate([first * cosine - second * sine, second * cosine + first * sine], axis=-1)

def silu(values):
    return values * jax.nn.sigmoid(values)

def group_attention(items):
    query_abs, query_rope, latent, key_rope, segments = items
    rows = segments.shape[0]
    index = jnp.arange(rows, dtype=jnp.int32)
    raw = jnp.einsum('thk,gk->htg', query_abs, latent, precision=highest)
    raw = raw + jnp.einsum('thr,gr->htg', query_rope, key_rope, precision=highest)
    visible = (segments[:, None] == segments[None, :]) & (index[None, :] <= index[:, None])
    scaled = raw * (1.0 / (DN + DR) ** 0.5)
    scores = low_back(jnp.where(visible[None], scaled, masked_score))
    probs = low(jax.nn.softmax(scores, axis=-1))
    return low_back(low(jnp.einsum('htg,gk->thk', probs, latent, precision=highest)))

def reference(tokens, segment_ids, routes, cotangent, gain_attn, gain_query, gain_latent, gain_ffn, w_qa, w_qb, w_kva, w_kvb, w_out, w_router, shared_gate, shared_up, shared_down, expert_gate, expert_up, expert_down):
    params = tuple((v.astype(jnp.float32) for v in (gain_attn, gain_query, gain_latent, gain_ffn, w_qa, w_qb, w_kva, w_kvb, w_out, w_router, shared_gate, shared_up, shared_down, expert_gate, expert_up, expert_down)))
    token_count = tokens.shape[0]
    groups = token_count // GROUP_TOK
    positions = jax.vmap(seq_positions)(segment_ids.reshape(groups, GROUP_TOK)).reshape(token_count)
    cosine, sine = rope_tables(positions, DR // 2)
    chosen = lax.optimization_barrier(jnp.sum((routes[:, :, None] == jnp.arange(EXPERTS, dtype=jnp.int32)[None, None, :]).astype(jnp.float32), axis=1))

    def forward(resid, routing_weights):
        attention_norm_gain, query_norm_gain, latent_norm_gain, feedforward_norm_gain, query_down_weight, query_up_weight, key_value_down_weight, key_value_up_weight, output_projection_weight, router_weight_matrix, shared_gate_weight, shared_up_weight, shared_down_weight, expert_gate_weight, expert_up_weight, expert_down_weight = routing_weights
        attn_in = low(normed(resid, attention_norm_gain))
        query_lat = low_back(matmul(attn_in, query_down_weight))
        query_in = low(normed(query_lat, query_norm_gain))
        query_all = low_back(matmul(query_in, query_up_weight)).reshape(token_count, H, DN + DR)
        query_nope = low(query_all[..., :DN])
        query_rope = low(rotate(query_all[..., DN:], cosine[:, None, :], sine[:, None, :]))
        latent_raw = low_back(matmul(attn_in, key_value_down_weight))
        latent = low(normed(latent_raw[:, :KR], latent_norm_gain))
        key_rope = low(rotate(latent_raw[:, KR:], cosine, sine))
        kvb = key_value_up_weight.reshape(KR, H, DN + DV)
        w_uk = kvb[..., :DN]
        w_uv = kvb[..., DN:]
        query_abs = low_back(low(jnp.einsum('thn,khn->thk', query_nope, w_uk, precision=highest)))
        attn_lat = lax.map(jax.checkpoint(group_attention), (query_abs.reshape(groups, GROUP_TOK, H, KR), query_rope.reshape(groups, GROUP_TOK, H, DR), latent.reshape(groups, GROUP_TOK, KR), key_rope.reshape(groups, GROUP_TOK, DR), segment_ids.reshape(groups, GROUP_TOK))).reshape(token_count, H, KR)
        attn_heads = low_back(low(jnp.einsum('thk,khv->thv', attn_lat, w_uv, precision=highest))).reshape(token_count, H * DV)
        mid = resid + low_back(matmul(attn_heads, output_projection_weight))
        ffn_in = low(normed(mid, feedforward_norm_gain))
        logits = matmul(ffn_in, router_weight_matrix)
        sig = jax.nn.sigmoid(logits)
        denom = lax.optimization_barrier(jnp.sum(chosen * sig, axis=-1, keepdims=True))
        routing_weight = route_scale * chosen * sig / denom
        shared_pre_gate = low_back(matmul(ffn_in, shared_gate_weight))
        shared_pre_up = low_back(matmul(ffn_in, shared_up_weight))
        shared_hidden = low(silu(shared_pre_gate) * shared_pre_up)
        shared_out = low_back(matmul(shared_hidden, shared_down_weight))

        def expert_loop_body(total, item):
            gate_w, up_w, down_w, column = item
            pre_gate = low_back(matmul(ffn_in, gate_w))
            pre_up = low_back(matmul(ffn_in, up_w))
            hidden = low(silu(pre_gate) * pre_up)
            output = low_back(low(matmul(hidden, down_w)))
            return (total + column[:, None] * output, None)
        routed_output, ignored_value = lax.scan(jax.checkpoint(expert_loop_body), jnp.zeros((token_count, MODEL_WIDTH), jnp.float32), (expert_gate_weight, expert_up_weight, expert_down_weight, routing_weight.T))
        return mid + shared_out + routed_output
    result, pull = jax.vjp(forward, tokens.astype(jnp.float32), params)
    grad_tokens, grads = pull(cotangent.astype(jnp.float32))
    return (result, grad_tokens, grads[0], grads[1], grads[2], grads[3], grads[4], grads[5], grads[6], grads[7], grads[8], grads[9], grads[10], grads[11], grads[12], grads[13], grads[14], grads[15])
```

```python
import functools
import math

import jax
import jax.numpy as jnp
import numpy as np
from jax import lax
from jax.experimental import pallas as pl
from jax.experimental.pallas import tpu as pltpu
from jax.sharding import PartitionSpec as P

H = 16
DN = 128
DR = 64
DV = 128
KR = 512
TOP = 6


norm_eps = 1e-06
rope_base = 50000.0
route_scale = 2.446
masked_score = -1e30
highest = lax.Precision.HIGHEST
bfloat = jnp.bfloat16
single = jnp.float32


def row_scale(values):
    return lax.rsqrt(jnp.mean(values * values, axis=-1, keepdims=True) + norm_eps)


def norm_back(grad_out, normed_rows, scale_rows, gain):
    grad_normed = grad_out * gain
    grad_input = scale_rows * (
        grad_normed - normed_rows * jnp.mean(grad_normed * normed_rows, axis=-1, keepdims=True)
    )
    return (grad_input, jnp.sum(grad_out * normed_rows, axis=0))


def seq_positions(segments):
    token_count = segments.shape[0]
    index = jnp.arange(token_count, dtype=jnp.int32)
    change = jnp.concatenate([jnp.ones((1,), bool), segments[1:] != segments[:-1]])
    starts = lax.cummax(jnp.where(change, index, 0), axis=0)
    return index - starts


def rope_tables(positions, half):
    freq = rope_base ** (-jnp.arange(half, dtype=jnp.float32) / half)
    angles = positions.astype(jnp.float32)[:, None] * freq[None, :]
    return (jnp.cos(angles), jnp.sin(angles))


def rotate(values, cosine, sine):
    half = values.shape[-1] // 2
    first = values[..., :half]
    second = values[..., half:]
    return jnp.concatenate(
        [first * cosine - second * sine, second * cosine + first * sine], axis=-1
    )


def rotate_back(grads, cosine, sine):
    half = grads.shape[-1] // 2
    first = grads[..., :half]
    second = grads[..., half:]
    return jnp.concatenate(
        [first * cosine + second * sine, second * cosine - first * sine], axis=-1
    )


def silu_grads(grad_hidden, pre_gate, pre_up):
    sigma = jax.nn.sigmoid(pre_gate)
    grad_gate = grad_hidden * pre_up * sigma * (1.0 + pre_gate * (1.0 - sigma))
    grad_up = grad_hidden * pre_gate * sigma
    return (grad_gate.astype(bfloat), grad_up.astype(bfloat))


def dot(left, right):
    return jnp.dot(left, right, preferred_element_type=single)


def dot_t(left, right):
    return lax.dot_general(left, right, (((1,), (1,)), ((), ())), preferred_element_type=single)


def t_dot(left, right):
    return lax.dot_general(left, right, (((0,), (0,)), ((), ())), preferred_element_type=single)


def expert_kernel(count, pieces, capacity, experts, group, first, *refs):
    refs = list(refs)
    me_ref = refs.pop(0)
    blocks = [refs.pop(0) for _ in range(count)]
    cots = [refs.pop(0) for _ in range(count)]
    weights = [[refs.pop(0) for _ in range(pieces)] for _ in range(3)]
    if not first:
        refs = refs[4 + 3 * pieces:]
    backs = [refs.pop(0) for _ in range(count)]
    outs = [refs.pop(0) for _ in range(count)]
    kept = [refs.pop(0) for _ in range(4)]
    acts = [[refs.pop(0) for _ in range(pieces)] for _ in range(3)]
    full = [refs.pop(0) for _ in range(3)]
    rows, grads = refs.pop(0), refs.pop(0)
    act_scr = [[refs.pop(0) for _ in range(pieces)] for _ in range(3)]
    sem_w, sem_o = refs.pop(0), refs.pop(0)
    assert not refs
    model = cots[0].shape[1]
    tok = cots[0].shape[0]
    width = weights[0][0].shape[0]
    loads = []
    for k in range(3):
        loads.append([])
        for j in range(pieces):
            c = pltpu.make_async_copy(weights[k][j], full[k].at[pl.ds(j * width, width)], sem_w.at[k, j])
            c.start()
            loads[k].append(c)
    stores = []
    def store(src, dst, at):
        c = pltpu.make_async_copy(src, dst, sem_o.at[at])
        c.start()
        stores.append(c)
    me = me_ref[0]
    lane = lax.broadcasted_iota(jnp.int32, (tok, 128), 1)
    place = lax.broadcasted_iota(jnp.int32, (tok, capacity), 1).astype(single)
    picks, wcols = [], []
    for i in range(count):
        marks = blocks[i][:, model:model + 128].astype(single)
        code = jnp.sum(jnp.where(lane == me, marks, 0.0), axis=1, keepdims=True)
        weight = jnp.sum(jnp.where((lane == me + experts) | (lane == me + 2 * experts), marks, 0.0), axis=1, keepdims=True)
        pick = (code == place).astype(single).astype(bfloat)
        picks.append(pick)
        wcols.append(weight)
        here = pl.ds(i * capacity, capacity)
        rows[here] = t_dot(pick, blocks[i][:, :model]).astype(bfloat)
        scaled = (weight * cots[i][...].astype(single)).astype(bfloat)
        grads[here] = t_dot(pick, scaled).astype(bfloat)
    n = count * capacity
    store(rows, kept[0].at[pl.ds(group * n, n)], 0)
    store(grads, kept[1].at[pl.ds(group * n, n)], 1)
    for i in range(count):
        store(blocks[i].at[:, pl.ds(0, model)], kept[2].at[pl.ds((group * count + i) * tok, tok)], 2 + i)
        store(cots[i], kept[3].at[pl.ds((group * count + i) * tok, tok)], 2 + count + i)
    for c in loads[0]: c.wait()
    pre_gate = dot_t(rows[...], full[0][...])
    for c in loads[1]: c.wait()
    pre_up = dot_t(rows[...], full[1][...])
    sigma = jax.nn.sigmoid(pre_gate)
    silu = pre_gate * sigma
    hidden = (silu * pre_up).astype(bfloat)
    for c in loads[2]: c.wait()
    grad_hidden = dot_t(grads[...], full[2][...])
    grad_gate = (grad_hidden * pre_up * sigma * (1.0 + pre_gate * (1.0 - sigma))).astype(bfloat)
    grad_up = (grad_hidden * silu).astype(bfloat)
    at = 2 + 2 * count
    for k, v in enumerate((hidden, grad_gate, grad_up)):
        for j in range(pieces):
            act_scr[k][j][...] = v[:, j * width:(j + 1) * width]
            store(act_scr[k][j], acts[k][j].at[pl.ds(group * n, n)], at)
            at += 1
    back = (dot(grad_gate, full[0][...]) + dot(grad_up, full[1][...])).astype(bfloat)
    out = dot(hidden, full[2][...]).astype(bfloat)
    for i in range(count):
        here = slice(i * capacity, (i + 1) * capacity)
        got = dot(picks[i], out[here])
        dots = jnp.sum(got * cots[i][...].astype(single), axis=1, keepdims=True)
        outs[i][...] = (wcols[i] * got).astype(bfloat)
        backs[i][:, :model] = dot(picks[i], back[here]).astype(bfloat)
        high = dots.astype(bfloat).astype(single)
        tail = jnp.where(lane == me, high, 0.0) + jnp.where(lane == me + experts, dots - high, 0.0)
        backs[i][:, model:model + 128] = tail.astype(bfloat)
    for c in stores: c.wait()

def run_experts(me, blocks, cots, weights, capacity, experts, group, groups, carried):
    count, pieces = len(blocks), len(weights[0])
    tok, model = cots[0].shape
    width = weights[0][0].shape[0]
    n = count * capacity
    first = carried is None
    shape = jax.ShapeDtypeStruct
    kept = [shape((groups * n, model), bfloat)] * 2 + [shape((groups * count * tok, model), bfloat)] * 2
    kept += [shape((groups * n, width), bfloat)] * (3 * pieces)
    vm = pl.BlockSpec(memory_space=pltpu.VMEM)
    hbm = pl.BlockSpec(memory_space=pl.ANY)
    flat = [w for ws in weights for w in ws]
    operands = [me, *blocks, *cots, *flat]
    in_specs = [pl.BlockSpec(memory_space=pltpu.SMEM)] + [vm] * (2 * count) + [hbm] * len(flat)
    alias = {}
    if not first:
        base = len(operands)
        operands += list(carried)
        in_specs += [hbm] * len(kept)
        alias = {base + i: 2 * count + i for i in range(len(kept))}
    rows = n
    flops = 2 * rows * model * width * pieces * 6
    out = pl.pallas_call(
        functools.partial(expert_kernel, count, pieces, capacity, experts, group, first),
        out_shape=[shape(b.shape, bfloat) for b in blocks] + [shape((tok, model), bfloat)] * count + kept,
        in_specs=in_specs,
        out_specs=[vm] * (2 * count) + [hbm] * len(kept),
        input_output_aliases=alias,
        scratch_shapes=[pltpu.VMEM((pieces * width, model), bfloat)] * 3
        + [pltpu.VMEM((n, model), bfloat)] * 2
        + [pltpu.VMEM((n, width), bfloat)] * (3 * pieces)
        + [pltpu.SemaphoreType.DMA((3, pieces)), pltpu.SemaphoreType.DMA((2 + 2 * count + 3 * pieces,))],
        compiler_params=pltpu.CompilerParams(vmem_limit_bytes=58 << 20),
        cost_estimate=pl.CostEstimate(flops=flops, bytes_accessed=30 << 20, transcendentals=0),
    )(*operands)
    return out[:count], out[count:2 * count], out[2 * count:]


def shared_kernel(parts, tiles, start, width, first, *refs):
    refs = list(refs)
    xs = [refs.pop(0) for _ in range(parts)]
    cs = [refs.pop(0) for _ in range(parts)]
    weights = [refs.pop(0) for _ in range(3)]
    if not first:
        refs = refs[3:]
    outs = [refs.pop(0) for _ in range(3)]
    wgu, wd = (refs.pop(0) for _ in range(2))
    accs = [refs.pop(0) for _ in range(2)]
    sem_w, sem_o = refs
    step = pl.program_id(0)
    cols = pl.ds(start, width)
    loads = [
        pltpu.make_async_copy(weights[0].at[:, cols], wgu.at[:, pl.ds(0, width)], sem_w.at[0]),
        pltpu.make_async_copy(weights[1].at[:, cols], wgu.at[:, pl.ds(width, width)], sem_w.at[1]),
        pltpu.make_async_copy(weights[2].at[cols], wd, sem_w.at[2]),
    ]

    @pl.when(step == 0)
    def _():
        for c in loads:
            c.start()
        for a in accs:
            a[...] = jnp.zeros_like(a)
        for c in loads:
            c.wait()

    def work(x_ref, c_ref):
        x, c = x_ref[...], c_ref[...]
        pre = dot(x, wgu[...])
        pre_gate, pre_up = pre[:, :width], pre[:, width:]
        grad_hidden = dot_t(c, wd[...])
        sigma = jax.nn.sigmoid(pre_gate)
        silu = pre_gate * sigma
        hidden = (silu * pre_up).astype(bfloat)
        grad_gate = (grad_hidden * pre_up * sigma * (1.0 + pre_gate * (1.0 - sigma))).astype(bfloat)
        grad_up = (grad_hidden * silu).astype(bfloat)
        accs[0][...] += t_dot(x, jnp.concatenate([grad_gate, grad_up], axis=1))
        accs[1][...] += t_dot(hidden, c)

    if parts == 1:
        work(xs[0], cs[0])
    else:
        per = tiles // parts
        for p in range(parts):
            pl.when(step // per == p)(functools.partial(work, xs[p], cs[p]))

    @pl.when(step == tiles - 1)
    def _():
        puts = [
            pltpu.make_async_copy(accs[0].at[:, pl.ds(0, width)], outs[0].at[:, cols], sem_o.at[0]),
            pltpu.make_async_copy(accs[0].at[:, pl.ds(width, width)], outs[1].at[:, cols], sem_o.at[1]),
            pltpu.make_async_copy(accs[1], outs[2].at[cols], sem_o.at[2]),
        ]
        for c in puts:
            c.start()
        for c in puts:
            c.wait()

def run_shared(xs, cs, weights, start, width, carried, tile=512):
    parts = len(xs)
    rows, model = xs[0].shape
    per = rows // tile
    tiles = per * parts
    shape = jax.ShapeDtypeStruct
    hbm = pl.BlockSpec(memory_space=pl.ANY)
    specs = [
        pl.BlockSpec((tile, model), lambda i, p=p: (jnp.clip(i - p * per, 0, per - 1), 0))
        for p in range(parts)
    ]
    outs = [shape(w.shape, single) for w in weights]
    operands = [*xs, *cs, *weights]
    in_specs = specs + specs + [hbm] * 3
    alias = {}
    if carried is not None:
        alias = {len(operands) + i: i for i in range(3)}
        operands += list(carried)
        in_specs += [hbm] * 3
    return pl.pallas_call(
        functools.partial(shared_kernel, parts, tiles, start, width, carried is None),
        grid=(tiles,),
        out_shape=outs,
        in_specs=in_specs,
        out_specs=[hbm] * 3,
        input_output_aliases=alias,
        scratch_shapes=[
            pltpu.VMEM((model, 2 * width), bfloat),
            pltpu.VMEM((width, model), bfloat),
            pltpu.VMEM((model, 2 * width), single),
            pltpu.VMEM((width, model), single),
            pltpu.SemaphoreType.DMA((3,)),
            pltpu.SemaphoreType.DMA((3,)),
        ],
        compiler_params=pltpu.CompilerParams(vmem_limit_bytes=60 << 20),
        cost_estimate=pl.CostEstimate(flops=12 * tiles * tile * model * width, bytes_accessed=4 * tiles * tile * model, transcendentals=0),
    )(*operands)


def widths_of(total):
    if total % 128:
        return [total]
    out = []
    while total > 0:
        out.append(min(512, total))
        total -= out[-1]
    return out


def tie(value, *others):
    hbm = pl.BlockSpec(memory_space=pl.ANY)
    return pl.pallas_call(
        lambda *refs: None,
        out_shape=jax.ShapeDtypeStruct(value.shape, value.dtype),
        in_specs=[hbm] * (1 + len(others)),
        out_specs=hbm,
        input_output_aliases={0: 0},
    )(value, *others)


def grid_of(experts, shards):
    if shards == 2 and experts % 4 == 0:
        return (experts // 4, 2, 2)
    side = math.isqrt(experts)
    return (side, side) if side * side == experts else (experts,)


class Chips:
    def __init__(self, dims, names):
        self.dims = dims
        self.names = names
        self.size = int(np.prod(dims))
        self.plane = self.size // dims[0]
        self.places = [tuple(int(v) for v in np.unravel_index(i, dims)) for i in range(self.size)]
        self.offsets = [
            tuple(int(v) for v in np.unravel_index(i, dims[1:])) for i in range(self.plane)
        ]

    def index(self, place):
        return int(np.ravel_multi_index(place, self.dims))

    def own(self, axis):
        return lax.axis_index(self.names[axis])

    def me(self):
        return lax.axis_index(self.names)

    def pairs(self, axis_of, by):
        out = []
        for i, place in enumerate(self.places):
            axis = axis_of(place)
            to = list(place)
            to[axis] = (to[axis] + by) % self.dims[axis]
            out.append((i, self.index(to)))
        return out

    def turning(self, turn, second):
        return lambda place: 1 if ((place[0] + turn) % 2 == 0) != second else 2

    def along(self, value, axis, by):
        n = self.dims[axis]
        return lax.ppermute(value, self.names[axis], [(i, (i + by) % n) for i in range(n)])

    def in_plane(self, value, turn, second, by):
        return lax.ppermute(value, self.names, self.pairs(self.turning(turn, second), by))

    def offset_by(self, value, offset):
        out = []
        for i, place in enumerate(self.places):
            to = [place[0]] + [
                (p + o) % d for p, o, d in zip(place[1:], offset, self.dims[1:])
            ]
            out.append((i, self.index(to)))
        return lax.ppermute(value, self.names, out)

    def tree(self, block, along, in_plane):
        first = [block] + [along(block, 0, j) for j in range(1, self.dims[0])]
        out = []
        for j, b in enumerate(first):
            if len(self.dims) == 1:
                out.append(b)
            elif len(self.dims) == 2:
                out += [b] + [along(b, 1, s) for s in range(1, self.dims[1])]
            else:
                n = self.dims[1]
                hops = [b] + [in_plane(b, j, False, s) for s in range(1, n)]
                for h in hops:
                    out += [h] + [in_plane(h, j, True, s) for s in range(1, n)]
        return out

    def spread(self, block):
        return self.tree(block, self.along, self.in_plane)

    def sources(self):
        def apply(values, pairs):
            out = [0] * len(values)
            for i, to in pairs:
                out[to] = values[i]
            return out

        def along(values, axis, by):
            return apply(values, self.pairs(lambda place: axis, by))

        def in_plane(values, turn, second, by):
            return apply(values, self.pairs(self.turning(turn, second), by))

        table = self.tree(list(range(self.size)), along, in_plane)
        return jnp.asarray(np.array(table, np.int32).T)[self.me()]

    def collect(self, blocks, fillers=()):
        fillers = list(fillers)
        rest = self.plane
        total = None
        for j in range(self.dims[0] - 1, -1, -1):
            part = blocks[j * rest : (j + 1) * rest]
            if len(self.dims) == 1:
                acc = part[0].astype(single)
            elif len(self.dims) == 2:
                acc = part[0].astype(single)
                for s in range(1, self.dims[1]):
                    acc = acc + self.along(part[s], 1, -s).astype(single)
            else:
                n = self.dims[1]
                accs = []
                for h in range(n):
                    a = part[h * n].astype(single)
                    for s in range(1, n):
                        a = a + self.in_plane(part[h * n + s], j, True, -s).astype(single)
                    accs.append(a)
                acc = accs[0]
                for s in range(1, n):
                    acc = acc + self.in_plane(accs[s].astype(bfloat), j, False, -s).astype(single)
            if j > 0:
                acc = self.along(acc.astype(bfloat), 0, -j).astype(single)
            total = acc if total is None else total + acc
        return total

    def own_part(self):
        part = 0
        for axis in range(1, len(self.dims)):
            part = part * self.dims[axis] + self.own(axis)
        return part

    def swap_columns(self, value):
        size = value.shape[1] // self.plane
        out = []
        for offset in self.offsets:
            part = 0
            for axis, by in enumerate(offset):
                n = self.dims[axis + 1]
                part = part * n + (self.own(axis + 1) + by) % n
            piece = lax.dynamic_slice_in_dim(value, part * size, size, 1)
            out.append(self.offset_by(piece, offset) if any(offset) else piece)
        return jnp.concatenate(out, axis=0)

    def stack(self, value):
        if len(self.dims) != 3:
            rows = [self.offset_by(value, o) if any(o) else value for o in self.offsets]
            return [jnp.concatenate(rows, axis=0)]
        n = self.dims[1]
        cut = value.shape[1] // 256 * 128
        out = []
        for half, (one, two) in zip((value[:, :cut], value[:, cut:]), ((2, 1), (1, 2))):
            first = [half] + [self.along(half, one, s) for s in range(1, n)]
            first = jnp.concatenate(first, axis=0)
            second = [first] + [self.along(first, two, s) for s in range(1, n)]
            rows = half.shape[0]
            if one == 2:
                out.append(jnp.concatenate(second, axis=0))
            else:
                out.append(
                    jnp.concatenate(
                        [v[s * rows : (s + 1) * rows] for s in range(n) for v in second], axis=0
                    )
                )
        return out

    def plane_sums(self, value):
        if len(self.dims) != 3:
            return [self.scatter_axis(value, axis) for axis in range(1, len(self.dims))]
        cut = value.shape[1] // 2
        out = []
        for half, order in zip((value[:, :cut], value[:, cut:]), ((1, 2), (2, 1))):
            for axis in order:
                half = self.scatter_axis(half, axis)
            out.append(half)
        return out

    def plane_part(self, value):
        size = value.shape[0] // self.plane
        total = None
        for offset in self.offsets:
            part = 0
            for axis, by in enumerate(offset):
                n = self.dims[axis + 1]
                part = part * n + (self.own(axis + 1) + by) % n
            piece = lax.dynamic_slice_in_dim(value, part * size, size, 0)
            if any(offset):
                piece = self.offset_by(piece.astype(bfloat), offset).astype(single)
            total = piece if total is None else total + piece
        return total.astype(bfloat)

    def unstack(self, halves, swapped):
        if len(self.dims) != 3:
            out = halves[0]
            for axis in range(len(self.dims) - 1, 0, -1):
                out = self.gather_axis(out, axis)
            return out
        one = self.gather_axis(self.gather_axis(halves[0], 2), 1)
        two = self.gather_axis(self.gather_axis(halves[1], 1), 2)
        if swapped:
            n, m = self.dims[1], self.dims[2]
            rows = two.shape[0] // (n * m)
            two = two.reshape(m, n, rows, -1).swapaxes(0, 1).reshape(two.shape)
        return jnp.concatenate([one, two], axis=1)

    def line_sums(self, halves, before=()):
        halves = lax.optimization_barrier((*halves, *before))[: len(halves)]
        return lax.psum(tuple(halves), self.names[0])

    def scatter_axis(self, value, axis):
        n = self.dims[axis]
        rows = value.shape[0] // n
        own = self.own(axis)
        total = lax.dynamic_slice_in_dim(value, own * rows, rows, 0).astype(single)
        for j in range(1, n):
            piece = lax.dynamic_slice_in_dim(value, ((own + j) % n) * rows, rows, 0)
            total = total + self.along(piece, axis, j).astype(single)
        return total.astype(bfloat)

    def gather_axis(self, value, axis):
        n = self.dims[axis]
        pieces = [value] + [self.along(value, axis, j) for j in range(1, n)]
        return in_order(pieces, self.own(axis), 0)


def after(value, *others):
    return lax.optimization_barrier((value, *others))[0]


def in_order(pieces, own, axis):
    n = len(pieces)
    if n == 1:
        return pieces[0]
    if n == 2:
        return jnp.where(
            own == 0,
            jnp.concatenate(pieces, axis=axis),
            jnp.concatenate([pieces[1], pieces[0]], axis=axis),
        )
    turned = pieces[::-1]
    line = jnp.concatenate(turned + turned[:-1], axis=axis)
    extent = pieces[0].shape[axis]
    return lax.dynamic_slice_in_dim(line, (n - 1 - own) * extent, n * extent, axis)


class Cores:
    def __init__(self, count):
        self.count = count
        self.own = lax.axis_index("shard")

    def along(self, value, by):
        n = self.count
        return lax.ppermute(value, "shard", [(i, (i + by) % n) for i in range(n)])

    def spread(self, value):
        return [value] + [self.along(value, j) for j in range(1, self.count)]

    def whole(self, value, axis):
        return in_order(self.spread(value), self.own, axis)

    def chunk(self, value, j, axis):
        size = value.shape[axis] // self.count
        place = (self.own + j + self.count) % self.count
        return lax.dynamic_slice_in_dim(value, place * size, size, axis)

    def rows_times(self, left, pieces):
        out = None
        for j, piece in enumerate(pieces):
            term = dot(self.chunk(left, -j, 1), piece)
            out = term if out is None else out + term
        return out

    def times_rows_t(self, left, pieces):
        return in_order([dot_t(left, piece) for piece in pieces], self.own, 1)

    def swap_columns(self, value, axis=1):
        parts = [self.chunk(value, 0, axis)]
        parts += [self.along(self.chunk(value, j, axis), j) for j in range(1, self.count)]
        return jnp.concatenate(parts, axis=0)

    def stack(self, value):
        return jnp.concatenate(self.spread(value), axis=0)

    def give_back(self, value):
        rows = value.shape[0] // self.count
        total = value[:rows]
        for j in range(1, self.count):
            total = total + self.along(value[j * rows : (j + 1) * rows], -j)
        return total

    def scatter(self, value, axis):
        total = self.chunk(value, 0, axis).astype(single)
        for j in range(1, self.count):
            total = total + self.along(self.chunk(value, j, axis).astype(bfloat), j).astype(single)
        return total


def per_device(
    chips,
    shards,
    tokens,
    segment_ids,
    routes,
    cotangent,
    gain_attn,
    gain_query,
    gain_latent,
    gain_ffn,
    w_qa,
    w_qb,
    w_kva,
    w_kvb,
    w_out,
    w_router,
    shared_gate,
    shared_up,
    shared_down,
    expert_gate,
    expert_up,
    expert_down,
):
    cores = Cores(shards)
    me = chips.me()
    shard_pos = cores.own
    tok_rows = tokens.shape[0]
    model = tokens.shape[1]
    group_rows = tok_rows * shards
    score_scale = 1.0 / (DN + DR) ** 0.5
    query_rank = w_qa.shape[1]

    gains = jnp.concatenate([gain_attn, gain_query, gain_latent, gain_ffn])
    gain_pieces = cores.spread(gains)
    sizes = [v.shape[0] for v in (gain_attn, gain_query, gain_latent, gain_ffn)]
    full_gains = []
    start = 0
    for size in sizes:
        full_gains.append(
            in_order([g[start : start + size] for g in gain_pieces], shard_pos, 0).astype(single)
        )
        start += size
    gain_attn_f, gain_query_f, gain_latent_f, gain_ffn_f = full_gains
    qa_pieces = cores.spread(w_qa)
    kva_pieces = cores.spread(w_kva)
    qb_pieces = cores.spread(w_qb)
    kvb_full = cores.whole(w_kvb, 0)
    out_pieces = cores.spread(w_out)
    router_full = cores.whole(w_router, 0)
    expert_weights = [
        cores.spread(expert_gate[0].T),
        cores.spread(expert_up[0].T),
        cores.spread(expert_down[0]),
    ]
    cot_blocks = chips.spread(cotangent)

    resid = tokens.astype(single)
    attn_scale = row_scale(resid)
    attn_normed = resid * attn_scale
    attn_in = (attn_normed * gain_attn_f).astype(bfloat)
    query_lat = cores.rows_times(attn_in, qa_pieces)
    query_scale = row_scale(query_lat)
    query_normed = query_lat * query_scale
    query_in = (query_normed * gain_query_f).astype(bfloat)
    query_all = cores.rows_times(query_in, qb_pieces).reshape(tok_rows, H, DN + DR)
    group_pos = seq_positions(segment_ids)
    own_start = shard_pos * tok_rows
    own_pos = lax.dynamic_slice_in_dim(group_pos, own_start, tok_rows, 0)
    own_seg = lax.dynamic_slice_in_dim(segment_ids, own_start, tok_rows, 0)
    cosine, sine = rope_tables(own_pos, DR // 2)
    query_nope = query_all[..., :DN].astype(bfloat)
    query_rope = rotate(query_all[..., DN:], cosine[:, None, :], sine[:, None, :]).astype(bfloat)
    latent_raw = cores.rows_times(attn_in, kva_pieces)
    latent_part = latent_raw[:, :KR]
    latent_scale = row_scale(latent_part)
    latent_normed = latent_part * latent_scale
    latent = (latent_normed * gain_latent_f).astype(bfloat)
    key_rope = rotate(latent_raw[:, KR:], cosine, sine).astype(bfloat)
    keys = cores.whole(jnp.concatenate([latent, key_rope], axis=1), 0)
    keys_latent, keys_rope = keys[:, :KR], keys[:, KR:]
    kvb_heads = kvb_full.reshape(KR, H, DN + DV)
    w_uk = kvb_heads[..., :DN]
    w_uv = kvb_heads[..., DN:]
    query_abs = jnp.einsum(
        "thn,khn->thk", query_nope, w_uk, preferred_element_type=single
    ).astype(bfloat)
    group_index = jnp.arange(group_rows, dtype=jnp.int32)
    own_index = own_start + jnp.arange(tok_rows, dtype=jnp.int32)
    visible = (own_seg[:, None] == segment_ids[None, :]) & (
        group_index[None, :] <= own_index[:, None]
    )

    def scores_of():
        raw = jnp.einsum("thk,gk->htg", query_abs, keys_latent, preferred_element_type=single)
        raw = raw + jnp.einsum("thr,gr->htg", query_rope, keys_rope, preferred_element_type=single)
        return jnp.where(visible[None], raw * score_scale, masked_score)

    scores = scores_of()
    top_score = jnp.max(scores, axis=-1, keepdims=True)
    expd = jnp.exp(scores - top_score)
    total = jnp.sum(expd, axis=-1, keepdims=True)
    probs = expd / total
    probs_low = probs.astype(bfloat)
    attn_lat = jnp.einsum(
        "htg,gk->thk", probs_low, keys_latent, preferred_element_type=single
    ).astype(bfloat)
    attn_heads = (
        jnp.einsum("thk,khv->thv", attn_lat, w_uv, preferred_element_type=single)
        .astype(bfloat)
        .reshape(tok_rows, H * DV)
    )
    mid = resid + cores.rows_times(attn_heads, out_pieces)
    ffn_scale = row_scale(mid)
    ffn_normed = mid * ffn_scale
    ffn_in = (ffn_normed * gain_ffn_f).astype(bfloat)

    experts_all = router_full.shape[1]
    lanes = -(-4 * experts_all // 128) * 128
    logits = dot(ffn_in, router_full)
    chosen = jnp.sum(
        (routes[:, :, None] == jnp.arange(experts_all, dtype=jnp.int32)[None, None, :]).astype(
            single
        ),
        axis=1,
    )
    sig = jax.nn.sigmoid(logits)
    denom = jnp.sum(chosen * sig, axis=-1, keepdims=True)
    routing_weights = route_scale * chosen * sig / denom
    capacity = min(tok_rows, 4 * tok_rows * TOP // (3 * experts_all))
    earlier = (jnp.arange(tok_rows)[:, None] > jnp.arange(tok_rows)[None, :]).astype(bfloat)
    slot = dot(earlier, chosen.astype(bfloat))
    code = jnp.where(chosen > 0, slot, -1.0)
    weight_high = routing_weights.astype(bfloat)
    weight_rest = (routing_weights - weight_high.astype(single)).astype(bfloat)
    marks = jnp.concatenate(
        [
            code.astype(bfloat),
            weight_high,
            weight_rest,
            jnp.zeros((tok_rows, lanes - 3 * experts_all), bfloat),
        ],
        axis=1,
    )
    blocks = chips.spread(jnp.concatenate([ffn_in, marks], axis=1))

    stack_ffn = cores.stack(ffn_in)
    stack_cot = cores.stack(cotangent)

    def feed_forward(rows, grads, gate, up, down):
        pre_gate = dot(rows, gate)
        pre_up = dot(rows, up)
        hidden = (jax.nn.silu(pre_gate) * pre_up).astype(bfloat)
        grad_gate, grad_up = silu_grads(dot_t(grads, down), pre_gate, pre_up)
        return hidden, grad_gate, grad_up

    sh_hidden, sh_gate, sh_up = feed_forward(
        stack_ffn, stack_cot, shared_gate, shared_up, shared_down
    )
    shared_out = cores.give_back(dot(sh_hidden, shared_down))
    shared_back = cores.give_back(dot_t(sh_gate, shared_gate) + dot_t(sh_up, shared_up))

    back_blocks, out_blocks, kept = [], [], None
    turns = chips.dims[0]
    per_turn = chips.plane
    who = me.astype(jnp.int32).reshape(1)
    for turn in range(turns):
        here = slice(turn * per_turn, (turn + 1) * per_turn)
        backs, outs, kept = run_experts(
            who,
            blocks[here],
            cot_blocks[here],
            expert_weights,
            capacity,
            experts_all,
            turn,
            turns,
            kept,
        )
        back_blocks += backs
        out_blocks += outs
    rows, row_grads, chip_ffn, chip_cot = kept[:4]
    acts = [kept[4 + k * shards : 4 + (k + 1) * shards] for k in range(3)]
    hiddens, gate_grads, up_grads = acts
    routed_back = chips.collect(back_blocks)
    routed_out = chips.collect(out_blocks)
    result = mid + shared_out + routed_out

    def over_cores(lefts, right):
        sent = [t_dot(lefts[j], right).astype(bfloat) for j in range(1, shards)]
        got = [cores.along(v, -j - 1).astype(single) for j, v in enumerate(sent)]
        return sum(got, t_dot(lefts[0], right))

    grad_egate = over_cores(gate_grads, rows).T[None]
    grad_eup = over_cores(up_grads, rows).T[None]
    grad_edown = over_cores(hiddens, row_grads)[None]

    if shards == 2:
        xs, cs = cores.spread(chip_ffn), cores.spread(chip_cot)
        shared_weights = (shared_gate, shared_up, shared_down)
        shared_grads = None
        start = 0
        for width in widths_of(shared_gate.shape[1]):
            shared_grads = run_shared(xs, cs, shared_weights, start, width, shared_grads)
            start += width
        grad_sgate, grad_sup, grad_sdown = shared_grads
    else:
        grad_sgate = grad_sup = grad_sdown = 0.0
        all_ffn, all_cot = chip_ffn, chip_cot
        for turn in range(shards):
            if turn > 0:
                tied = lax.optimization_barrier(
                    (all_ffn, all_cot, grad_sgate, grad_sup, grad_sdown)
                )
                grad_sgate, grad_sup, grad_sdown = tied[2:]
                all_ffn, all_cot = cores.along(tied[0], 1), cores.along(tied[1], 1)
            all_hidden, all_gate, all_up = feed_forward(
                all_ffn, all_cot, shared_gate, shared_up, shared_down
            )
            grad_sgate = grad_sgate + t_dot(all_ffn, all_gate)
            grad_sup = grad_sup + t_dot(all_ffn, all_up)
            grad_sdown = grad_sdown + t_dot(all_hidden, all_cot)

    grad_out = cotangent.astype(single)
    grad_weights = (
        routed_back[:, model : model + experts_all]
        + routed_back[:, model + experts_all : model + 2 * experts_all]
    )
    grad_sig = chosen * (
        route_scale * grad_weights / denom
        - jnp.sum(grad_weights * routing_weights, axis=-1, keepdims=True) / denom
    )
    grad_logits = grad_sig * sig * (1.0 - sig)
    grad_router = jnp.einsum("te,td->ed", grad_logits, ffn_in.astype(single), precision=highest)
    grad_ffn_in = (
        routed_back[:, :model]
        + shared_back
        + jnp.einsum("te,de->td", grad_logits, router_full.astype(single), precision=highest)
    )
    grad_mid, grad_gffn = norm_back(grad_ffn_in, ffn_normed, ffn_scale, gain_ffn_f)
    grad_mid = grad_mid + grad_out

    def over_plane(rows, grads, extra=None):
        left = chips.swap_columns(cores.swap_columns(rows))
        halves = [t_dot(left, right).astype(bfloat) for right in chips.stack(cores.stack(grads))]
        if extra is not None:
            halves[-1] = jnp.concatenate([halves[-1], extra], axis=1)
        sums = chips.line_sums(halves, done)
        done[:] = sums
        return chips.unstack(sums, True)

    done = []

    grad_attn_out = grad_mid.astype(bfloat)
    grad_wout = over_plane(attn_heads, grad_attn_out)
    grad_heads = (
        cores.times_rows_t(grad_attn_out, out_pieces).astype(bfloat).reshape(tok_rows, H, DV)
    )
    grad_uv = jnp.einsum("thk,thv->khv", attn_lat, grad_heads, preferred_element_type=single)
    grad_attn_lat = jnp.einsum(
        "thv,khv->thk", grad_heads, w_uv, preferred_element_type=single
    ).astype(bfloat)
    grad_probs = jnp.einsum(
        "thk,gk->htg", grad_attn_lat, keys_latent, preferred_element_type=single
    )
    delta = jnp.sum(probs * grad_probs, axis=-1, keepdims=True)
    grad_scores = (probs * (grad_probs - delta)).astype(bfloat)
    grad_qabs = (
        jnp.einsum("htg,gk->thk", grad_scores, keys_latent, preferred_element_type=single)
        * score_scale
    ).astype(bfloat)
    grad_qrope = (
        jnp.einsum("htg,gr->thr", grad_scores, keys_rope, preferred_element_type=single)
        * score_scale
    )
    key_terms = (
        jnp.einsum("htg,thk->gk", grad_scores, query_abs, preferred_element_type=single)
        * score_scale
    )
    key_terms = key_terms + jnp.einsum(
        "htg,thk->gk", probs_low, grad_attn_lat, preferred_element_type=single
    )
    rope_terms = (
        jnp.einsum("htg,thr->gr", grad_scores, query_rope, preferred_element_type=single)
        * score_scale
    )
    grad_keys = cores.scatter(jnp.concatenate([key_terms, rope_terms], axis=1), 0)
    grad_latent, grad_krope = grad_keys[:, :KR], grad_keys[:, KR:]
    grad_uk = jnp.einsum("thn,thk->khn", query_nope, grad_qabs, preferred_element_type=single)
    kvb_terms = jnp.concatenate([grad_uk, grad_uv], axis=-1).reshape(KR, H * (DN + DV))
    kvb_sums = chips.line_sums(
        chips.plane_sums(cores.scatter(kvb_terms, 0).astype(bfloat)), done
    )
    done[:] = kvb_sums
    grad_wkvb = chips.unstack(kvb_sums, False)
    grad_qnope = jnp.einsum("thk,khn->thn", grad_qabs, w_uk, preferred_element_type=single)
    grad_qrope_raw = rotate_back(grad_qrope, cosine[:, None, :], sine[:, None, :])
    grad_query = (
        jnp.concatenate([grad_qnope, grad_qrope_raw], axis=-1)
        .astype(bfloat)
        .reshape(tok_rows, H * (DN + DR))
    )
    grad_wqb = over_plane(query_in, grad_query)
    grad_query_in = cores.times_rows_t(grad_query, qb_pieces)
    grad_qlat, grad_gquery = norm_back(grad_query_in, query_normed, query_scale, gain_query_f)
    grad_kvpart, grad_glatent = norm_back(grad_latent, latent_normed, latent_scale, gain_latent_f)
    grad_kvrope = rotate_back(grad_krope, cosine, sine)
    grad_low = jnp.concatenate([grad_qlat, grad_kvpart, grad_kvrope], axis=-1).astype(bfloat)
    grad_attn_in = in_order(
        [
            dot_t(grad_low[:, :query_rank], qa) + dot_t(grad_low[:, query_rank:], kva)
            for qa, kva in zip(qa_pieces, kva_pieces)
        ],
        shard_pos,
        1,
    )
    grad_resid, grad_gattn = norm_back(grad_attn_in, attn_normed, attn_scale, gain_attn_f)
    grad_tokens = grad_mid + grad_resid

    mixed = jnp.concatenate(
        [grad_gquery.reshape(shards, -1), grad_glatent.reshape(shards, -1)], axis=1
    ).reshape(-1)
    small = jnp.concatenate(
        [grad_gattn[None], grad_gffn[None], mixed[None], grad_router], axis=0
    )
    small = cores.scatter(small, 1)
    grad_wlow = over_plane(attn_in, grad_low, chips.plane_part(small.T))
    low_cols = grad_low.shape[1]
    small = grad_wlow[:, low_cols : low_cols + small.shape[0]].astype(single)
    query_part = gain_query.shape[0]
    return (
        result,
        grad_tokens,
        small[:, 0],
        small[:query_part, 2],
        small[query_part:, 2],
        small[:, 1],
        grad_wlow[:, :query_rank].astype(single),
        grad_wqb.astype(single),
        grad_wlow[:, query_rank:low_cols].astype(single),
        grad_wkvb.astype(single),
        grad_wout.astype(single),
        small[:, 3:],
        grad_sgate,
        grad_sup,
        grad_sdown,
        grad_egate,
        grad_eup,
        grad_edown,
    )


def solution(mesh):
    shards = mesh.shape["shard"]
    dims = grid_of(mesh.shape["expert"], shards)
    names = tuple(f"line{i}" for i in range(len(dims)))
    grid = jax.sharding.Mesh(mesh.devices.reshape(dims + (shards,)), names + ("shard",))
    chips = Chips(dims, names)
    both = names + ("shard",)
    in_specs = (
        P(both, None),
        P(names),
        P(both, None),
        P(both, None),
        P("shard"),
        P("shard"),
        P("shard"),
        P("shard"),
        P("shard", None),
        P("shard", None),
        P("shard", None),
        P("shard", None),
        P("shard", None),
        P("shard", None),
        P(None, "shard"),
        P(None, "shard"),
        P("shard", None),
        P(names, None, "shard"),
        P(names, None, "shard"),
        P(names, "shard", None),
    )
    out_specs = (
        P(both, None),
        P(both, None),
        P("shard"),
        P("shard"),
        P("shard"),
        P("shard"),
        P("shard", None),
        P("shard", None),
        P("shard", None),
        P("shard", None),
        P("shard", None),
        P("shard", None),
        P(None, "shard"),
        P(None, "shard"),
        P("shard", None),
        P(names, None, "shard"),
        P(names, None, "shard"),
        P(names, "shard", None),
    )

    def body(*args):
        return per_device(chips, shards, *args)

    return jax.shard_map(
        body, mesh=grid, in_specs=in_specs, out_specs=out_specs, check_vma=False
    )
```

```python
import functools
import math

import jax
import jax.numpy as jnp
import numpy as np
from jax import lax
from jax.experimental import pallas as pl
from jax.experimental.pallas import tpu as pltpu
from jax.sharding import PartitionSpec as P

H = 16
DN = 128
DR = 64
DV = 128
KR = 512
TOP = 6


norm_eps = 1e-06
rope_base = 50000.0
route_scale = 2.446
masked_score = -1e30
highest = lax.Precision.HIGHEST
bfloat = jnp.bfloat16
single = jnp.float32


def row_scale(values):
    return lax.rsqrt(jnp.mean(values * values, axis=-1, keepdims=True) + norm_eps)


def norm_back(grad_out, normed_rows, scale_rows, gain):
    grad_normed = grad_out * gain
    grad_input = scale_rows * (
        grad_normed - normed_rows * jnp.mean(grad_normed * normed_rows, axis=-1, keepdims=True)
    )
    return (grad_input, jnp.sum(grad_out * normed_rows, axis=0))


def seq_positions(segments):
    token_count = segments.shape[0]
    index = jnp.arange(token_count, dtype=jnp.int32)
    change = jnp.concatenate([jnp.ones((1,), bool), segments[1:] != segments[:-1]])
    starts = lax.cummax(jnp.where(change, index, 0), axis=0)
    return index - starts


def rope_tables(positions, half):
    freq = rope_base ** (-jnp.arange(half, dtype=jnp.float32) / half)
    angles = positions.astype(jnp.float32)[:, None] * freq[None, :]
    return (jnp.cos(angles), jnp.sin(angles))


def rotate(values, cosine, sine):
    half = values.shape[-1] // 2
    first = values[..., :half]
    second = values[..., half:]
    return jnp.concatenate(
        [first * cosine - second * sine, second * cosine + first * sine], axis=-1
    )


def rotate_back(grads, cosine, sine):
    half = grads.shape[-1] // 2
    first = grads[..., :half]
    second = grads[..., half:]
    return jnp.concatenate(
        [first * cosine + second * sine, second * cosine - first * sine], axis=-1
    )


def silu_grads(grad_hidden, pre_gate, pre_up):
    sigma = jax.nn.sigmoid(pre_gate)
    grad_gate = grad_hidden * pre_up * sigma * (1.0 + pre_gate * (1.0 - sigma))
    grad_up = grad_hidden * pre_gate * sigma
    return (grad_gate.astype(bfloat), grad_up.astype(bfloat))


def dot(left, right):
    return jnp.dot(left, right, preferred_element_type=single)


def dot_t(left, right):
    return lax.dot_general(left, right, (((1,), (1,)), ((), ())), preferred_element_type=single)


def t_dot(left, right):
    return lax.dot_general(left, right, (((0,), (0,)), ((), ())), preferred_element_type=single)


def expert_kernel(count, pieces, capacity, experts, group, first, waits, *refs):
    refs = list(refs)
    me_ref = refs.pop(0)
    blocks = [refs.pop(0) for _ in range(count)]
    all_cots = refs.pop(0)
    weights = [[refs.pop(0) for _ in range(pieces)] for _ in range(3)]
    refs = refs[waits:]
    if not first:
        refs = refs[4 + 3 * pieces:]
    backs = [refs.pop(0) for _ in range(count)]
    outs = [refs.pop(0) for _ in range(count)]
    kept = [refs.pop(0) for _ in range(4)]
    acts = [[refs.pop(0) for _ in range(pieces)] for _ in range(3)]
    full = [refs.pop(0) for _ in range(3)]
    rows, grads, cot_scr = refs.pop(0), refs.pop(0), refs.pop(0)
    act_scr = [[refs.pop(0) for _ in range(pieces)] for _ in range(3)]
    sem_w, sem_o, sem_c = refs.pop(0), refs.pop(0), refs.pop(0)
    assert not refs
    tok = blocks[0].shape[0]
    model = all_cots.shape[1]
    width = weights[0][0].shape[0]
    fetches = []
    for i in range(count):
        source = pl.multiple_of(me_ref[1 + group * count + i] * tok, tok)
        c = pltpu.make_async_copy(all_cots.at[pl.ds(source, tok)], cot_scr.at[i], sem_c.at[i])
        c.start()
        fetches.append(c)
    cots = [cot_scr.at[i] for i in range(count)]
    loads = []
    for k in range(3):
        loads.append([])
        for j in range(pieces):
            c = pltpu.make_async_copy(weights[k][j], full[k].at[pl.ds(j * width, width)], sem_w.at[k, j])
            c.start()
            loads[k].append(c)
    stores = []
    def store(src, dst, at):
        c = pltpu.make_async_copy(src, dst, sem_o.at[at])
        c.start()
        stores.append(c)
    me = me_ref[0]
    lane = lax.broadcasted_iota(jnp.int32, (tok, 128), 1)
    place = lax.broadcasted_iota(jnp.int32, (tok, capacity), 1).astype(single)
    picks, wcols = [], []
    for c in fetches:
        c.wait()
    for i in range(count):
        marks = blocks[i][:, model:model + 128].astype(single)
        code = jnp.sum(jnp.where(lane == me, marks, 0.0), axis=1, keepdims=True)
        weight = jnp.sum(jnp.where((lane == me + experts) | (lane == me + 2 * experts), marks, 0.0), axis=1, keepdims=True)
        pick = (code == place).astype(single).astype(bfloat)
        picks.append(pick)
        wcols.append(weight)
        here = pl.ds(i * capacity, capacity)
        rows[here] = t_dot(pick, blocks[i][:, :model]).astype(bfloat)
        scaled = (weight * cots[i][...].astype(single)).astype(bfloat)
        grads[here] = t_dot(pick, scaled).astype(bfloat)
    n = count * capacity
    store(rows, kept[0].at[pl.ds(group * n, n)], 0)
    store(grads, kept[1].at[pl.ds(group * n, n)], 1)
    for i in range(count):
        store(blocks[i].at[:, pl.ds(0, model)], kept[2].at[pl.ds((group * count + i) * tok, tok)], 2 + i)
        store(cots[i], kept[3].at[pl.ds((group * count + i) * tok, tok)], 2 + count + i)
    for c in loads[0]: c.wait()
    pre_gate = dot_t(rows[...], full[0][...])
    for c in loads[1]: c.wait()
    pre_up = dot_t(rows[...], full[1][...])
    sigma = jax.nn.sigmoid(pre_gate)
    silu = pre_gate * sigma
    hidden = (silu * pre_up).astype(bfloat)
    for c in loads[2]: c.wait()
    grad_hidden = dot_t(grads[...], full[2][...])
    grad_gate = (grad_hidden * pre_up * sigma * (1.0 + pre_gate * (1.0 - sigma))).astype(bfloat)
    grad_up = (grad_hidden * silu).astype(bfloat)
    at = 2 + 2 * count
    for k, v in enumerate((hidden, grad_gate, grad_up)):
        for j in range(pieces):
            act_scr[k][j][...] = v[:, j * width:(j + 1) * width]
            store(act_scr[k][j], acts[k][j].at[pl.ds(group * n, n)], at)
            at += 1
    back = (dot(grad_gate, full[0][...]) + dot(grad_up, full[1][...])).astype(bfloat)
    out = dot(hidden, full[2][...]).astype(bfloat)
    for i in range(count):
        here = slice(i * capacity, (i + 1) * capacity)
        got = dot(picks[i], out[here])
        dots = jnp.sum(got * cots[i][...].astype(single), axis=1, keepdims=True)
        outs[i][...] = (wcols[i] * got).astype(bfloat)
        backs[i][:, :model] = dot(picks[i], back[here]).astype(bfloat)
        high = dots.astype(bfloat).astype(single)
        tail = jnp.where(lane == me, high, 0.0) + jnp.where(lane == me + experts, dots - high, 0.0)
        backs[i][:, model:model + 128] = tail.astype(bfloat)
    for c in stores: c.wait()

def run_experts(me, blocks, all_cots, weights, capacity, experts, group, groups, carried, others):
    count, pieces = len(blocks), len(weights[0])
    tok, model = blocks[0].shape[0], weights[0][0].shape[1]
    width = weights[0][0].shape[0]
    n = count * capacity
    first = carried is None
    shape = jax.ShapeDtypeStruct
    kept = [shape((groups * n, model), bfloat)] * 2 + [shape((groups * count * tok, model), bfloat)] * 2
    kept += [shape((groups * n, width), bfloat)] * (3 * pieces)
    vm = pl.BlockSpec(memory_space=pltpu.VMEM)
    hbm = pl.BlockSpec(memory_space=pl.ANY)
    flat = [w for ws in weights for w in ws]
    operands = [me, *blocks, all_cots, *flat, *others]
    in_specs = [pl.BlockSpec(memory_space=pltpu.SMEM)] + [vm] * count
    in_specs += [hbm] * (1 + len(flat) + len(others))
    alias = {}
    if not first:
        base = len(operands)
        operands += list(carried)
        in_specs += [hbm] * len(kept)
        alias = {base + i: 2 * count + i for i in range(len(kept))}
    rows = n
    flops = 2 * rows * model * width * pieces * 6
    out = pl.pallas_call(
        functools.partial(expert_kernel, count, pieces, capacity, experts, group, first, len(others)),
        out_shape=[shape(b.shape, bfloat) for b in blocks] + [shape((tok, model), bfloat)] * count + kept,
        in_specs=in_specs,
        out_specs=[vm] * (2 * count) + [hbm] * len(kept),
        input_output_aliases=alias,
        scratch_shapes=[pltpu.VMEM((pieces * width, model), bfloat)] * 3
        + [pltpu.VMEM((n, model), bfloat)] * 2
        + [pltpu.VMEM((count, tok, model), bfloat)]
        + [pltpu.VMEM((n, width), bfloat)] * (3 * pieces)
        + [pltpu.SemaphoreType.DMA((3, pieces)), pltpu.SemaphoreType.DMA((2 + 2 * count + 3 * pieces,))]
        + [pltpu.SemaphoreType.DMA((count,))],
        compiler_params=pltpu.CompilerParams(vmem_limit_bytes=58 << 20),
        cost_estimate=pl.CostEstimate(flops=flops, bytes_accessed=30 << 20, transcendentals=0),
    )(*operands)
    return out[:count], out[count:2 * count], out[2 * count:]


def shared_kernel(parts, tiles, start, width, first, waits, *refs):
    refs = list(refs)
    xs = [refs.pop(0) for _ in range(parts)]
    cs = [refs.pop(0) for _ in range(parts)]
    weights = [refs.pop(0) for _ in range(3)]
    refs = refs[waits:]
    if not first:
        refs = refs[3:]
    outs = [refs.pop(0) for _ in range(3)]
    wgu, wd = (refs.pop(0) for _ in range(2))
    accs = [refs.pop(0) for _ in range(2)]
    sem_w, sem_o = refs
    step = pl.program_id(0)
    cols = pl.ds(start, width)
    loads = [
        pltpu.make_async_copy(weights[0].at[:, cols], wgu.at[:, pl.ds(0, width)], sem_w.at[0]),
        pltpu.make_async_copy(weights[1].at[:, cols], wgu.at[:, pl.ds(width, width)], sem_w.at[1]),
        pltpu.make_async_copy(weights[2].at[cols], wd, sem_w.at[2]),
    ]

    @pl.when(step == 0)
    def _():
        for c in loads:
            c.start()
        for a in accs:
            a[...] = jnp.zeros_like(a)
        for c in loads:
            c.wait()

    def work(x_ref, c_ref):
        x, c = x_ref[...], c_ref[...]
        pre = dot(x, wgu[...])
        pre_gate, pre_up = pre[:, :width], pre[:, width:]
        grad_hidden = dot_t(c, wd[...])
        sigma = jax.nn.sigmoid(pre_gate)
        silu = pre_gate * sigma
        hidden = (silu * pre_up).astype(bfloat)
        grad_gate = (grad_hidden * pre_up * sigma * (1.0 + pre_gate * (1.0 - sigma))).astype(bfloat)
        grad_up = (grad_hidden * silu).astype(bfloat)
        accs[0][...] += t_dot(x, jnp.concatenate([grad_gate, grad_up], axis=1))
        accs[1][...] += t_dot(hidden, c)

    if parts == 1:
        work(xs[0], cs[0])
    else:
        per = tiles // parts
        for p in range(parts):
            pl.when(step // per == p)(functools.partial(work, xs[p], cs[p]))

    @pl.when(step == tiles - 1)
    def _():
        puts = [
            pltpu.make_async_copy(accs[0].at[:, pl.ds(0, width)], outs[0].at[:, cols], sem_o.at[0]),
            pltpu.make_async_copy(accs[0].at[:, pl.ds(width, width)], outs[1].at[:, cols], sem_o.at[1]),
            pltpu.make_async_copy(accs[1], outs[2].at[cols], sem_o.at[2]),
        ]
        for c in puts:
            c.start()
        for c in puts:
            c.wait()

def run_shared(xs, cs, weights, start, width, carried, others=(), tile=512):
    parts = len(xs)
    rows, model = xs[0].shape
    per = rows // tile
    tiles = per * parts
    shape = jax.ShapeDtypeStruct
    hbm = pl.BlockSpec(memory_space=pl.ANY)
    specs = [
        pl.BlockSpec((tile, model), lambda i, p=p: (jnp.clip(i - p * per, 0, per - 1), 0))
        for p in range(parts)
    ]
    outs = [shape(w.shape, single) for w in weights]
    operands = [*xs, *cs, *weights, *others]
    in_specs = specs + specs + [hbm] * (3 + len(others))
    alias = {}
    if carried is not None:
        alias = {len(operands) + i: i for i in range(3)}
        operands += list(carried)
        in_specs += [hbm] * 3
    return pl.pallas_call(
        functools.partial(shared_kernel, parts, tiles, start, width, carried is None, len(others)),
        grid=(tiles,),
        out_shape=outs,
        in_specs=in_specs,
        out_specs=[hbm] * 3,
        input_output_aliases=alias,
        scratch_shapes=[
            pltpu.VMEM((model, 2 * width), bfloat),
            pltpu.VMEM((width, model), bfloat),
            pltpu.VMEM((model, 2 * width), single),
            pltpu.VMEM((width, model), single),
            pltpu.SemaphoreType.DMA((3,)),
            pltpu.SemaphoreType.DMA((3,)),
        ],
        compiler_params=pltpu.CompilerParams(vmem_limit_bytes=60 << 20),
        cost_estimate=pl.CostEstimate(flops=12 * tiles * tile * model * width, bytes_accessed=4 * tiles * tile * model, transcendentals=0),
    )(*operands)


def turned(values, cosine, sine, way):
    half = values.shape[-1] // 2
    first, second = values[:, :half], values[:, half:]
    return jnp.concatenate(
        [first * cosine - way * second * sine, second * cosine + way * first * sine], axis=1
    )


def heads_kernel(pieces, score_scale, *refs):
    refs = list(refs)
    q_ref = refs.pop(0)
    kvbs = [refs.pop(0) for _ in range(pieces)]
    latent, rope, shown, cosine, sine = (refs.pop(0) for _ in range(5))
    heads_ref, nope_ref, qrope_ref, abs_ref, probs_ref, lat_ref = refs
    latents, ropes = latent[...], rope[...]
    visible = shown[...] > 0
    q = q_ref[...]
    rank = latents.shape[1]
    for h in range(2):
        nope = q[:, h * (DN + DR) : h * (DN + DR) + DN].astype(bfloat)
        tail = q[:, h * (DN + DR) + DN : (h + 1) * (DN + DR)]
        qrope = turned(tail, cosine[...], sine[...], 1.0).astype(bfloat)
        at = h * (DN + DV)
        w_uk = jnp.concatenate([w[:, at : at + DN] for w in kvbs], axis=0)
        w_uv = jnp.concatenate([w[:, at + DN : at + DN + DV] for w in kvbs], axis=0)
        query = dot_t(nope, w_uk).astype(bfloat)
        raw = dot_t(query, latents) + dot_t(qrope, ropes)
        scores = jnp.where(visible, raw * score_scale, masked_score)
        expd = jnp.exp(scores - jnp.max(scores, axis=1, keepdims=True))
        probs = expd / jnp.sum(expd, axis=1, keepdims=True)
        lat = dot(probs.astype(bfloat), latents).astype(bfloat)
        heads_ref[:, h * DV : (h + 1) * DV] = dot(lat, w_uv).astype(bfloat)
        nope_ref[:, h * DN : (h + 1) * DN] = nope
        qrope_ref[:, h * DR : (h + 1) * DR] = qrope
        abs_ref[:, h * rank : (h + 1) * rank] = query
        keys = probs.shape[1]
        probs_ref[:, h * keys : (h + 1) * keys] = probs
        lat_ref[:, h * rank : (h + 1) * rank] = lat


def heads_back_kernel(pieces, score_scale, *refs):
    refs = list(refs)
    g_ref = refs.pop(0)
    kvbs = [refs.pop(0) for _ in range(pieces)]
    latent, rope, cosine, sine = (refs.pop(0) for _ in range(4))
    nope_ref, qrope_ref, abs_ref, probs_ref, lat_ref = (refs.pop(0) for _ in range(5))
    gq_ref = refs.pop(0)
    gkvbs = [refs.pop(0) for _ in range(pieces)]
    key_ref, rope_out = refs
    latents, ropes = latent[...], rope[...]
    rank, keys = latents.shape[1], latents.shape[0]

    @pl.when(pl.program_id(0) == 0)
    def _():
        key_ref[...] = jnp.zeros_like(key_ref)
        rope_out[...] = jnp.zeros_like(rope_out)

    parts = []
    key_sum = key_ref[...]
    rope_sum = rope_out[...]
    for h in range(2):
        at = h * (DN + DV)
        w_uk = jnp.concatenate([w[:, at : at + DN] for w in kvbs], axis=0)
        w_uv = jnp.concatenate([w[:, at + DN : at + DN + DV] for w in kvbs], axis=0)
        grad = g_ref[:, h * DV : (h + 1) * DV]
        lat = lat_ref[:, h * rank : (h + 1) * rank]
        query = abs_ref[:, h * rank : (h + 1) * rank]
        nope = nope_ref[:, h * DN : (h + 1) * DN]
        qrope = qrope_ref[:, h * DR : (h + 1) * DR]
        probs = probs_ref[:, h * keys : (h + 1) * keys]
        grad_uv = t_dot(lat, grad).astype(bfloat)
        grad_lat = dot_t(grad, w_uv).astype(bfloat)
        grad_probs = dot_t(grad_lat, latents)
        delta = jnp.sum(probs * grad_probs, axis=1, keepdims=True)
        grad_scores = (probs * (grad_probs - delta)).astype(bfloat)
        grad_abs = (dot(grad_scores, latents) * score_scale).astype(bfloat)
        grad_rope = dot(grad_scores, ropes) * score_scale
        key_sum = key_sum + t_dot(grad_scores, query) * score_scale
        key_sum = key_sum + t_dot(probs.astype(bfloat), grad_lat)
        rope_sum = rope_sum + t_dot(grad_scores, qrope) * score_scale
        grad_uk = t_dot(grad_abs, nope).astype(bfloat)
        rows = rank // pieces
        for j in range(pieces):
            gkvbs[j][:, at : at + DN] = grad_uk[j * rows : (j + 1) * rows]
            gkvbs[j][:, at + DN : at + DN + DV] = grad_uv[j * rows : (j + 1) * rows]
        parts.append(dot(grad_abs, w_uk))
        parts.append(turned(grad_rope, cosine[...], sine[...], -1.0))
    gq_ref[...] = jnp.concatenate(parts, axis=1).astype(bfloat)
    key_ref[...] = key_sum
    rope_out[...] = rope_sum


def run_heads(q, kvbs, latent, rope, shown, cosine, sine, heads, score_scale):
    rows, pieces = q.shape[0], len(kvbs)
    keys, rank = latent.shape
    shape = jax.ShapeDtypeStruct
    own = lambda width: pl.BlockSpec((rows, width), lambda g: (0, g))
    still = lambda v: pl.BlockSpec(v.shape, lambda g: (0, 0))
    kvb = [pl.BlockSpec((w.shape[0], 2 * (DN + DV)), lambda g: (0, g)) for w in kvbs]
    widths = (DV, DN, DR, rank, keys, rank)
    kinds = (bfloat, bfloat, bfloat, bfloat, single, bfloat)
    return pl.pallas_call(
        functools.partial(heads_kernel, pieces, score_scale),
        grid=(heads // 2,),
        out_shape=[shape((rows, heads * w), k) for w, k in zip(widths, kinds)],
        in_specs=[own(2 * (DN + DR)), *kvb] + [still(v) for v in (latent, rope, shown, cosine, sine)],
        out_specs=[own(2 * w) for w in widths],
        compiler_params=pltpu.CompilerParams(vmem_limit_bytes=40 << 20),
        cost_estimate=pl.CostEstimate(flops=3 << 30, bytes_accessed=14 << 20, transcendentals=heads * rows * keys),
    )(q, *kvbs, latent, rope, shown, cosine, sine)


def run_heads_back(grad, kvbs, latent, rope, cosine, sine, saved, heads, score_scale, others):
    rows, pieces = grad.shape[0], len(kvbs)
    keys, rank = latent.shape
    shape = jax.ShapeDtypeStruct
    own = lambda width: pl.BlockSpec((rows, width), lambda g: (0, g))
    still = lambda v: pl.BlockSpec(v.shape, lambda g: (0, 0))
    kvb = [pl.BlockSpec((w.shape[0], 2 * (DN + DV)), lambda g: (0, g)) for w in kvbs]
    widths = (DN, DR, rank, keys, rank)

    def body(*refs):
        cut = 1 + pieces + 4 + 5
        heads_back_kernel(pieces, score_scale, *refs[:cut], *refs[cut + len(others) :])

    out = pl.pallas_call(
        body,
        grid=(heads // 2,),
        out_shape=[shape((rows, heads * (DN + DR)), bfloat)]
        + [shape(w.shape, bfloat) for w in kvbs]
        + [shape((keys, rank), single), shape((keys, DR), single)],
        in_specs=[own(2 * DV), *kvb]
        + [still(v) for v in (latent, rope, cosine, sine)]
        + [own(2 * w) for w in widths]
        + [pl.BlockSpec(memory_space=pl.ANY)] * len(others),
        out_specs=[own(2 * (DN + DR)), *kvb]
        + [pl.BlockSpec((keys, rank), lambda g: (0, 0)), pl.BlockSpec((keys, DR), lambda g: (0, 0))],
        compiler_params=pltpu.CompilerParams(vmem_limit_bytes=40 << 20),
        cost_estimate=pl.CostEstimate(flops=6 << 30, bytes_accessed=20 << 20, transcendentals=0),
    )(grad, *kvbs, latent, rope, cosine, sine, *saved, *others)
    return out[0], out[1 : 1 + pieces], out[1 + pieces], out[2 + pieces]


def assemble_kernel(parts, cuts, fold, *refs):
    where, one_0, one_1, two_0, two_1, *outs = refs
    step = pl.program_id(0)
    _, m = parts
    row = jnp.where(step // m == where[0], one_0[...], one_1[...])
    column = jnp.where(step % m == where[1], two_0[...], two_1[...])
    value = jnp.concatenate([row, column], axis=1).astype(single)
    start = 0
    for i, (width, out) in enumerate(zip(cuts, outs)):
        piece = value[:, start : start + width]
        start += width
        if i == 0 and fold > 1:
            rows = piece.shape[0] // fold
            piece = jnp.concatenate(
                [piece[k * rows : (k + 1) * rows] for k in range(fold)], axis=1
            )
        if out.shape[0] == width and out.shape[0] != piece.shape[0]:
            piece = piece.T
        out[...] = piece


def assemble(chips, lines, cuts, fold, turned):
    n, m = chips.dims[1:]
    parts = n * m
    rows = lines[0][0].shape[0] * n // parts
    where = jnp.stack([chips.own(1), chips.own(2)]).astype(jnp.int32)
    one = pl.BlockSpec((rows, lines[0][0].shape[1]), lambda p: (p % m, 0))
    two = pl.BlockSpec((rows, lines[1][0].shape[1]), lambda p: (p // m, 0))
    shapes, specs = [], []
    for i, width in enumerate(cuts):
        if i == 0 and fold > 1:
            shapes.append((rows * parts // fold, width * fold))
            specs.append(pl.BlockSpec((rows // fold, width * fold), lambda p: (p, 0)))
        elif i in turned:
            shapes.append((width, rows * parts))
            specs.append(pl.BlockSpec((width, rows), lambda p: (0, p)))
        else:
            shapes.append((rows * parts, width))
            specs.append(pl.BlockSpec((rows, width), lambda p: (p, 0)))
    return pl.pallas_call(
        functools.partial(assemble_kernel, (n, m), cuts, fold),
        grid=(parts,),
        out_shape=[jax.ShapeDtypeStruct(v, single) for v in shapes],
        in_specs=[pl.BlockSpec(memory_space=pltpu.SMEM), one, one, two, two],
        out_specs=specs,
        compiler_params=pltpu.CompilerParams(vmem_limit_bytes=56 << 20),
        cost_estimate=pl.CostEstimate(flops=0, bytes_accessed=50 << 20, transcendentals=0),
    )(where, *lines[0], *lines[1])


def widths_of(total):
    if total % 128:
        return [total]
    out = []
    while total > 0:
        out.append(min(384, total))
        total -= out[-1]
    return out


def tie(value, *others):
    hbm = pl.BlockSpec(memory_space=pl.ANY)
    return pl.pallas_call(
        lambda *refs: None,
        out_shape=jax.ShapeDtypeStruct(value.shape, value.dtype),
        in_specs=[hbm] * (1 + len(others)),
        out_specs=hbm,
        input_output_aliases={0: 0},
    )(value, *others)


def grid_of(experts, shards):
    if shards == 2 and experts % 4 == 0:
        return (experts // 4, 2, 2)
    side = math.isqrt(experts)
    return (side, side) if side * side == experts else (experts,)


class Chips:
    def __init__(self, dims, names):
        self.dims = dims
        self.names = names
        self.size = int(np.prod(dims))
        self.plane = self.size // dims[0]
        self.places = [tuple(int(v) for v in np.unravel_index(i, dims)) for i in range(self.size)]
        self.offsets = [
            tuple(int(v) for v in np.unravel_index(i, dims[1:])) for i in range(self.plane)
        ]

    def index(self, place):
        return int(np.ravel_multi_index(place, self.dims))

    def own(self, axis):
        return lax.axis_index(self.names[axis])

    def me(self):
        return lax.axis_index(self.names)

    def pairs(self, axis_of, by):
        out = []
        for i, place in enumerate(self.places):
            axis = axis_of(place)
            to = list(place)
            to[axis] = (to[axis] + by) % self.dims[axis]
            out.append((i, self.index(to)))
        return out

    def along(self, value, axis, by):
        n = self.dims[axis]
        return lax.ppermute(value, self.names[axis], [(i, (i + by) % n) for i in range(n)])

    def offset_by(self, value, offset):
        out = []
        for i, place in enumerate(self.places):
            to = [place[0]] + [
                (p + o) % d for p, o, d in zip(place[1:], offset, self.dims[1:])
            ]
            out.append((i, self.index(to)))
        return lax.ppermute(value, self.names, out)

    def first(self, block):
        return [block] + [self.along(block, 0, j) for j in range(1, self.dims[0])]

    def hop_one(self, block, j):
        if len(self.dims) < 3:
            return [block]
        return [block] + [self.along(block, 1, s) for s in range(1, self.dims[1])]

    def hop_two(self, blocks, j):
        last = len(self.dims) - 1
        if last == 0:
            return blocks
        return [v for b in blocks for v in self.hop_line(b, last)]

    def hop_line(self, block, axis):
        return [block] + [self.along(block, axis, s) for s in range(1, self.dims[axis])]

    def straight(self, block):
        return [self.offset_by(block, o) if any(o) else block for o in self.offsets]

    def straight_back(self, blocks):
        return [
            self.offset_by(b, [-v for v in o]) if any(o) else b
            for b, o in zip(blocks, self.offsets)
        ]

    def back_two(self, blocks, j, turn=False):
        if len(self.dims) == 1:
            return [(blocks[0], [])]
        n = self.dims[-1]
        if len(self.dims) == 2:
            return [(blocks[0], [self.along(blocks[s], 1, -s) for s in range(1, n)])]
        m = self.dims[1]
        if turn:
            return [
                (blocks[h * n], [self.along(blocks[h * n + t], 2, -t) for t in range(1, n)])
                for h in range(m)
            ]
        return [
            (blocks[t], [self.along(blocks[h * n + t], 1, -h) for h in range(1, m)])
            for t in range(n)
        ]

    def back_one(self, sums, j, turn=False):
        axis = 1 if turn else 2
        got = [self.along(v.astype(bfloat), axis, -s) for s, v in enumerate(sums) if s]
        return [sums[0], got]

    def sources(self):
        table = [
            [
                self.index([(p - o) % d for p, o, d in zip(place, self.places[i], self.dims)])
                for i in range(self.size)
            ]
            for place in self.places
        ]
        return jnp.asarray(np.array(table, np.int32))[self.me()]

    def back_first(self, total, j):
        return self.along(total.astype(bfloat), 0, -j) if j else total

    def own_part(self):
        part = 0
        for axis in range(1, len(self.dims)):
            part = part * self.dims[axis] + self.own(axis)
        return part

    def swap_columns(self, *values):
        out = []
        for offset in self.offsets:
            part = 0
            for axis, by in enumerate(offset):
                n = self.dims[axis + 1]
                part = part * n + (self.own(axis + 1) + by) % n
            pieces = []
            for v in values:
                size = v.shape[1] // self.plane
                pieces.append(lax.dynamic_slice_in_dim(v, part * size, size, 1))
            piece = jnp.concatenate(pieces, axis=1)
            out.append(self.offset_by(piece, offset) if any(offset) else piece)
        return out

    def orders(self):
        return ((2, 1), (1, 2)) if len(self.dims) == 3 else ((1,),)

    def halves(self, value):
        if len(self.dims) != 3:
            return [value]
        cut = value.shape[1] // 256 * 128
        return [value[:, :cut], value[:, cut:]]

    def stack_one(self, value):
        return [self.hop_line(v, o[0]) for v, o in zip(self.halves(value), self.orders())]

    def stack_two(self, lines, mark):
        out = []
        for line, order in zip(lines, self.orders()):
            both = jnp.concatenate(hold(line, mark), axis=0)
            out.append(self.hop_line(both, order[1]) if len(order) > 1 else [both])
        return out

    def stack_done(self, lines, mark):
        out = []
        for line, order in zip(lines, self.orders()):
            line = hold(line, mark)
            if order == (1, 2):
                n = self.dims[1]
                rows = line[0].shape[0] // n
                line = [v[s * rows : (s + 1) * rows] for s in range(n) for v in line]
            out.append(jnp.concatenate(line, axis=0))
        return out

    def send_rows(self, value):
        size = value.shape[0] // self.plane
        out = []
        for offset in self.offsets:
            part = 0
            for axis, by in enumerate(offset):
                n = self.dims[axis + 1]
                part = part * n + (self.own(axis + 1) + by) % n
            piece = lax.dynamic_slice_in_dim(value, part * size, size, 0)
            out.append(self.offset_by(piece, offset) if any(offset) else piece)
        return out

    def line_send(self, value):
        n = self.dims[0]
        rows = value.shape[0] // n
        own = self.own(0)
        out = [lax.dynamic_slice_in_dim(value, own * rows, rows, 0)]
        for j in range(1, n):
            piece = lax.dynamic_slice_in_dim(value, ((own + j) % n) * rows, rows, 0)
            out.append(self.along(piece, 0, j))
        return out

    def gather_one(self, halves):
        return [self.hop_line(v, o[0]) for v, o in zip(halves, self.orders())]

    def gather_two(self, lines, mark):
        out = []
        for line, order in zip(lines, self.orders()):
            line = hold(line, mark)
            own = self.own(order[0])
            if len(order) == 1:
                out.append([in_order(line, own, 0)])
            else:
                both = in_order(line, own, 0)
                out.append(self.hop_line(both, order[1]))
        return out

    def gather_done(self, lines, mark):
        out = []
        for line, order in zip(lines, self.orders()):
            line = hold(line, mark)
            if len(order) == 1:
                out.append(line[0])
            elif order == (1, 2):
                n = self.dims[1]
                rows = line[0].shape[0] // n
                cut = [[v[i * rows : (i + 1) * rows] for v in line] for i in range(n)]
                out += [jnp.concatenate([in_order(v, self.own(2), 0) for v in cut], axis=0)]
            else:
                out.append(in_order(line, self.own(order[1]), 0))
        return jnp.concatenate(out, axis=1)


def after(value, *others):
    return lax.optimization_barrier((value, *others))[0]


def hold(values, *others):
    return [values[0]] + [tie(v, *others) for v in values[1:]]


def add_up(values):
    return sum([v.astype(single) for v in values[1:]], values[0].astype(single)).astype(bfloat)


def split(value, widths):
    out, start = [], 0
    for width in widths:
        out.append(value[:, start : start + width])
        start += width
    return out


def in_order(pieces, own, axis):
    n = len(pieces)
    if n == 1:
        return pieces[0]
    if n == 2:
        return jnp.where(
            own == 0,
            jnp.concatenate(pieces, axis=axis),
            jnp.concatenate([pieces[1], pieces[0]], axis=axis),
        )
    turned = pieces[::-1]
    line = jnp.concatenate(turned + turned[:-1], axis=axis)
    extent = pieces[0].shape[axis]
    return lax.dynamic_slice_in_dim(line, (n - 1 - own) * extent, n * extent, axis)


class Cores:
    def __init__(self, count):
        self.count = count
        self.own = lax.axis_index("shard")

    def along(self, value, by):
        n = self.count
        return lax.ppermute(value, "shard", [(i, (i + by) % n) for i in range(n)])

    def spread(self, value):
        return [value] + [self.along(value, j) for j in range(1, self.count)]

    def whole(self, value, axis):
        return in_order(self.spread(value), self.own, axis)

    def chunk(self, value, j, axis):
        size = value.shape[axis] // self.count
        place = (self.own + j + self.count) % self.count
        return lax.dynamic_slice_in_dim(value, place * size, size, axis)

    def rows_times(self, left, pieces):
        out = None
        for j, piece in enumerate(pieces):
            term = dot(self.chunk(left, -j, 1), piece)
            out = term if out is None else out + term
        return out

    def times_rows_t(self, left, pieces):
        return in_order([dot_t(left, piece) for piece in pieces], self.own, 1)

    def swap_columns(self, *values):
        out = []
        for j in range(self.count):
            piece = jnp.concatenate([self.chunk(v, j, 1) for v in values], axis=1)
            out.append(self.along(piece, j) if j else piece)
        return split(jnp.concatenate(out, axis=0), [v.shape[1] // self.count for v in values])

    def stack(self, value):
        return jnp.concatenate(self.spread(value), axis=0)

    def give_back(self, value):
        rows = value.shape[0] // self.count
        total = value[:rows]
        for j in range(1, self.count):
            total = total + self.along(value[j * rows : (j + 1) * rows], -j)
        return total

    def scatter(self, value, axis):
        total = self.chunk(value, 0, axis).astype(single)
        for j in range(1, self.count):
            total = total + self.along(self.chunk(value, j, axis).astype(bfloat), j).astype(single)
        return total


def per_device(
    chips,
    shards,
    tokens,
    segment_ids,
    routes,
    cotangent,
    gain_attn,
    gain_query,
    gain_latent,
    gain_ffn,
    w_qa,
    w_qb,
    w_kva,
    w_kvb,
    w_out,
    w_router,
    shared_gate,
    shared_up,
    shared_down,
    expert_gate,
    expert_up,
    expert_down,
):
    cores = Cores(shards)
    me = chips.me()
    shard_pos = cores.own
    tok_rows = tokens.shape[0]
    model = tokens.shape[1]
    group_rows = tok_rows * shards
    score_scale = 1.0 / (DN + DR) ** 0.5
    query_rank = w_qa.shape[1]

    gains = jnp.concatenate([gain_attn, gain_query, gain_latent, gain_ffn])
    gain_pieces = cores.spread(gains)
    sizes = [v.shape[0] for v in (gain_attn, gain_query, gain_latent, gain_ffn)]
    full_gains = []
    start = 0
    for size in sizes:
        full_gains.append(
            in_order([g[start : start + size] for g in gain_pieces], shard_pos, 0).astype(single)
        )
        start += size
    gain_attn_f, gain_query_f, gain_latent_f, gain_ffn_f = full_gains
    qa_pieces = cores.spread(w_qa)
    kva_pieces = cores.spread(w_kva)
    qb_pieces = cores.spread(w_qb)
    kvb_pieces = cores.spread(w_kvb)
    out_pieces = cores.spread(w_out)
    router_full = cores.whole(w_router, 0)
    expert_weights = [
        cores.spread(expert_gate[0].T),
        cores.spread(expert_up[0].T),
        cores.spread(expert_down[0]),
    ]
    turns = chips.dims[0]
    order = [0] + list(range(2, turns, 2)) + list(range(1, turns, 2))
    all_cots = lax.all_gather(cotangent, chips.names, axis=0, tiled=True)

    resid = tokens.astype(single)
    attn_scale = row_scale(resid)
    attn_normed = resid * attn_scale
    attn_in = (attn_normed * gain_attn_f).astype(bfloat)
    query_lat = cores.rows_times(attn_in, qa_pieces)
    query_scale = row_scale(query_lat)
    query_normed = query_lat * query_scale
    query_in = (query_normed * gain_query_f).astype(bfloat)
    query_all = cores.rows_times(query_in, qb_pieces)
    group_pos = seq_positions(segment_ids)
    own_start = shard_pos * tok_rows
    own_pos = lax.dynamic_slice_in_dim(group_pos, own_start, tok_rows, 0)
    own_seg = lax.dynamic_slice_in_dim(segment_ids, own_start, tok_rows, 0)
    cosine, sine = rope_tables(own_pos, DR // 2)
    latent_raw = cores.rows_times(attn_in, kva_pieces)
    latent_part = latent_raw[:, :KR]
    latent_scale = row_scale(latent_part)
    latent_normed = latent_part * latent_scale
    latent = (latent_normed * gain_latent_f).astype(bfloat)
    key_rope = rotate(latent_raw[:, KR:], cosine, sine).astype(bfloat)
    keys = cores.whole(jnp.concatenate([latent, key_rope], axis=1), 0)
    keys_latent, keys_rope = keys[:, :KR], keys[:, KR:]
    keys_turned = jnp.concatenate(
        [cores.chunk(keys_latent, -j, 1) for j in range(shards)], axis=1
    )
    group_index = jnp.arange(group_rows, dtype=jnp.int32)
    own_index = own_start + jnp.arange(tok_rows, dtype=jnp.int32)
    visible = (own_seg[:, None] == segment_ids[None, :]) & (
        group_index[None, :] <= own_index[:, None]
    )

    attn_heads, *saved = run_heads(
        query_all,
        kvb_pieces,
        keys_turned,
        keys_rope,
        visible.astype(single),
        cosine,
        sine,
        H,
        score_scale,
    )
    mid = resid + cores.rows_times(attn_heads, out_pieces)
    ffn_scale = row_scale(mid)
    ffn_normed = mid * ffn_scale
    ffn_in = (ffn_normed * gain_ffn_f).astype(bfloat)

    experts_all = router_full.shape[1]
    lanes = -(-4 * experts_all // 128) * 128
    logits = dot(ffn_in, router_full)
    chosen = jnp.sum(
        (routes[:, :, None] == jnp.arange(experts_all, dtype=jnp.int32)[None, None, :]).astype(
            single
        ),
        axis=1,
    )
    sig = jax.nn.sigmoid(logits)
    denom = jnp.sum(chosen * sig, axis=-1, keepdims=True)
    routing_weights = route_scale * chosen * sig / denom
    capacity = min(tok_rows, 4 * tok_rows * TOP // (3 * experts_all))
    earlier = (jnp.arange(tok_rows)[:, None] > jnp.arange(tok_rows)[None, :]).astype(bfloat)
    slot = dot(earlier, chosen.astype(bfloat))
    code = jnp.where(chosen > 0, slot, -1.0)
    weight_high = routing_weights.astype(bfloat)
    weight_rest = (routing_weights - weight_high.astype(single)).astype(bfloat)
    marks = jnp.concatenate(
        [
            code.astype(bfloat),
            weight_high,
            weight_rest,
            jnp.zeros((tok_rows, lanes - 3 * experts_all), bfloat),
        ],
        axis=1,
    )
    payload = jnp.concatenate([ffn_in, marks], axis=1)
    first = chips.first(payload)
    one, two = [None] * turns, [None] * turns
    two[0] = chips.straight(payload)
    one[1] = None

    stack_ffn = cores.stack(ffn_in)
    stack_cot = cores.stack(cotangent)

    def feed_forward(rows, grads, gate, up, down):
        pre_gate = dot(rows, gate)
        pre_up = dot(rows, up)
        hidden = (jax.nn.silu(pre_gate) * pre_up).astype(bfloat)
        grad_gate, grad_up = silu_grads(dot_t(grads, down), pre_gate, pre_up)
        return hidden, grad_gate, grad_up

    def got_two(j, *others):
        out = []
        for own, got in back_two[j]:
            total = own.astype(single)
            for v in got:
                total = total + tie(v, *others).astype(single)
            out.append(total)
        return out

    def got_one(j, *others):
        own, got = back_one[j]
        for v in got:
            own = own + tie(v, *others).astype(single)
        return own

    sh_hidden, sh_gate, sh_up = feed_forward(
        stack_ffn, stack_cot, shared_gate, shared_up, shared_down
    )
    sh_back = dot_t(sh_gate, shared_gate) + dot_t(sh_up, shared_up)
    shared_out = cores.give_back(dot(sh_hidden, shared_down))
    shared_back = cores.give_back(sh_back)

    who = jnp.concatenate([me.astype(jnp.int32).reshape(1), chips.sources()])
    kept = None
    back_blocks, out_blocks = [None] * turns, [None] * turns
    sent, grads_of = [], []

    def others_part(i, waits):
        base = 4 + ((i + 1) % 3) * shards
        left = kept[base : base + shards]
        right = kept[1] if i == 2 else kept[0]
        out = [t_dot(tie(v, *waits), right).astype(bfloat) for v in left[1:]]
        sent.append([cores.along(v, -j - 1) for j, v in enumerate(out)])
        return out[-1]

    def own_part(i, waits):
        left = kept[4 + ((i + 1) % 3) * shards]
        right = kept[1] if i == 2 else kept[0]
        got = [tie(v, *waits).astype(single) for v in sent[i]]
        grads_of.append(sum(got, t_dot(tie(left, *waits), right)))
        return grads_of[-1]

    fillers = [
        lambda waits: others_part(1, [others_part(0, waits)]),
        lambda waits: own_part(0, [others_part(2, waits)]),
        lambda waits: own_part(2, [own_part(1, waits)]),
    ]
    mark = sh_back
    backs = [None] * turns
    for step in range(turns + 2):
        waits = []
        if step + 1 < turns:
            k = order[step + 1]
            if step == 0:
                first[k] = tie(first[k], mark)
                two[k] = chips.straight(first[k])
                waits.append(first[k])
            else:
                one[k] = hold(one[k], mark)
                two[k] = chips.hop_two(one[k], k)
                waits += one[k]
        if step + 2 < turns:
            k = order[step + 2]
            first[k] = tie(first[k], mark)
            one[k] = chips.hop_one(first[k], k)
            waits.append(first[k])
        if 2 <= step:
            k = order[step - 2]
            total = add_up(hold(backs[k], mark))
            backs[k] = chips.back_first(total, k)
            waits.append(total)
        if step >= turns:
            mark = fillers[step - turns](waits)
            continue
        j = order[step]
        back_blocks[j], out_blocks[j], kept = run_experts(
            who,
            two[j],
            all_cots,
            expert_weights,
            capacity,
            experts_all,
            j,
            turns,
            kept,
            waits,
        )
        backs[j] = chips.straight_back(back_blocks[j])
        mark = back_blocks[j][0]
    routed_back = backs[0].astype(single)
    for j in order[1:]:
        routed_back = routed_back + tie(backs[j], mark).astype(single)
    chip_ffn, chip_cot = kept[2:4]

    grad_out = cotangent.astype(single)
    grad_weights = (
        routed_back[:, model : model + experts_all]
        + routed_back[:, model + experts_all : model + 2 * experts_all]
    )
    grad_sig = chosen * (
        route_scale * grad_weights / denom
        - jnp.sum(grad_weights * routing_weights, axis=-1, keepdims=True) / denom
    )
    grad_logits = grad_sig * sig * (1.0 - sig)
    grad_router = jnp.einsum("te,td->ed", grad_logits, ffn_in.astype(single), precision=highest)
    grad_ffn_in = (
        routed_back[:, :model]
        + shared_back
        + jnp.einsum("te,de->td", grad_logits, router_full.astype(single), precision=highest)
    )
    grad_mid, grad_gffn = norm_back(grad_ffn_in, ffn_normed, ffn_scale, gain_ffn_f)
    grad_mid = grad_mid + grad_out

    grad_attn_out = grad_mid.astype(bfloat)
    heads_line = chips.stack_one(cores.stack(grad_attn_out))
    lefts = cores.swap_columns(attn_in, query_in, tie(attn_heads, mark))
    lefts = chips.swap_columns(*[tie(v, grad_attn_out) for v in lefts])
    mark = fillers[2]([grad_attn_out, heads_line[0][0]])
    grad_egate = grads_of[0].T[None]
    grad_eup = grads_of[1].T[None]
    grad_edown = grads_of[2][None]
    grad_heads = cores.times_rows_t(tie(grad_attn_out, mark), out_pieces).astype(bfloat)
    heads_line = chips.stack_two(heads_line, grad_heads)
    grad_query, kvb_parts, key_terms, rope_terms = run_heads_back(
        grad_heads,
        kvb_pieces,
        keys_turned,
        keys_rope,
        cosine,
        sine,
        saved,
        H,
        score_scale,
        [v[0] for v in heads_line],
    )
    query_line = chips.stack_one(cores.stack(grad_query))
    kvb_terms = add_up(
        [kvb_parts[0]] + [cores.along(v, -j - 1) for j, v in enumerate(kvb_parts[1:])]
    )
    kvb_line = chips.send_rows(kvb_terms)
    size = KR // shards
    key_terms = in_order(
        [key_terms[:, j * size : (j + 1) * size] for j in range(shards)], shard_pos, 1
    )
    grad_keys = cores.scatter(jnp.concatenate([key_terms, rope_terms], axis=1), 0)
    grad_latent, grad_krope = grad_keys[:, :KR], grad_keys[:, KR:]
    grad_query_in = cores.times_rows_t(grad_query, qb_pieces)
    grad_qlat, grad_gquery = norm_back(grad_query_in, query_normed, query_scale, gain_query_f)
    grad_kvpart, grad_glatent = norm_back(grad_latent, latent_normed, latent_scale, gain_latent_f)
    grad_kvrope = rotate_back(grad_krope, cosine, sine)
    grad_low = jnp.concatenate([grad_qlat, grad_kvpart, grad_kvrope], axis=-1).astype(bfloat)
    shared_weights = (shared_gate, shared_up, shared_down)
    xs, cs = cores.spread(tie(chip_ffn, routed_back)), cores.spread(tie(chip_cot, routed_back))
    widths = widths_of(shared_gate.shape[1]) if shards == 2 else []
    shared_grads = None
    start = 0

    def shared_step(waits):
        nonlocal shared_grads, start
        if not widths:
            return waits[0]
        width = widths.pop(0)
        shared_grads = run_shared(xs, cs, shared_weights, start, width, shared_grads, waits)
        start += width
        return shared_grads[0]

    low_wide = jnp.pad(grad_low, ((0, 0), (0, -grad_low.shape[1] % 128)))
    low_line = chips.straight(cores.stack(low_wide))
    query_line = chips.stack_two(query_line, grad_low)
    lefts = jnp.concatenate(hold(lefts, grad_low), axis=0)
    sizes = [v.shape[1] // (shards * chips.plane) for v in (attn_in, query_in, attn_heads)]
    left_in, left_query, left_heads = split(lefts, sizes)
    heads_all = chips.stack_done(heads_line, grad_low)
    out_part = [t_dot(left_heads, right).astype(bfloat) for right in heads_all]
    kvb_part = add_up(hold(kvb_line, out_part[0]))
    fold = left_heads.shape[1] // kvb_part.shape[0]
    kvb_cols = kvb_part.shape[1] // fold
    kvb_part = jnp.concatenate(split(kvb_part, [kvb_cols] * fold), axis=0)
    part = jnp.concatenate([kvb_part, *out_part], axis=1)
    part_sums = lax.psum_scatter(part, chips.names[0], scatter_dimension=0, tiled=True)
    mark = shared_step([part, low_line[0]] + [v[0] for v in query_line])
    part_all = lax.all_gather(tie(part_sums, mark), chips.names[0], axis=0, tiled=True)
    grad_low = tie(grad_low, mark)
    grad_attn_in = in_order(
        [
            dot_t(grad_low[:, :query_rank], qa) + dot_t(grad_low[:, query_rank:], kva)
            for qa, kva in zip(qa_pieces, kva_pieces)
        ],
        shard_pos,
        1,
    )
    grad_resid, grad_gattn = norm_back(grad_attn_in, attn_normed, attn_scale, gain_attn_f)
    grad_tokens = grad_mid + grad_resid
    mixed = jnp.concatenate(
        [grad_gquery.reshape(shards, -1), grad_glatent.reshape(shards, -1)], axis=1
    ).reshape(-1)
    small = jnp.concatenate(
        [grad_gattn[None], grad_gffn[None], mixed[None], grad_router], axis=0
    )
    small_line = chips.send_rows(cores.scatter(small, 1).T.astype(bfloat))
    query_all = chips.stack_done(query_line, mark)
    query_part = jnp.concatenate(
        [t_dot(left_query, right).astype(bfloat) for right in query_all], axis=1
    )
    query_sums = lax.psum_scatter(query_part, chips.names[0], scatter_dimension=0, tiled=True)
    low_all = jnp.concatenate(hold(low_line, mark), axis=0)
    low_part = t_dot(left_in, low_all).astype(bfloat)
    small_part = add_up(hold(small_line, query_part))
    low_cols = grad_low.shape[1]
    spare = low_part.shape[1] - low_cols - small_part.shape[1]
    low_part = jnp.concatenate(
        [low_part[:, :low_cols], jnp.pad(small_part, ((0, 0), (0, spare)))], axis=1
    )
    low_line = chips.line_send(low_part)
    turn_of = [j % 2 == 1 for j in range(turns)]
    back_two = [
        chips.back_two([tie(v, mark) for v in out_blocks[j]], j, turn_of[j])
        for j in range(turns)
    ]
    mark = shared_step([query_part, low_line[0]])
    part_line = chips.gather_one(chips.halves(tie(part_all, mark)))
    query_all = lax.all_gather(tie(query_sums, mark), chips.names[0], axis=0, tiled=True)
    low_line = chips.hop_line(add_up(hold(low_line, mark)), 0)
    back_one = [chips.back_one(got_two(j, mark), j, turn_of[j]) for j in range(turns)]
    waits = [v[0] for v in part_line] + [v[0] for v in back_one]
    mark = shared_step(waits + [low_line[0]])
    low_all = in_order(hold(low_line, mark), chips.own(0), 0)
    low_line = chips.gather_one(chips.halves(low_all))
    query_line = chips.gather_one(chips.halves(tie(query_all, mark)))
    part_line = chips.gather_two(part_line, mark)
    back_sums = [chips.back_first(got_one(j, mark), j) for j in range(turns)]
    waits = [v[0] for line in (part_line, query_line, low_line) for v in line]
    mark = shared_step(waits + back_sums)
    low_line = chips.gather_two(low_line, mark)
    query_line = chips.gather_two(query_line, mark)
    routed_out = back_sums[0]
    for j in range(1, turns):
        routed_out = routed_out + tie(back_sums[j], mark).astype(single)
    result = mid + shared_out + routed_out
    cuts = [kvb_cols, w_out.shape[1]]
    low_cuts = [query_rank, low_cols - query_rank, small_part.shape[1] + spare]
    if len(chips.dims) == 3:
        part_line = [hold(v, mark) for v in part_line]
        grad_wkvb, grad_wout = assemble(chips, part_line, cuts, fold, ())
        low_line = [hold(v, grad_wout, result) for v in low_line]
        grad_wqa, grad_wkva, small = assemble(chips, low_line, low_cuts, 1, (1,))
        grad_wkva = grad_wkva.T
        query_line = [hold(v, grad_wqa) for v in query_line]
        (grad_wqb,) = assemble(chips, query_line, [w_qb.shape[1]], 1, ())
    else:
        part_all = chips.gather_done(part_line, mark).astype(single)
        kvb_all, grad_wout = split(part_all, cuts)
        kvb_all = kvb_all.reshape(chips.plane, fold, -1, kvb_cols)
        grad_wkvb = kvb_all.swapaxes(1, 2).reshape(-1, fold * kvb_cols)
        low_all = chips.gather_done(low_line, mark).astype(single)
        grad_wqa, grad_wkva, small = split(low_all, low_cuts)
        grad_wqb = chips.gather_done(query_line, mark).astype(single)

    if shards == 2:
        grad_sgate, grad_sup, grad_sdown = shared_grads
    else:
        grad_sgate = grad_sup = grad_sdown = 0.0
        all_ffn, all_cot = chip_ffn, chip_cot
        for turn in range(shards):
            if turn > 0:
                tied = lax.optimization_barrier(
                    (all_ffn, all_cot, grad_sgate, grad_sup, grad_sdown)
                )
                grad_sgate, grad_sup, grad_sdown = tied[2:]
                all_ffn, all_cot = cores.along(tied[0], 1), cores.along(tied[1], 1)
            all_hidden, all_gate, all_up = feed_forward(
                all_ffn, all_cot, shared_gate, shared_up, shared_down
            )
            grad_sgate = grad_sgate + t_dot(all_ffn, all_gate)
            grad_sup = grad_sup + t_dot(all_ffn, all_up)
            grad_sdown = grad_sdown + t_dot(all_hidden, all_cot)
    query_part = gain_query.shape[0]
    return (
        result,
        grad_tokens,
        small[:, 0],
        small[:query_part, 2],
        small[query_part:, 2],
        small[:, 1],
        grad_wqa,
        grad_wqb,
        grad_wkva,
        grad_wkvb,
        grad_wout,
        small[:, 3 : 3 + experts_all],
        grad_sgate,
        grad_sup,
        grad_sdown,
        grad_egate,
        grad_eup,
        grad_edown,
    )


def solution(mesh):
    shards = mesh.shape["shard"]
    dims = grid_of(mesh.shape["expert"], shards)
    names = tuple(f"line{i}" for i in range(len(dims)))
    grid = jax.sharding.Mesh(mesh.devices.reshape(dims + (shards,)), names + ("shard",))
    chips = Chips(dims, names)
    both = names + ("shard",)
    in_specs = (
        P(both, None),
        P(names),
        P(both, None),
        P(both, None),
        P("shard"),
        P("shard"),
        P("shard"),
        P("shard"),
        P("shard", None),
        P("shard", None),
        P("shard", None),
        P("shard", None),
        P("shard", None),
        P("shard", None),
        P(None, "shard"),
        P(None, "shard"),
        P("shard", None),
        P(names, None, "shard"),
        P(names, None, "shard"),
        P(names, "shard", None),
    )
    out_specs = (
        P(both, None),
        P(both, None),
        P("shard"),
        P("shard"),
        P("shard"),
        P("shard"),
        P("shard", None),
        P("shard", None),
        P("shard", None),
        P("shard", None),
        P("shard", None),
        P("shard", None),
        P(None, "shard"),
        P(None, "shard"),
        P("shard", None),
        P(names, None, "shard"),
        P(names, None, "shard"),
        P(names, "shard", None),
    )

    def body(*args):
        return per_device(chips, shards, *args)

    return jax.shard_map(
        body, mesh=grid, in_specs=in_specs, out_specs=out_specs, check_vma=False
    )
```

```python
import functools
import math

import jax
import jax.numpy as jnp
import numpy as np
from jax import lax
from jax.experimental import pallas as pl
from jax.experimental.pallas import tpu as pltpu
from jax.sharding import PartitionSpec as P

H = 16
DN = 128
DR = 64
DV = 128
KR = 512
TOP = 6


norm_eps = 1e-06
rope_base = 50000.0
route_scale = 2.446
masked_score = -1e30
highest = lax.Precision.HIGHEST
bfloat = jnp.bfloat16
single = jnp.float32


def row_scale(values):
    return lax.rsqrt(jnp.mean(values * values, axis=-1, keepdims=True) + norm_eps)


def norm_back(grad_out, normed_rows, scale_rows, gain):
    grad_normed = grad_out * gain
    grad_input = scale_rows * (
        grad_normed - normed_rows * jnp.mean(grad_normed * normed_rows, axis=-1, keepdims=True)
    )
    return (grad_input, jnp.sum(grad_out * normed_rows, axis=0))


def seq_positions(segments):
    token_count = segments.shape[0]
    index = jnp.arange(token_count, dtype=jnp.int32)
    change = jnp.concatenate([jnp.ones((1,), bool), segments[1:] != segments[:-1]])
    starts = lax.cummax(jnp.where(change, index, 0), axis=0)
    return index - starts


def rope_tables(positions, half):
    freq = rope_base ** (-jnp.arange(half, dtype=jnp.float32) / half)
    angles = positions.astype(jnp.float32)[:, None] * freq[None, :]
    return (jnp.cos(angles), jnp.sin(angles))


def rotate(values, cosine, sine):
    half = values.shape[-1] // 2
    first = values[..., :half]
    second = values[..., half:]
    return jnp.concatenate(
        [first * cosine - second * sine, second * cosine + first * sine], axis=-1
    )


def rotate_back(grads, cosine, sine):
    half = grads.shape[-1] // 2
    first = grads[..., :half]
    second = grads[..., half:]
    return jnp.concatenate(
        [first * cosine + second * sine, second * cosine - first * sine], axis=-1
    )


def silu_grads(grad_hidden, pre_gate, pre_up):
    sigma = jax.nn.sigmoid(pre_gate)
    grad_gate = grad_hidden * pre_up * sigma * (1.0 + pre_gate * (1.0 - sigma))
    grad_up = grad_hidden * pre_gate * sigma
    return (grad_gate.astype(bfloat), grad_up.astype(bfloat))


def dot(left, right):
    return jnp.dot(left, right, preferred_element_type=single)


def dot_t(left, right):
    return lax.dot_general(left, right, (((1,), (1,)), ((), ())), preferred_element_type=single)


def t_dot(left, right):
    return lax.dot_general(left, right, (((0,), (0,)), ((), ())), preferred_element_type=single)


def expert_marks(marks, me, experts, capacity):
    marks = marks.astype(single)
    lane = lax.broadcasted_iota(jnp.int32, marks.shape, 1)
    place = lax.broadcasted_iota(jnp.int32, (marks.shape[0], capacity), 1).astype(single)
    code = jnp.sum(jnp.where(lane == me, marks, 0.0), axis=1, keepdims=True)
    weight = (lane == me + experts) | (lane == me + 2 * experts)
    weight = jnp.sum(jnp.where(weight, marks, 0.0), axis=1, keepdims=True)
    return (code == place).astype(single).astype(bfloat), weight, lane


def views(arrays, tok):
    return [(v, at) for v in arrays for at in range(0, v.shape[0], tok)]


def expert_kernel(arrays, tok, pieces, capacity, experts, group, places, first, waits, *refs):
    refs = list(refs)
    me_ref = refs.pop(0)
    count = len(places)
    blocks = views([refs.pop(0) for _ in range(arrays)], tok)
    weights = [[refs.pop(0) for _ in range(pieces)] for _ in range(3)]
    refs = refs[waits:]
    if not first:
        refs = refs[5 + pieces + count :]
    mark = refs.pop(0)
    rows_all, ffn_all, gate_all, up_all, out_all = (refs.pop(0) for _ in range(5))
    hidden_all = [refs.pop(0) for _ in range(pieces)]
    packs = [refs.pop(0) for _ in range(count)]
    full = [refs.pop(0) for _ in range(3)]
    rows, gate_scr, up_scr, out_scr = (refs.pop(0) for _ in range(4))
    hidden_scr = [refs.pop(0) for _ in range(pieces)]
    outs = refs.pop(0)
    sem_w, sem_o = refs
    model = rows.shape[1]
    width = weights[0][0].shape[0]
    loads = [[], [], []]
    for k in range(3):
        for j in range(pieces):
            c = pltpu.make_async_copy(
                weights[k][j], full[k].at[pl.ds(j * width, width)], sem_w.at[k, j]
            )
            c.start()
            loads[k].append(c)
    stores = []

    def store(src, dst):
        c = pltpu.make_async_copy(src, dst, sem_o.at[len(stores)])
        c.start()
        stores.append(c)

    me = me_ref[0]
    n = count * capacity
    mine = pl.ds(group * n, n)
    picks = []
    for i in range(count):
        ref, at = blocks[i]
        pick, weight, _ = expert_marks(
            ref[at : at + tok, model : model + 128], me, experts, capacity
        )
        picks.append((pick, weight))
        rows[pl.ds(i * capacity, capacity)] = t_dot(pick, ref[at : at + tok, :model]).astype(bfloat)
    store(rows, rows_all.at[mine])
    for i in range(count):
        store(
            blocks[i][0].at[pl.ds(blocks[i][1], tok), pl.ds(0, model)],
            ffn_all.at[pl.ds((group * count + i) * tok, tok)],
        )
    for c in loads[0]:
        c.wait()
    pre_gate = dot_t(rows[...], full[0][...])
    gate_scr[...] = pre_gate
    store(gate_scr, gate_all.at[mine])
    for c in loads[1]:
        c.wait()
    pre_up = dot_t(rows[...], full[1][...])
    up_scr[...] = pre_up
    store(up_scr, up_all.at[mine])
    hidden = (pre_gate * jax.nn.sigmoid(pre_gate) * pre_up).astype(bfloat)
    for j in range(pieces):
        hidden_scr[j][...] = hidden[:, j * width : (j + 1) * width]
        store(hidden_scr[j], hidden_all[j].at[mine])
    for c in loads[2]:
        c.wait()
    out = dot(hidden, full[2][...]).astype(bfloat)
    out_scr[...] = out
    store(out_scr, out_all.at[mine])
    for i, (pick, weight) in enumerate(picks):
        got = dot(pick, out[i * capacity : (i + 1) * capacity])
        outs[i] = (weight * got).astype(bfloat)
        pack, at = places[i]
        store(outs.at[i], packs[pack].at[pl.ds(at * tok, tok)])
    mark[...] = jnp.zeros_like(mark)
    for c in stores:
        c.wait()


def run_experts(me, blocks, weights, capacity, experts, group, groups, places, carried, others):
    count, pieces = len(places), len(weights[0])
    tok, model = sum(v.shape[0] for v in blocks) // count, weights[0][0].shape[1]
    width = weights[0][0].shape[0]
    n = count * capacity
    shape = jax.ShapeDtypeStruct
    kept = [
        shape((groups * n, model), bfloat),
        shape((groups * count * tok, model), bfloat),
        shape((groups * n, pieces * width), single),
        shape((groups * n, pieces * width), single),
        shape((groups * n, model), bfloat),
    ] + [shape((groups * n, width), bfloat)] * pieces
    kept += [shape((groups * tok, model), bfloat)] * count
    vm = pl.BlockSpec(memory_space=pltpu.VMEM)
    hbm = pl.BlockSpec(memory_space=pl.ANY)
    flat = [w for ws in weights for w in ws]
    operands = [me, *blocks, *flat, *others]
    in_specs = [pl.BlockSpec(memory_space=pltpu.SMEM)] + [vm] * len(blocks)
    in_specs += [hbm] * (len(flat) + len(others))
    alias = {}
    if carried is not None:
        alias = {len(operands) + i: 1 + i for i in range(len(kept))}
        operands += list(carried)
        in_specs += [hbm] * len(kept)
    out = pl.pallas_call(
        functools.partial(
            expert_kernel,
            len(blocks),
            tok,
            pieces,
            capacity,
            experts,
            group,
            places,
            carried is None,
            len(others),
        ),
        out_shape=[shape((16, 128), bfloat)] + kept,
        in_specs=in_specs,
        out_specs=[vm] + [hbm] * len(kept),
        input_output_aliases=alias,
        scratch_shapes=[pltpu.VMEM((pieces * width, model), bfloat)] * 3
        + [pltpu.VMEM((n, model), bfloat)]
        + [pltpu.VMEM((n, pieces * width), single)] * 2
        + [pltpu.VMEM((n, model), bfloat)]
        + [pltpu.VMEM((n, width), bfloat)] * pieces
        + [pltpu.VMEM((count, tok, model), bfloat)]
        + [pltpu.SemaphoreType.DMA((3, pieces)), pltpu.SemaphoreType.DMA((4 + 2 * count + pieces,))],
        compiler_params=pltpu.CompilerParams(vmem_limit_bytes=56 << 20),
        cost_estimate=pl.CostEstimate(flops=0, bytes_accessed=0, transcendentals=0),
    )(*operands)
    return out[0], out[1:]


def expert_back_kernel(
    arrays, results, tok, pieces, capacity, experts, group, first, waits, *refs
):
    refs = list(refs)
    me_ref = refs.pop(0)
    blocks = views([refs.pop(0) for _ in range(arrays)], tok)
    count = len(blocks)
    all_cots = refs.pop(0)
    weights = [[refs.pop(0) for _ in range(pieces)] for _ in range(3)]
    gate_all, up_all, out_all = (refs.pop(0) for _ in range(3))
    refs = refs[waits:]
    if not first:
        refs = refs[2 + 2 * pieces :]
    backs = views([refs.pop(0) for _ in range(results)], tok)
    grads_all, cot_all = refs.pop(0), refs.pop(0)
    acts = [[refs.pop(0) for _ in range(pieces)] for _ in range(2)]
    full = [refs.pop(0) for _ in range(3)]
    grads, gate_scr, up_scr, out_scr, cot_scr, mark_scr = (refs.pop(0) for _ in range(6))
    act_scr = [[refs.pop(0) for _ in range(pieces)] for _ in range(2)]
    sem_w, sem_i, sem_c, sem_o = refs
    model = grads.shape[1]
    width = weights[0][0].shape[0]
    n = count * capacity
    mine = pl.ds(group * n, n)

    def fetch(src, dst, sem):
        c = pltpu.make_async_copy(src, dst, sem)
        c.start()
        return c

    cots = []
    for i in range(count):
        source = pl.multiple_of(me_ref[1 + group * count + i] * tok, tok)
        cots.append(fetch(all_cots.at[pl.ds(source, tok)], cot_scr.at[i], sem_c.at[0, i]))
        marks = blocks[i][0].at[pl.ds(blocks[i][1], tok), pl.ds(model, 128)]
        cots.append(fetch(marks, mark_scr.at[i], sem_c.at[1, i]))
    loads = {}
    for k in (2, 0, 1):
        loads[k] = [
            fetch(weights[k][j], full[k].at[pl.ds(j * width, width)], sem_w.at[k, j])
            for j in range(pieces)
        ]
    saved = [
        fetch(gate_all.at[mine], gate_scr, sem_i.at[0]),
        fetch(up_all.at[mine], up_scr, sem_i.at[1]),
        fetch(out_all.at[mine], out_scr, sem_i.at[2]),
    ]
    stores = []

    def store(src, dst):
        stores.append(fetch(src, dst, sem_o.at[len(stores)]))

    me = me_ref[0]
    for c in cots:
        c.wait()
    picks = []
    for i in range(count):
        pick, weight, lane = expert_marks(mark_scr[i], me, experts, capacity)
        picks.append(pick)
        scaled = (weight * cot_scr[i].astype(single)).astype(bfloat)
        grads[pl.ds(i * capacity, capacity)] = t_dot(pick, scaled).astype(bfloat)
        store(cot_scr.at[i], cot_all.at[pl.ds((group * count + i) * tok, tok)])
    store(grads, grads_all.at[mine])
    for c in loads[2]:
        c.wait()
    grad_hidden = dot_t(grads[...], full[2][...])
    for c in saved:
        c.wait()
    pre_gate, pre_up = gate_scr[...], up_scr[...]
    sigma = jax.nn.sigmoid(pre_gate)
    grad_gate = grad_hidden * pre_up * sigma * (1.0 + pre_gate * (1.0 - sigma))
    grad_gate = grad_gate.astype(bfloat)
    grad_up = (grad_hidden * pre_gate * sigma).astype(bfloat)
    for k, v in enumerate((grad_gate, grad_up)):
        for j in range(pieces):
            act_scr[k][j][...] = v[:, j * width : (j + 1) * width]
            store(act_scr[k][j], acts[k][j].at[mine])
    for c in loads[0] + loads[1]:
        c.wait()
    back = (dot(grad_gate, full[0][...]) + dot(grad_up, full[1][...])).astype(bfloat)
    for i in range(count):
        here = slice(i * capacity, (i + 1) * capacity)
        got = dot(picks[i], out_scr[here])
        dots = jnp.sum(got * cot_scr[i].astype(single), axis=1, keepdims=True)
        ref, at = backs[i]
        ref[at : at + tok, :model] = dot(picks[i], back[here]).astype(bfloat)
        high = dots.astype(bfloat).astype(single)
        tail = jnp.where(lane == me, high, 0.0) + jnp.where(lane == me + experts, dots - high, 0.0)
        ref[at : at + tok, model : model + 128] = tail.astype(bfloat)
    for c in stores:
        c.wait()


def run_experts_back(
    me, blocks, all_cots, weights, saved, capacity, experts, group, groups, apart, carried, others
):
    pieces, model = len(weights[0]), weights[0][0].shape[1]
    count = saved[0].shape[0] // groups // capacity
    tok = sum(v.shape[0] for v in blocks) // count
    results = [tok] * count if apart else [v.shape[0] for v in blocks]
    width = weights[0][0].shape[0]
    n = count * capacity
    shape = jax.ShapeDtypeStruct
    kept = [shape((groups * n, model), bfloat), shape((groups * count * tok, model), bfloat)]
    kept += [shape((groups * n, width), bfloat)] * (2 * pieces)
    hbm = pl.BlockSpec(memory_space=pl.ANY)
    flat = [w for ws in weights for w in ws]
    operands = [me, *blocks, all_cots, *flat, *saved, *others]
    in_specs = [pl.BlockSpec(memory_space=pltpu.SMEM)] + [hbm] * (len(operands) - 1)
    alias = {}
    if carried is not None:
        alias = {len(operands) + i: len(results) + i for i in range(len(kept))}
        operands += list(carried)
        in_specs += [hbm] * len(kept)
    out = pl.pallas_call(
        functools.partial(
            expert_back_kernel,
            len(blocks),
            len(results),
            tok,
            pieces,
            capacity,
            experts,
            group,
            carried is None,
            len(others),
        ),
        out_shape=[shape((v, model + 128), bfloat) for v in results] + kept,
        in_specs=in_specs,
        out_specs=[pl.BlockSpec(memory_space=pltpu.VMEM)] * len(results) + [hbm] * len(kept),
        input_output_aliases=alias,
        scratch_shapes=[pltpu.VMEM((pieces * width, model), bfloat)] * 3
        + [pltpu.VMEM((n, model), bfloat)]
        + [pltpu.VMEM((n, pieces * width), single)] * 2
        + [
            pltpu.VMEM((n, model), bfloat),
            pltpu.VMEM((count, tok, model), bfloat),
            pltpu.VMEM((count, tok, 128), bfloat),
        ]
        + [pltpu.VMEM((n, width), bfloat)] * (2 * pieces)
        + [
            pltpu.SemaphoreType.DMA((3, pieces)),
            pltpu.SemaphoreType.DMA((3,)),
            pltpu.SemaphoreType.DMA((2, count)),
            pltpu.SemaphoreType.DMA((1 + count + 2 * pieces,)),
        ],
        compiler_params=pltpu.CompilerParams(vmem_limit_bytes=56 << 20),
        cost_estimate=pl.CostEstimate(flops=0, bytes_accessed=0, transcendentals=0),
    )(*operands)
    return out[: len(results)], out[len(results) :]


def shared_kernel(parts, tiles, start, width, first, waits, *refs):
    refs = list(refs)
    xs = [refs.pop(0) for _ in range(parts)]
    cs = [refs.pop(0) for _ in range(parts)]
    weights = [refs.pop(0) for _ in range(3)]
    refs = refs[waits:]
    if not first:
        refs = refs[3:]
    outs = [refs.pop(0) for _ in range(3)]
    wgu, wd = (refs.pop(0) for _ in range(2))
    accs = [refs.pop(0) for _ in range(2)]
    sem_w, sem_o = refs
    step = pl.program_id(0)
    cols = pl.ds(start, width)
    loads = [
        pltpu.make_async_copy(weights[0].at[:, cols], wgu.at[:, pl.ds(0, width)], sem_w.at[0]),
        pltpu.make_async_copy(weights[1].at[:, cols], wgu.at[:, pl.ds(width, width)], sem_w.at[1]),
        pltpu.make_async_copy(weights[2].at[cols], wd, sem_w.at[2]),
    ]

    @pl.when(step == 0)
    def _():
        for c in loads:
            c.start()
        for a in accs:
            a[...] = jnp.zeros_like(a)
        for c in loads:
            c.wait()

    def work(x_ref, c_ref):
        x, c = x_ref[...], c_ref[...]
        pre = dot(x, wgu[...])
        pre_gate, pre_up = pre[:, :width], pre[:, width:]
        grad_hidden = dot_t(c, wd[...])
        sigma = jax.nn.sigmoid(pre_gate)
        silu = pre_gate * sigma
        hidden = (silu * pre_up).astype(bfloat)
        grad_gate = (grad_hidden * pre_up * sigma * (1.0 + pre_gate * (1.0 - sigma))).astype(bfloat)
        grad_up = (grad_hidden * silu).astype(bfloat)
        accs[0][...] += t_dot(x, jnp.concatenate([grad_gate, grad_up], axis=1))
        accs[1][...] += t_dot(hidden, c)

    if parts == 1:
        work(xs[0], cs[0])
    else:
        per = tiles // parts
        for p in range(parts):
            pl.when(step // per == p)(functools.partial(work, xs[p], cs[p]))

    @pl.when(step == tiles - 1)
    def _():
        puts = [
            pltpu.make_async_copy(accs[0].at[:, pl.ds(0, width)], outs[0].at[:, cols], sem_o.at[0]),
            pltpu.make_async_copy(accs[0].at[:, pl.ds(width, width)], outs[1].at[:, cols], sem_o.at[1]),
            pltpu.make_async_copy(accs[1], outs[2].at[cols], sem_o.at[2]),
        ]
        for c in puts:
            c.start()
        for c in puts:
            c.wait()

def run_shared(xs, cs, weights, start, width, carried, others=(), tile=512):
    parts = len(xs)
    rows, model = xs[0].shape
    per = rows // tile
    tiles = per * parts
    shape = jax.ShapeDtypeStruct
    hbm = pl.BlockSpec(memory_space=pl.ANY)
    specs = [
        pl.BlockSpec((tile, model), lambda i, p=p: (jnp.clip(i - p * per, 0, per - 1), 0))
        for p in range(parts)
    ]
    outs = [shape(w.shape, single) for w in weights]
    operands = [*xs, *cs, *weights, *others]
    in_specs = specs + specs + [hbm] * (3 + len(others))
    alias = {}
    if carried is not None:
        alias = {len(operands) + i: i for i in range(3)}
        operands += list(carried)
        in_specs += [hbm] * 3
    return pl.pallas_call(
        functools.partial(shared_kernel, parts, tiles, start, width, carried is None, len(others)),
        grid=(tiles,),
        out_shape=outs,
        in_specs=in_specs,
        out_specs=[hbm] * 3,
        input_output_aliases=alias,
        scratch_shapes=[
            pltpu.VMEM((model, 2 * width), bfloat),
            pltpu.VMEM((width, model), bfloat),
            pltpu.VMEM((model, 2 * width), single),
            pltpu.VMEM((width, model), single),
            pltpu.SemaphoreType.DMA((3,)),
            pltpu.SemaphoreType.DMA((3,)),
        ],
        compiler_params=pltpu.CompilerParams(vmem_limit_bytes=60 << 20),
        cost_estimate=pl.CostEstimate(flops=0, bytes_accessed=0, transcendentals=0),
    )(*operands)


def turned(values, cosine, sine, way):
    half = values.shape[-1] // 2
    first, second = values[:, :half], values[:, half:]
    return jnp.concatenate(
        [first * cosine - way * second * sine, second * cosine + way * first * sine], axis=1
    )


def heads_kernel(pieces, score_scale, *refs):
    refs = list(refs)
    q_ref = refs.pop(0)
    kvbs = [refs.pop(0) for _ in range(pieces)]
    latent, rope, shown, cosine, sine = (refs.pop(0) for _ in range(5))
    heads_ref, nope_ref, qrope_ref, abs_ref, probs_ref, lat_ref = refs
    latents, ropes = latent[...], rope[...]
    visible = shown[...] > 0
    q = q_ref[...]
    rank = latents.shape[1]
    for h in range(2):
        nope = q[:, h * (DN + DR) : h * (DN + DR) + DN].astype(bfloat)
        tail = q[:, h * (DN + DR) + DN : (h + 1) * (DN + DR)]
        qrope = turned(tail, cosine[...], sine[...], 1.0).astype(bfloat)
        at = h * (DN + DV)
        w_uk = jnp.concatenate([w[:, at : at + DN] for w in kvbs], axis=0)
        w_uv = jnp.concatenate([w[:, at + DN : at + DN + DV] for w in kvbs], axis=0)
        query = dot_t(nope, w_uk).astype(bfloat)
        raw = dot_t(query, latents) + dot_t(qrope, ropes)
        scores = jnp.where(visible, raw * score_scale, masked_score)
        expd = jnp.exp(scores - jnp.max(scores, axis=1, keepdims=True))
        probs = expd / jnp.sum(expd, axis=1, keepdims=True)
        lat = dot(probs.astype(bfloat), latents).astype(bfloat)
        heads_ref[:, h * DV : (h + 1) * DV] = dot(lat, w_uv).astype(bfloat)
        nope_ref[:, h * DN : (h + 1) * DN] = nope
        qrope_ref[:, h * DR : (h + 1) * DR] = qrope
        abs_ref[:, h * rank : (h + 1) * rank] = query
        keys = probs.shape[1]
        probs_ref[:, h * keys : (h + 1) * keys] = probs
        lat_ref[:, h * rank : (h + 1) * rank] = lat


def heads_back_kernel(pieces, score_scale, *refs):
    refs = list(refs)
    g_ref = refs.pop(0)
    kvbs = [refs.pop(0) for _ in range(pieces)]
    latent, rope, cosine, sine = (refs.pop(0) for _ in range(4))
    nope_ref, qrope_ref, abs_ref, probs_ref, lat_ref = (refs.pop(0) for _ in range(5))
    gq_ref = refs.pop(0)
    gkvbs = [refs.pop(0) for _ in range(pieces)]
    key_ref, rope_out = refs
    latents, ropes = latent[...], rope[...]
    rank, keys = latents.shape[1], latents.shape[0]

    @pl.when(pl.program_id(0) == 0)
    def _():
        key_ref[...] = jnp.zeros_like(key_ref)
        rope_out[...] = jnp.zeros_like(rope_out)

    parts = []
    key_sum = key_ref[...]
    rope_sum = rope_out[...]
    for h in range(2):
        at = h * (DN + DV)
        w_uk = jnp.concatenate([w[:, at : at + DN] for w in kvbs], axis=0)
        w_uv = jnp.concatenate([w[:, at + DN : at + DN + DV] for w in kvbs], axis=0)
        grad = g_ref[:, h * DV : (h + 1) * DV]
        lat = lat_ref[:, h * rank : (h + 1) * rank]
        query = abs_ref[:, h * rank : (h + 1) * rank]
        nope = nope_ref[:, h * DN : (h + 1) * DN]
        qrope = qrope_ref[:, h * DR : (h + 1) * DR]
        probs = probs_ref[:, h * keys : (h + 1) * keys]
        grad_uv = t_dot(lat, grad).astype(bfloat)
        grad_lat = dot_t(grad, w_uv).astype(bfloat)
        grad_probs = dot_t(grad_lat, latents)
        delta = jnp.sum(probs * grad_probs, axis=1, keepdims=True)
        grad_scores = (probs * (grad_probs - delta)).astype(bfloat)
        grad_abs = (dot(grad_scores, latents) * score_scale).astype(bfloat)
        grad_rope = dot(grad_scores, ropes) * score_scale
        key_sum = key_sum + t_dot(grad_scores, query) * score_scale
        key_sum = key_sum + t_dot(probs.astype(bfloat), grad_lat)
        rope_sum = rope_sum + t_dot(grad_scores, qrope) * score_scale
        grad_uk = t_dot(grad_abs, nope).astype(bfloat)
        rows = rank // pieces
        for j in range(pieces):
            gkvbs[j][:, at : at + DN] = grad_uk[j * rows : (j + 1) * rows]
            gkvbs[j][:, at + DN : at + DN + DV] = grad_uv[j * rows : (j + 1) * rows]
        parts.append(dot(grad_abs, w_uk))
        parts.append(turned(grad_rope, cosine[...], sine[...], -1.0))
    gq_ref[...] = jnp.concatenate(parts, axis=1).astype(bfloat)
    key_ref[...] = key_sum
    rope_out[...] = rope_sum


def run_heads(q, kvbs, latent, rope, shown, cosine, sine, heads, score_scale):
    rows, pieces = q.shape[0], len(kvbs)
    keys, rank = latent.shape
    shape = jax.ShapeDtypeStruct
    own = lambda width: pl.BlockSpec((rows, width), lambda g: (0, g))
    still = lambda v: pl.BlockSpec(v.shape, lambda g: (0, 0))
    kvb = [pl.BlockSpec((w.shape[0], 2 * (DN + DV)), lambda g: (0, g)) for w in kvbs]
    widths = (DV, DN, DR, rank, keys, rank)
    kinds = (bfloat, bfloat, bfloat, bfloat, single, bfloat)
    return pl.pallas_call(
        functools.partial(heads_kernel, pieces, score_scale),
        grid=(heads // 2,),
        out_shape=[shape((rows, heads * w), k) for w, k in zip(widths, kinds)],
        in_specs=[own(2 * (DN + DR)), *kvb] + [still(v) for v in (latent, rope, shown, cosine, sine)],
        out_specs=[own(2 * w) for w in widths],
        compiler_params=pltpu.CompilerParams(vmem_limit_bytes=40 << 20),
        cost_estimate=pl.CostEstimate(flops=0, bytes_accessed=0, transcendentals=0),
    )(q, *kvbs, latent, rope, shown, cosine, sine)


def run_heads_back(grad, kvbs, latent, rope, cosine, sine, saved, heads, score_scale, others):
    rows, pieces = grad.shape[0], len(kvbs)
    keys, rank = latent.shape
    shape = jax.ShapeDtypeStruct
    own = lambda width: pl.BlockSpec((rows, width), lambda g: (0, g))
    still = lambda v: pl.BlockSpec(v.shape, lambda g: (0, 0))
    kvb = [pl.BlockSpec((w.shape[0], 2 * (DN + DV)), lambda g: (0, g)) for w in kvbs]
    widths = (DN, DR, rank, keys, rank)

    def body(*refs):
        cut = 1 + pieces + 4 + 5
        heads_back_kernel(pieces, score_scale, *refs[:cut], *refs[cut + len(others) :])

    out = pl.pallas_call(
        body,
        grid=(heads // 2,),
        out_shape=[shape((rows, heads * (DN + DR)), bfloat)]
        + [shape(w.shape, bfloat) for w in kvbs]
        + [shape((keys, rank), single), shape((keys, DR), single)],
        in_specs=[own(2 * DV), *kvb]
        + [still(v) for v in (latent, rope, cosine, sine)]
        + [own(2 * w) for w in widths]
        + [pl.BlockSpec(memory_space=pl.ANY)] * len(others),
        out_specs=[own(2 * (DN + DR)), *kvb]
        + [pl.BlockSpec((keys, rank), lambda g: (0, 0)), pl.BlockSpec((keys, DR), lambda g: (0, 0))],
        compiler_params=pltpu.CompilerParams(vmem_limit_bytes=40 << 20),
        cost_estimate=pl.CostEstimate(flops=0, bytes_accessed=0, transcendentals=0),
    )(grad, *kvbs, latent, rope, cosine, sine, *saved, *others)
    return out[0], out[1 : 1 + pieces], out[1 + pieces], out[2 + pieces]


def assemble_kernel(parts, cuts, fold, *refs):
    where, one_0, one_1, two_0, two_1, *outs = refs
    step = pl.program_id(0)
    _, m = parts
    row = jnp.where(step // m == where[0], one_0[...], one_1[...])
    column = jnp.where(step % m == where[1], two_0[...], two_1[...])
    value = jnp.concatenate([row, column], axis=1).astype(single)
    start = 0
    for i, (width, out) in enumerate(zip(cuts, outs)):
        piece = value[:, start : start + width]
        start += width
        if i == 0 and fold > 1:
            rows = piece.shape[0] // fold
            piece = jnp.concatenate(
                [piece[k * rows : (k + 1) * rows] for k in range(fold)], axis=1
            )
        if out.shape[0] == width and out.shape[0] != piece.shape[0]:
            piece = piece.T
        out[...] = piece


def assemble(chips, lines, cuts, fold, turned):
    n, m = chips.dims[1:]
    parts = n * m
    rows = lines[0][0].shape[0] * n // parts
    where = jnp.stack([chips.own(1), chips.own(2)]).astype(jnp.int32)
    one = pl.BlockSpec((rows, lines[0][0].shape[1]), lambda p: (p % m, 0))
    two = pl.BlockSpec((rows, lines[1][0].shape[1]), lambda p: (p // m, 0))
    shapes, specs = [], []
    for i, width in enumerate(cuts):
        if i == 0 and fold > 1:
            shapes.append((rows * parts // fold, width * fold))
            specs.append(pl.BlockSpec((rows // fold, width * fold), lambda p: (p, 0)))
        elif i in turned:
            shapes.append((width, rows * parts))
            specs.append(pl.BlockSpec((width, rows), lambda p: (0, p)))
        else:
            shapes.append((rows * parts, width))
            specs.append(pl.BlockSpec((rows, width), lambda p: (p, 0)))
    return pl.pallas_call(
        functools.partial(assemble_kernel, (n, m), cuts, fold),
        grid=(parts,),
        out_shape=[jax.ShapeDtypeStruct(v, single) for v in shapes],
        in_specs=[pl.BlockSpec(memory_space=pltpu.SMEM), one, one, two, two],
        out_specs=specs,
        compiler_params=pltpu.CompilerParams(vmem_limit_bytes=56 << 20),
        cost_estimate=pl.CostEstimate(flops=0, bytes_accessed=0, transcendentals=0),
    )(where, *lines[0], *lines[1])


def plane_kernel(count, rows, start, widths, fold, *refs):
    refs = list(refs)
    lefts = [refs.pop(0) for _ in range(count)]
    rights = [[refs.pop(0) for _ in range(rows)] for _ in widths]
    extra = refs[:-1]
    out = refs[-1]
    tok = lefts[0].shape[0] // rows
    cols = out.shape[0]
    at = 0
    if extra:
        kvb, small = extra
        size = kvb.shape[1] // fold
        for k in range(fold):
            here = pl.ds(k * kvb.shape[0], kvb.shape[0])
            out[here, :size] = kvb[:, k * size : (k + 1) * size]
        at = size
    for width, parts in zip(widths, rights):
        total = None
        for c in range(rows):
            for o in range(count):
                left = lefts[o][c * tok : (c + 1) * tok, start : start + cols]
                term = t_dot(left, parts[c][o * tok : (o + 1) * tok, :width])
                total = term if total is None else total + term
        value = total.astype(bfloat)
        if extra:
            value = jnp.concatenate([value, small[...]], axis=1)
        out[:, at : at + value.shape[1]] = value
        at += value.shape[1]


def plane_dot(lefts, start, cols, rights, widths, fold=1, extra=()):
    total = sum(widths)
    if extra:
        total += extra[0].shape[1] // fold + extra[1].shape[1]
    flat = [v for parts in rights for v in parts]
    vm = pl.BlockSpec(memory_space=pltpu.VMEM)
    return pl.pallas_call(
        functools.partial(plane_kernel, len(lefts), len(rights[0]), start, widths, fold),
        out_shape=jax.ShapeDtypeStruct((cols, total), bfloat),
        in_specs=[vm] * (len(lefts) + len(flat) + len(extra)),
        out_specs=vm,
        compiler_params=pltpu.CompilerParams(vmem_limit_bytes=48 << 20),
        cost_estimate=pl.CostEstimate(flops=0, bytes_accessed=0, transcendentals=0),
    )(*lefts, *flat, *extra)


def rows_kernel(value, out):
    lines, rows = value.shape[0], value.shape[2]
    for i in range(lines):
        out[i * rows : (i + 1) * rows] = value[i, 0].astype(single)


def in_rows(chips, value):
    lines, parts = chips.dims[0], chips.plane
    rows = value.shape[0] // (lines * parts)
    value = value.reshape(lines, parts, rows, -1)
    if rows % 16:
        return value.swapaxes(0, 1).reshape(lines * parts * rows, -1).astype(single)
    width = value.shape[3]
    return pl.pallas_call(
        rows_kernel,
        grid=(parts,),
        out_shape=jax.ShapeDtypeStruct((lines * parts * rows, width), single),
        in_specs=[pl.BlockSpec((lines, 1, rows, width), lambda p: (0, p, 0, 0))],
        out_specs=pl.BlockSpec((lines * rows, width), lambda p: (p, 0)),
        compiler_params=pltpu.CompilerParams(vmem_limit_bytes=48 << 20),
        cost_estimate=pl.CostEstimate(flops=0, bytes_accessed=0, transcendentals=0),
    )(value)


def widths_of(total):
    if total % 128:
        return [total]
    out = []
    while total > 0:
        out.append(min(384, total))
        total -= out[-1]
    return out


def tie(value, *others):
    hbm = pl.BlockSpec(memory_space=pl.ANY)
    return pl.pallas_call(
        lambda *refs: None,
        out_shape=jax.ShapeDtypeStruct(value.shape, value.dtype),
        in_specs=[hbm] * (1 + len(others)),
        out_specs=hbm,
        input_output_aliases={0: 0},
    )(value, *others)


def grid_of(experts, shards):
    if shards == 2 and experts % 4 == 0:
        return (experts // 4, 2, 2)
    side = math.isqrt(experts)
    return (side, side) if side * side == experts else (experts,)


class Chips:
    def __init__(self, dims, names):
        self.dims = dims
        self.names = names
        self.size = int(np.prod(dims))
        self.plane = self.size // dims[0]
        self.places = [tuple(int(v) for v in np.unravel_index(i, dims)) for i in range(self.size)]
        self.offsets = [
            tuple(int(v) for v in np.unravel_index(i, dims[1:])) for i in range(self.plane)
        ]

    def index(self, place):
        return int(np.ravel_multi_index(place, self.dims))

    def own(self, axis):
        return lax.axis_index(self.names[axis])

    def me(self):
        return lax.axis_index(self.names)

    def pairs(self, axis_of, by):
        out = []
        for i, place in enumerate(self.places):
            axis = axis_of(place)
            to = list(place)
            to[axis] = (to[axis] + by) % self.dims[axis]
            out.append((i, self.index(to)))
        return out

    def along(self, value, axis, by):
        n = self.dims[axis]
        return lax.ppermute(value, self.names[axis], [(i, (i + by) % n) for i in range(n)])

    def offset_by(self, value, offset):
        out = []
        for i, place in enumerate(self.places):
            to = [place[0]] + [
                (p + o) % d for p, o, d in zip(place[1:], offset, self.dims[1:])
            ]
            out.append((i, self.index(to)))
        return lax.ppermute(value, self.names, out)

    def first(self, block):
        return [block] + [self.along(block, 0, j) for j in range(1, self.dims[0])]

    def axes(self, j):
        if len(self.dims) < 3:
            return (0, len(self.dims) - 1)
        return (1, 2) if j % 2 == 0 else (2, 1)

    def hop_one(self, block, j):
        axis, _ = self.axes(j)
        return self.hop_line(block, axis) if axis else [block]

    def hop_two(self, blocks, j):
        _, axis = self.axes(j)
        both = jnp.concatenate(blocks, axis=0) if len(blocks) > 1 else blocks[0]
        return self.hop_line(both, axis) if axis else [both]

    def places_of(self, j):
        one, two = self.axes(j)
        if not one:
            return list(range(self.plane))
        out = []
        for t in range(self.dims[two]):
            for h in range(self.dims[one]):
                out.append(self.offsets.index((h, t) if one == 1 else (t, h)))
        return out

    def hop_line(self, block, axis):
        return [block] + [self.along(block, axis, s) for s in range(1, self.dims[axis])]

    def straight(self, block):
        return [self.offset_by(block, o) if any(o) else block for o in self.offsets]

    def straight_back(self, blocks):
        return [
            self.offset_by(b, [-v for v in o]) if any(o) else b
            for b, o in zip(blocks, self.offsets)
        ]

    def pack_of(self, j, p):
        if len(self.dims) != 3:
            return (p, j)
        half = self.dims[0] // 2
        y, x = self.offsets[p]
        part, rest = (x, y) if j < half else (y, x)
        return (j // half * 2 + part, rest * half + j % half)

    def packs_one(self, packs):
        if len(self.dims) != 3:
            return [self.straight_back(packs)]
        return [
            [packs[0], self.along(packs[1], 2, -1)],
            [packs[2], self.along(packs[3], 1, -1)],
        ]

    def packs_two(self, totals):
        if len(self.dims) != 3:
            return [[v] for v in totals]
        out = []
        for v, axis in zip(totals, (1, 2)):
            rows = v.shape[0] // 2
            out.append([v[:rows], self.along(v[rows:], axis, -1)])
        return out

    def sources(self, at_once):
        table = []
        for place in self.places:
            row = []
            for j in range(self.dims[0]):
                for p in range(self.plane) if j in at_once else self.places_of(j):
                    offset = (j, *self.offsets[p])
                    row.append(self.index([(q - o) % d for q, o, d in zip(place, offset, self.dims)]))
            table.append(row)
        return jnp.asarray(np.array(table, np.int32))[self.me()]

    def back_first(self, total, j):
        return self.along(total.astype(bfloat), 0, -j) if j else total

    def own_part(self):
        part = 0
        for axis in range(1, len(self.dims)):
            part = part * self.dims[axis] + self.own(axis)
        return part

    def swap_columns(self, *values):
        out = []
        for offset in self.offsets:
            part = 0
            for axis, by in enumerate(offset):
                n = self.dims[axis + 1]
                part = part * n + (self.own(axis + 1) + by) % n
            pieces = []
            for v in values:
                size = v.shape[1] // self.plane
                pieces.append(lax.dynamic_slice_in_dim(v, part * size, size, 1))
            piece = jnp.concatenate(pieces, axis=1)
            out.append(self.offset_by(piece, offset) if any(offset) else piece)
        return out

    def orders(self):
        return ((2, 1), (1, 2)) if len(self.dims) == 3 else ((1,),)

    def halves(self, value):
        if len(self.dims) != 3:
            return [value]
        cut = value.shape[1] // 256 * 128
        return [value[:, :cut], value[:, cut:]]

    def stack_one(self, value):
        return [self.hop_line(v, o[0]) for v, o in zip(self.halves(value), self.orders())]

    def stack_two(self, lines, mark):
        out = []
        for line, order in zip(lines, self.orders()):
            both = jnp.concatenate(hold(line, mark), axis=0)
            out.append(self.hop_line(both, order[1]) if len(order) > 1 else [both])
        return out

    def stack_done(self, lines, mark):
        out = []
        for line, order in zip(lines, self.orders()):
            line = hold(line, mark)
            if order == (1, 2):
                n = self.dims[1]
                rows = line[0].shape[0] // n
                line = [v[s * rows : (s + 1) * rows] for s in range(n) for v in line]
            out.append(jnp.concatenate(line, axis=0))
        return out

    def send_rows(self, value):
        size = value.shape[0] // self.plane
        out = []
        for offset in self.offsets:
            part = 0
            for axis, by in enumerate(offset):
                n = self.dims[axis + 1]
                part = part * n + (self.own(axis + 1) + by) % n
            piece = lax.dynamic_slice_in_dim(value, part * size, size, 0)
            out.append(self.offset_by(piece, offset) if any(offset) else piece)
        return out

    def line_send(self, value):
        n = self.dims[0]
        rows = value.shape[0] // n
        own = self.own(0)
        out = [lax.dynamic_slice_in_dim(value, own * rows, rows, 0)]
        for j in range(1, n):
            piece = lax.dynamic_slice_in_dim(value, ((own + j) % n) * rows, rows, 0)
            out.append(self.along(piece, 0, j))
        return out

    def gather_one(self, halves):
        return [self.hop_line(v, o[0]) for v, o in zip(halves, self.orders())]

    def gather_two(self, lines, mark):
        out = []
        for line, order in zip(lines, self.orders()):
            line = hold(line, mark)
            own = self.own(order[0])
            if len(order) == 1:
                out.append([in_order(line, own, 0)])
            else:
                both = in_order(line, own, 0)
                out.append(self.hop_line(both, order[1]))
        return out

    def gather_done(self, lines, mark):
        out = []
        for line, order in zip(lines, self.orders()):
            line = hold(line, mark)
            if len(order) == 1:
                out.append(line[0])
            elif order == (1, 2):
                n = self.dims[1]
                rows = line[0].shape[0] // n
                cut = [[v[i * rows : (i + 1) * rows] for v in line] for i in range(n)]
                out += [jnp.concatenate([in_order(v, self.own(2), 0) for v in cut], axis=0)]
            else:
                out.append(in_order(line, self.own(order[1]), 0))
        return jnp.concatenate(out, axis=1)


def hold(values, *others):
    return [values[0]] + [tie(v, *others) for v in values[1:]]


def visit(mark, lines, singles=()):
    lines = [[v[0]] + [tie(x, mark) for x in v[1:]] for v in lines]
    singles = [tie(v, mark) for v in singles]
    mark = tie(lines[0][0], mark, *[x for v in lines for x in v[1:]], *singles)
    lines = [[mark] + lines[0][1:]] + [[tie(v[0], mark)] + v[1:] for v in lines[1:]]
    return mark, lines, [tie(v, mark) for v in singles]


def add_up(values):
    return sum([v.astype(single) for v in values[1:]], values[0].astype(single)).astype(bfloat)


def split(value, widths):
    out, start = [], 0
    for width in widths:
        out.append(value[:, start : start + width])
        start += width
    return out


def in_order(pieces, own, axis):
    n = len(pieces)
    if n == 1:
        return pieces[0]
    if n == 2:
        return jnp.where(
            own == 0,
            jnp.concatenate(pieces, axis=axis),
            jnp.concatenate([pieces[1], pieces[0]], axis=axis),
        )
    turned = pieces[::-1]
    line = jnp.concatenate(turned + turned[:-1], axis=axis)
    extent = pieces[0].shape[axis]
    return lax.dynamic_slice_in_dim(line, (n - 1 - own) * extent, n * extent, axis)


class Cores:
    def __init__(self, count):
        self.count = count
        self.own = lax.axis_index("shard")

    def along(self, value, by):
        n = self.count
        return lax.ppermute(value, "shard", [(i, (i + by) % n) for i in range(n)])

    def spread(self, value):
        return [value] + [self.along(value, j) for j in range(1, self.count)]

    def whole(self, value, axis):
        return in_order(self.spread(value), self.own, axis)

    def chunk(self, value, j, axis):
        size = value.shape[axis] // self.count
        place = (self.own + j + self.count) % self.count
        return lax.dynamic_slice_in_dim(value, place * size, size, axis)

    def rows_times(self, left, pieces):
        out = None
        for j, piece in enumerate(pieces):
            term = dot(self.chunk(left, -j, 1), piece)
            out = term if out is None else out + term
        return out

    def times_rows_t(self, left, pieces):
        return in_order([dot_t(left, piece) for piece in pieces], self.own, 1)

    def swap_columns(self, *values):
        out = []
        for j in range(self.count):
            piece = jnp.concatenate([self.chunk(v, j, 1) for v in values], axis=1)
            out.append(self.along(piece, j) if j else piece)
        return split(jnp.concatenate(out, axis=0), [v.shape[1] // self.count for v in values])

    def stack(self, value):
        return jnp.concatenate(self.spread(value), axis=0)

    def give_back(self, value):
        rows = value.shape[0] // self.count
        total = value[:rows]
        for j in range(1, self.count):
            total = total + self.along(value[j * rows : (j + 1) * rows], -j)
        return total

    def scatter(self, value, axis):
        total = self.chunk(value, 0, axis).astype(single)
        for j in range(1, self.count):
            total = total + self.along(self.chunk(value, j, axis).astype(bfloat), j).astype(single)
        return total


def per_device(
    chips,
    shards,
    tokens,
    segment_ids,
    routes,
    cotangent,
    gain_attn,
    gain_query,
    gain_latent,
    gain_ffn,
    w_qa,
    w_qb,
    w_kva,
    w_kvb,
    w_out,
    w_router,
    shared_gate,
    shared_up,
    shared_down,
    expert_gate,
    expert_up,
    expert_down,
):
    cores = Cores(shards)
    me = chips.me()
    shard_pos = cores.own
    tok_rows = tokens.shape[0]
    model = tokens.shape[1]
    group_rows = tok_rows * shards
    score_scale = 1.0 / (DN + DR) ** 0.5
    query_rank = w_qa.shape[1]

    gains = jnp.concatenate([gain_attn, gain_query, gain_latent, gain_ffn])
    gain_pieces = cores.spread(gains)
    sizes = [v.shape[0] for v in (gain_attn, gain_query, gain_latent, gain_ffn)]
    full_gains = []
    start = 0
    for size in sizes:
        full_gains.append(
            in_order([g[start : start + size] for g in gain_pieces], shard_pos, 0).astype(single)
        )
        start += size
    gain_attn_f, gain_query_f, gain_latent_f, gain_ffn_f = full_gains
    qa_pieces = cores.spread(w_qa)
    kva_pieces = cores.spread(w_kva)
    qb_pieces = cores.spread(w_qb)
    kvb_pieces = cores.spread(w_kvb)
    out_pieces = cores.spread(w_out)
    router_full = cores.whole(w_router, 0)
    expert_weights = [
        cores.spread(expert_gate[0].T),
        cores.spread(expert_up[0].T),
        cores.spread(expert_down[0]),
    ]
    turns = chips.dims[0]
    order = [0] + list(range(1, turns, 2)) + list(range(2, turns, 2))
    all_cots = lax.all_gather(cotangent, chips.names, axis=0, tiled=True)

    resid = tokens.astype(single)
    attn_scale = row_scale(resid)
    attn_normed = resid * attn_scale
    attn_in = (attn_normed * gain_attn_f).astype(bfloat)
    query_lat = cores.rows_times(attn_in, qa_pieces)
    query_scale = row_scale(query_lat)
    query_normed = query_lat * query_scale
    query_in = (query_normed * gain_query_f).astype(bfloat)
    query_all = cores.rows_times(query_in, qb_pieces)
    group_pos = seq_positions(segment_ids)
    own_start = shard_pos * tok_rows
    own_pos = lax.dynamic_slice_in_dim(group_pos, own_start, tok_rows, 0)
    own_seg = lax.dynamic_slice_in_dim(segment_ids, own_start, tok_rows, 0)
    cosine, sine = rope_tables(own_pos, DR // 2)
    latent_raw = cores.rows_times(attn_in, kva_pieces)
    latent_part = latent_raw[:, :KR]
    latent_scale = row_scale(latent_part)
    latent_normed = latent_part * latent_scale
    latent = (latent_normed * gain_latent_f).astype(bfloat)
    key_rope = rotate(latent_raw[:, KR:], cosine, sine).astype(bfloat)
    keys = cores.whole(jnp.concatenate([latent, key_rope], axis=1), 0)
    keys_latent, keys_rope = keys[:, :KR], keys[:, KR:]
    keys_turned = jnp.concatenate(
        [cores.chunk(keys_latent, -j, 1) for j in range(shards)], axis=1
    )
    group_index = jnp.arange(group_rows, dtype=jnp.int32)
    own_index = own_start + jnp.arange(tok_rows, dtype=jnp.int32)
    visible = (own_seg[:, None] == segment_ids[None, :]) & (
        group_index[None, :] <= own_index[:, None]
    )

    attn_heads, *saved = run_heads(
        query_all,
        kvb_pieces,
        keys_turned,
        keys_rope,
        visible.astype(single),
        cosine,
        sine,
        H,
        score_scale,
    )
    mid = resid + cores.rows_times(attn_heads, out_pieces)
    ffn_scale = row_scale(mid)
    ffn_normed = mid * ffn_scale
    ffn_in = (ffn_normed * gain_ffn_f).astype(bfloat)

    experts_all = router_full.shape[1]
    lanes = -(-4 * experts_all // 128) * 128
    logits = dot(ffn_in, router_full)
    chosen = jnp.sum(
        (routes[:, :, None] == jnp.arange(experts_all, dtype=jnp.int32)[None, None, :]).astype(
            single
        ),
        axis=1,
    )
    sig = jax.nn.sigmoid(logits)
    denom = jnp.sum(chosen * sig, axis=-1, keepdims=True)
    routing_weights = route_scale * chosen * sig / denom
    capacity = min(tok_rows, 4 * tok_rows * TOP // (3 * experts_all))
    earlier = (jnp.arange(tok_rows)[:, None] > jnp.arange(tok_rows)[None, :]).astype(bfloat)
    slot = dot(earlier, chosen.astype(bfloat))
    code = jnp.where(chosen > 0, slot, -1.0)
    weight_high = routing_weights.astype(bfloat)
    weight_rest = (routing_weights - weight_high.astype(single)).astype(bfloat)
    marks = jnp.concatenate(
        [
            code.astype(bfloat),
            weight_high,
            weight_rest,
            jnp.zeros((tok_rows, lanes - 3 * experts_all), bfloat),
        ],
        axis=1,
    )
    payload = jnp.concatenate([ffn_in, marks], axis=1)
    first = chips.first(payload)
    one, two = [None] * turns, [None] * turns
    two[0] = chips.straight(payload)

    stack_ffn = cores.stack(ffn_in)
    stack_cot = cores.stack(cotangent)

    def feed_forward(rows, grads, gate, up, down):
        pre_gate = dot(rows, gate)
        pre_up = dot(rows, up)
        hidden = (jax.nn.silu(pre_gate) * pre_up).astype(bfloat)
        grad_gate, grad_up = silu_grads(dot_t(grads, down), pre_gate, pre_up)
        return hidden, grad_gate, grad_up

    sh_hidden, sh_gate, sh_up = feed_forward(
        stack_ffn, stack_cot, shared_gate, shared_up, shared_down
    )
    sh_back = dot_t(sh_gate, shared_gate) + dot_t(sh_up, shared_up)
    shared_out = cores.give_back(dot(sh_hidden, shared_down))
    shared_back = cores.give_back(sh_back)

    at_once = order[:2]
    who = jnp.concatenate([me.astype(jnp.int32).reshape(1), chips.sources(at_once)])
    kept, kept_back = None, None
    sent, grads_of = [], []

    def parts_of(i):
        if i == 2:
            return kept[5 : 5 + shards], kept_back[0]
        return kept_back[2 + i * shards : 2 + (i + 1) * shards], kept[0]

    def others_part(i, waits):
        left, right = parts_of(i)
        out = [t_dot(tie(v, *waits), right).astype(bfloat) for v in left[1:]]
        sent.append([cores.along(v, -j - 1) for j, v in enumerate(out)])
        return out[-1]

    def own_part(i, waits):
        left, right = parts_of(i)
        got = [tie(v, *waits).astype(single) for v in sent[i]]
        grads_of.append(sum(got, t_dot(tie(left[0], *waits), right)))
        return grads_of[-1]

    fillers = [
        lambda waits: others_part(1, [others_part(0, waits)]),
        lambda waits: others_part(2, waits),
        lambda waits: own_part(1, [own_part(0, waits)]),
    ]
    mark = sh_back
    backs = [None] * turns

    def places_of(j):
        return list(range(chips.plane)) if j in at_once else chips.places_of(j)

    def forward_step(step):
        nonlocal kept, mark
        waits = [mark]
        if step + 1 < turns:
            k = order[step + 1]
            if k in at_once:
                first[k] = tie(first[k], mark)
                two[k] = chips.straight(first[k])
                waits.append(first[k])
            else:
                one[k] = hold(one[k], mark)
                two[k] = chips.hop_two(one[k], k)
                waits.append(one[k][0])
        if step + 2 < turns:
            k = order[step + 2]
            first[k] = tie(first[k], mark)
            one[k] = chips.hop_one(first[k], k)
            waits.append(first[k])
        j = order[step]
        mark, kept = run_experts(
            who,
            two[j],
            expert_weights,
            capacity,
            experts_all,
            j,
            turns,
            [chips.pack_of(j, p) for p in places_of(j)],
            kept,
            waits,
        )

    def backward_step(step):
        nonlocal kept_back, mark
        waits = [mark]
        if 2 <= step:
            k = step - 2
            total = add_up(hold(backs[k], mark))
            backs[k] = chips.back_first(total, k)
            waits.append(total)
        if step >= turns:
            mark = fillers[step - turns](waits)
            return
        j = step
        back_blocks, kept_back = run_experts_back(
            who,
            two[j],
            all_cots,
            expert_weights,
            kept[2:5],
            capacity,
            experts_all,
            j,
            turns,
            True,
            kept_back,
            waits,
        )
        places = places_of(j)
        back_blocks = [back_blocks[places.index(p)] for p in range(chips.plane)]
        backs[j] = chips.straight_back(back_blocks)
        mark = back_blocks[0]

    ahead = min(3, turns)
    for step in range(ahead):
        forward_step(step)
    for step in range(turns + 2):
        backward_step(step)
        if step + ahead < turns:
            forward_step(step + ahead)
    out_packs = kept[5 + shards :]
    routed_back = backs[0].astype(single)
    for j in order[1:]:
        routed_back = routed_back + tie(backs[j], mark).astype(single)
    chip_ffn, chip_cot = kept[1], kept_back[1]

    grad_out = cotangent.astype(single)
    grad_weights = (
        routed_back[:, model : model + experts_all]
        + routed_back[:, model + experts_all : model + 2 * experts_all]
    )
    grad_sig = chosen * (
        route_scale * grad_weights / denom
        - jnp.sum(grad_weights * routing_weights, axis=-1, keepdims=True) / denom
    )
    grad_logits = grad_sig * sig * (1.0 - sig)
    grad_router = jnp.einsum("te,td->ed", grad_logits, ffn_in.astype(single), precision=highest)
    grad_ffn_in = (
        routed_back[:, :model]
        + shared_back
        + jnp.einsum("te,de->td", grad_logits, router_full.astype(single), precision=highest)
    )
    grad_mid, grad_gffn = norm_back(grad_ffn_in, ffn_normed, ffn_scale, gain_ffn_f)
    grad_mid = grad_mid + grad_out

    grad_attn_out = grad_mid.astype(bfloat)
    heads_line = chips.stack_one(grad_attn_out)
    lefts = cores.swap_columns(attn_in, query_in, tie(attn_heads, sh_back))
    lefts = chips.swap_columns(*[tie(v, mark) for v in lefts])
    sent[:] = [[tie(v, grad_attn_out) for v in line] for line in sent]
    grad_attn_out = tie(grad_attn_out, *[v for line in sent for v in line])
    grad_heads = cores.times_rows_t(grad_attn_out, out_pieces).astype(bfloat)
    heads_line = chips.stack_two(heads_line, grad_heads)
    grad_query, kvb_parts, key_terms, rope_terms = run_heads_back(
        grad_heads,
        kvb_pieces,
        keys_turned,
        keys_rope,
        cosine,
        sine,
        saved,
        H,
        score_scale,
        [v[0] for v in heads_line],
    )
    heads_line = [hold(v, grad_query) for v in heads_line]
    lefts = hold(lefts, grad_query)
    there = [v for line in [*heads_line, lefts] for v in line[1:]]
    grad_query = tie(grad_query, *there)
    heads_all = [cores.spread(v) for v in chips.stack_done(heads_line, grad_query)]
    query_line = chips.stack_one(grad_query)
    kvb_terms = add_up(
        [kvb_parts[0]] + [cores.along(v, -j - 1) for j, v in enumerate(kvb_parts[1:])]
    )
    kvb_line = chips.send_rows(kvb_terms)
    size = KR // shards
    key_terms = in_order(
        [key_terms[:, j * size : (j + 1) * size] for j in range(shards)], shard_pos, 1
    )
    grad_keys = cores.scatter(jnp.concatenate([key_terms, rope_terms], axis=1), 0)
    grad_latent, grad_krope = grad_keys[:, :KR], grad_keys[:, KR:]
    grad_query_in = cores.times_rows_t(grad_query, qb_pieces)
    grad_qlat, grad_gquery = norm_back(grad_query_in, query_normed, query_scale, gain_query_f)
    grad_kvpart, grad_glatent = norm_back(grad_latent, latent_normed, latent_scale, gain_latent_f)
    grad_kvrope = rotate_back(grad_krope, cosine, sine)
    grad_low = jnp.concatenate([grad_qlat, grad_kvpart, grad_kvrope], axis=-1).astype(bfloat)
    shared_weights = (shared_gate, shared_up, shared_down)
    xs, cs = cores.spread(tie(chip_ffn, routed_back)), cores.spread(tie(chip_cot, routed_back))
    widths = widths_of(shared_gate.shape[1]) if shards == 2 else []
    shared_grads = None
    start = 0

    def shared_step(waits):
        nonlocal shared_grads, start
        if not widths:
            return waits[0]
        width = widths.pop(0)
        shared_grads = run_shared(xs, cs, shared_weights, start, width, shared_grads, waits)
        start += width
        return shared_grads[0]

    low_wide = jnp.pad(grad_low, ((0, 0), (0, -grad_low.shape[1] % 128)))
    low_line = chips.straight(low_wide)
    mark = fillers[2]([grad_low, kvb_line[0], *[v[0] for v in query_line]])
    query_line = chips.stack_two(query_line, mark)
    sizes = [v.shape[1] // (shards * chips.plane) for v in (attn_in, query_in, attn_heads)]
    kvb_line = hold(kvb_line, mark)
    part = plane_dot(
        lefts, sizes[0] + sizes[1], sizes[2], heads_all, [v[0].shape[1] for v in heads_all]
    )
    part_sums = lax.psum_scatter(part, chips.names[0], scatter_dimension=0, tiled=True)
    kvb_part = add_up(kvb_line)
    mark = shared_step([part, low_line[0], kvb_part] + [v[0] for v in query_line])
    mark, lines, (part_sums,) = visit(
        mark, [low_line, *query_line], [part_sums]
    )
    low_line, *query_line = lines
    part_all = lax.all_gather(part_sums, chips.names, axis=0, tiled=True)
    mark = tie(grad_low, mark)
    grad_low = mark
    grad_attn_in = in_order(
        [
            dot_t(grad_low[:, :query_rank], qa) + dot_t(grad_low[:, query_rank:], kva)
            for qa, kva in zip(qa_pieces, kva_pieces)
        ],
        shard_pos,
        1,
    )
    grad_resid, grad_gattn = norm_back(grad_attn_in, attn_normed, attn_scale, gain_attn_f)
    grad_tokens = grad_mid + grad_resid
    mixed = jnp.concatenate(
        [grad_gquery.reshape(shards, -1), grad_glatent.reshape(shards, -1)], axis=1
    ).reshape(-1)
    small = jnp.concatenate(
        [grad_gattn[None], grad_gffn[None], mixed[None], grad_router], axis=0
    )
    small_line = chips.send_rows(cores.scatter(small, 1).T.astype(bfloat))
    query_all = [cores.spread(v) for v in chips.stack_done(query_line, mark)]
    query_part = plane_dot(
        lefts, sizes[0], sizes[1], query_all, [v[0].shape[1] for v in query_all]
    )
    query_sums = lax.psum_scatter(query_part, chips.names[0], scatter_dimension=0, tiled=True)
    low_all = cores.spread(jnp.concatenate(low_line, axis=0))
    small_part = add_up(hold(small_line, query_part))
    low_cols = grad_low.shape[1]
    spare = low_wide.shape[1] - low_cols - small_part.shape[1]
    fold = sizes[2] // kvb_part.shape[0]
    kvb_cols = kvb_part.shape[1] // fold
    small_wide = jnp.pad(small_part, ((0, 0), (0, spare)))
    low_part = plane_dot(
        lefts, 0, sizes[0], [low_all], [low_cols], fold, (kvb_part, small_wide)
    )
    low_line = chips.line_send(low_part)
    out_lines = chips.packs_one([tie(v, small_part) for v in out_packs])
    mark = shared_step([query_part, low_line[0]])
    mark, lines, (query_sums,) = visit(mark, [low_line, *out_lines], [query_sums])
    low_line, *out_lines = lines
    query_all = lax.all_gather(query_sums, chips.names, axis=0, tiled=True)
    low_line = chips.hop_line(add_up(low_line), 0)
    out_lines = chips.packs_two([add_up(v) for v in out_lines])
    waits = [v[0] for v in out_lines]
    mark = shared_step(waits + [low_line[0]])
    mark, lines, (part_all,) = visit(mark, [low_line, *out_lines], [part_all])
    low_line, *out_lines = lines
    low_all = in_order(low_line, chips.own(0), 0)
    low_line = chips.gather_one(chips.halves(low_all))
    totals = jnp.concatenate([add_up(v) for v in out_lines], axis=0)
    back_sums = [
        chips.back_first(totals[j * tok_rows : (j + 1) * tok_rows], j) for j in range(turns)
    ]
    mark = shared_step([v[0] for v in low_line] + back_sums[:1])
    mark, low_line, back_sums[1:] = visit(mark, low_line, back_sums[1:])
    low_line = chips.gather_two(low_line, mark)
    routed_out = back_sums[0].astype(single)
    for j in range(1, turns):
        routed_out = routed_out + tie(back_sums[j], mark).astype(single)
    result = mid + shared_out + routed_out
    mark = own_part(2, [mark])
    grad_egate = grads_of[0].T[None]
    grad_eup = grads_of[1].T[None]
    grad_edown = grads_of[2][None]
    grad_wout = in_rows(chips, tie(part_all, result))
    grad_wqb = in_rows(chips, tie(query_all, grad_wout))
    low_cuts = [kvb_cols, query_rank, low_cols - query_rank, small_part.shape[1] + spare]
    if len(chips.dims) == 3:
        low_line = [hold(v, grad_wqb, mark) for v in low_line]
        grad_wkvb, grad_wqa, grad_wkva, small = assemble(chips, low_line, low_cuts, fold, (2,))
        grad_wkva = grad_wkva.T
    else:
        low_all = chips.gather_done(low_line, mark).astype(single)
        kvb_all, grad_wqa, grad_wkva, small = split(low_all, low_cuts)
        kvb_all = kvb_all.reshape(chips.plane, fold, -1, kvb_cols)
        grad_wkvb = kvb_all.swapaxes(1, 2).reshape(-1, fold * kvb_cols)

    if shards == 2:
        grad_sgate, grad_sup, grad_sdown = shared_grads
    else:
        grad_sgate = grad_sup = grad_sdown = 0.0
        all_ffn, all_cot = chip_ffn, chip_cot
        for turn in range(shards):
            if turn > 0:
                tied = lax.optimization_barrier(
                    (all_ffn, all_cot, grad_sgate, grad_sup, grad_sdown)
                )
                grad_sgate, grad_sup, grad_sdown = tied[2:]
                all_ffn, all_cot = cores.along(tied[0], 1), cores.along(tied[1], 1)
            all_hidden, all_gate, all_up = feed_forward(
                all_ffn, all_cot, shared_gate, shared_up, shared_down
            )
            grad_sgate = grad_sgate + t_dot(all_ffn, all_gate)
            grad_sup = grad_sup + t_dot(all_ffn, all_up)
            grad_sdown = grad_sdown + t_dot(all_hidden, all_cot)
    query_part = gain_query.shape[0]
    return (
        result,
        grad_tokens,
        small[:, 0],
        small[:query_part, 2],
        small[query_part:, 2],
        small[:, 1],
        grad_wqa,
        grad_wqb,
        grad_wkva,
        grad_wkvb,
        grad_wout,
        small[:, 3 : 3 + experts_all],
        grad_sgate,
        grad_sup,
        grad_sdown,
        grad_egate,
        grad_eup,
        grad_edown,
    )


def solution(mesh):
    shards = mesh.shape["shard"]
    dims = grid_of(mesh.shape["expert"], shards)
    names = tuple(f"line{i}" for i in range(len(dims)))
    grid = jax.sharding.Mesh(mesh.devices.reshape(dims + (shards,)), names + ("shard",))
    chips = Chips(dims, names)
    both = names + ("shard",)
    in_specs = (
        P(both, None),
        P(names),
        P(both, None),
        P(both, None),
        P("shard"),
        P("shard"),
        P("shard"),
        P("shard"),
        P("shard", None),
        P("shard", None),
        P("shard", None),
        P("shard", None),
        P("shard", None),
        P("shard", None),
        P(None, "shard"),
        P(None, "shard"),
        P("shard", None),
        P(names, None, "shard"),
        P(names, None, "shard"),
        P(names, "shard", None),
    )
    out_specs = (
        P(both, None),
        P(both, None),
        P("shard"),
        P("shard"),
        P("shard"),
        P("shard"),
        P("shard", None),
        P("shard", None),
        P("shard", None),
        P("shard", None),
        P("shard", None),
        P("shard", None),
        P(None, "shard"),
        P(None, "shard"),
        P("shard", None),
        P(names, None, "shard"),
        P(names, None, "shard"),
        P(names, "shard", None),
    )

    def body(*args):
        return per_device(chips, shards, *args)

    return jax.shard_map(
        body, mesh=grid, in_specs=in_specs, out_specs=out_specs, check_vma=False
    )
```

```python
import functools
import math

import jax
import jax.numpy as jnp
import numpy as np
from jax import lax
from jax.experimental import pallas as pl
from jax.experimental.pallas import tpu as pltpu
from jax.sharding import PartitionSpec as P

H = 16
DN = 128
DR = 64
DV = 128
KR = 512
TOP = 6


norm_eps = 1e-06
rope_base = 50000.0
route_scale = 2.446
masked_score = -1e30
highest = lax.Precision.HIGHEST
bfloat = jnp.bfloat16
single = jnp.float32


def row_scale(values):
    return lax.rsqrt(jnp.mean(values * values, axis=-1, keepdims=True) + norm_eps)


def norm_back(grad_out, normed_rows, scale_rows, gain):
    grad_normed = grad_out * gain
    grad_input = scale_rows * (
        grad_normed - normed_rows * jnp.mean(grad_normed * normed_rows, axis=-1, keepdims=True)
    )
    return (grad_input, jnp.sum(grad_out * normed_rows, axis=0))


def seq_positions(segments):
    token_count = segments.shape[0]
    index = jnp.arange(token_count, dtype=jnp.int32)
    change = jnp.concatenate([jnp.ones((1,), bool), segments[1:] != segments[:-1]])
    starts = lax.cummax(jnp.where(change, index, 0), axis=0)
    return index - starts


def rope_tables(positions, half):
    freq = rope_base ** (-jnp.arange(half, dtype=jnp.float32) / half)
    angles = positions.astype(jnp.float32)[:, None] * freq[None, :]
    return (jnp.cos(angles), jnp.sin(angles))


def rotate(values, cosine, sine):
    half = values.shape[-1] // 2
    first = values[..., :half]
    second = values[..., half:]
    return jnp.concatenate(
        [first * cosine - second * sine, second * cosine + first * sine], axis=-1
    )


def rotate_back(grads, cosine, sine):
    half = grads.shape[-1] // 2
    first = grads[..., :half]
    second = grads[..., half:]
    return jnp.concatenate(
        [first * cosine + second * sine, second * cosine - first * sine], axis=-1
    )


def silu_grads(grad_hidden, pre_gate, pre_up):
    sigma = jax.nn.sigmoid(pre_gate)
    grad_gate = grad_hidden * pre_up * sigma * (1.0 + pre_gate * (1.0 - sigma))
    grad_up = grad_hidden * pre_gate * sigma
    return (grad_gate.astype(bfloat), grad_up.astype(bfloat))


def dot(left, right):
    return jnp.dot(left, right, preferred_element_type=single)


def dot_t(left, right):
    return lax.dot_general(left, right, (((1,), (1,)), ((), ())), preferred_element_type=single)


def t_dot(left, right):
    return lax.dot_general(left, right, (((0,), (0,)), ((), ())), preferred_element_type=single)


def expert_marks(marks, me, experts, capacity):
    marks = marks.astype(single)
    lane = lax.broadcasted_iota(jnp.int32, marks.shape, 1)
    place = lax.broadcasted_iota(jnp.int32, (marks.shape[0], capacity), 1).astype(single)
    code = jnp.sum(jnp.where(lane == me, marks, 0.0), axis=1, keepdims=True)
    weight = (lane == me + experts) | (lane == me + 2 * experts)
    weight = jnp.sum(jnp.where(weight, marks, 0.0), axis=1, keepdims=True)
    return (code == place).astype(single).astype(bfloat), weight, lane


def views(arrays, tok):
    return [(v, at) for v in arrays for at in range(0, v.shape[0], tok)]


def expert_kernel(arrays, tok, pieces, capacity, experts, group, places, first, waits, *refs):
    refs = list(refs)
    me_ref = refs.pop(0)
    count = len(places)
    blocks = views([refs.pop(0) for _ in range(arrays)], tok)
    weights = [[refs.pop(0) for _ in range(pieces)] for _ in range(3)]
    refs = refs[waits:]
    if not first:
        refs = refs[5 + pieces + count :]
    mark = refs.pop(0)
    rows_all, ffn_all, gate_all, up_all, out_all = (refs.pop(0) for _ in range(5))
    hidden_all = [refs.pop(0) for _ in range(pieces)]
    packs = [refs.pop(0) for _ in range(count)]
    full = [refs.pop(0) for _ in range(3)]
    rows, gate_scr, up_scr, out_scr = (refs.pop(0) for _ in range(4))
    hidden_scr = [refs.pop(0) for _ in range(pieces)]
    outs = refs.pop(0)
    sem_w, sem_o = refs
    model = rows.shape[1]
    width = weights[0][0].shape[0]
    loads = [[], [], []]
    for k in range(3):
        for j in range(pieces):
            c = pltpu.make_async_copy(
                weights[k][j], full[k].at[pl.ds(j * width, width)], sem_w.at[k, j]
            )
            c.start()
            loads[k].append(c)
    stores = []

    def store(src, dst):
        c = pltpu.make_async_copy(src, dst, sem_o.at[len(stores)])
        c.start()
        stores.append(c)

    me = me_ref[0]
    n = count * capacity
    mine = pl.ds(group * n, n)
    picks = []
    for i in range(count):
        ref, at = blocks[i]
        pick, weight, _ = expert_marks(
            ref[at : at + tok, model : model + 128], me, experts, capacity
        )
        picks.append((pick, weight))
        rows[pl.ds(i * capacity, capacity)] = t_dot(pick, ref[at : at + tok, :model]).astype(bfloat)
    store(rows, rows_all.at[mine])
    for i in range(count):
        store(
            blocks[i][0].at[pl.ds(blocks[i][1], tok), pl.ds(0, model)],
            ffn_all.at[pl.ds((group * count + i) * tok, tok)],
        )
    for c in loads[0]:
        c.wait()
    pre_gate = dot_t(rows[...], full[0][...])
    gate_scr[...] = pre_gate
    store(gate_scr, gate_all.at[mine])
    for c in loads[1]:
        c.wait()
    pre_up = dot_t(rows[...], full[1][...])
    up_scr[...] = pre_up
    store(up_scr, up_all.at[mine])
    hidden = (pre_gate * jax.nn.sigmoid(pre_gate) * pre_up).astype(bfloat)
    for j in range(pieces):
        hidden_scr[j][...] = hidden[:, j * width : (j + 1) * width]
        store(hidden_scr[j], hidden_all[j].at[mine])
    for c in loads[2]:
        c.wait()
    out = dot(hidden, full[2][...]).astype(bfloat)
    out_scr[...] = out
    store(out_scr, out_all.at[mine])
    for i, (pick, weight) in enumerate(picks):
        got = dot(pick, out[i * capacity : (i + 1) * capacity])
        outs[i] = (weight * got).astype(bfloat)
        pack, at = places[i]
        store(outs.at[i], packs[pack].at[pl.ds(at * tok, tok)])
    mark[...] = jnp.zeros_like(mark)
    for c in stores:
        c.wait()


def run_experts(me, blocks, weights, capacity, experts, group, groups, places, carried, others):
    count, pieces = len(places), len(weights[0])
    tok, model = sum(v.shape[0] for v in blocks) // count, weights[0][0].shape[1]
    width = weights[0][0].shape[0]
    n = count * capacity
    shape = jax.ShapeDtypeStruct
    kept = [
        shape((groups * n, model), bfloat),
        shape((groups * count * tok, model), bfloat),
        shape((groups * n, pieces * width), single),
        shape((groups * n, pieces * width), single),
        shape((groups * n, model), bfloat),
    ] + [shape((groups * n, width), bfloat)] * pieces
    kept += [shape((groups * tok, model), bfloat)] * count
    vm = pl.BlockSpec(memory_space=pltpu.VMEM)
    hbm = pl.BlockSpec(memory_space=pl.ANY)
    flat = [w for ws in weights for w in ws]
    operands = [me, *blocks, *flat, *others]
    in_specs = [pl.BlockSpec(memory_space=pltpu.SMEM)] + [vm] * len(blocks)
    in_specs += [hbm] * (len(flat) + len(others))
    alias = {}
    if carried is not None:
        alias = {len(operands) + i: 1 + i for i in range(len(kept))}
        operands += list(carried)
        in_specs += [hbm] * len(kept)
    out = pl.pallas_call(
        functools.partial(
            expert_kernel,
            len(blocks),
            tok,
            pieces,
            capacity,
            experts,
            group,
            places,
            carried is None,
            len(others),
        ),
        out_shape=[shape((16, 128), bfloat)] + kept,
        in_specs=in_specs,
        out_specs=[vm] + [hbm] * len(kept),
        input_output_aliases=alias,
        scratch_shapes=[pltpu.VMEM((pieces * width, model), bfloat)] * 3
        + [pltpu.VMEM((n, model), bfloat)]
        + [pltpu.VMEM((n, pieces * width), single)] * 2
        + [pltpu.VMEM((n, model), bfloat)]
        + [pltpu.VMEM((n, width), bfloat)] * pieces
        + [pltpu.VMEM((count, tok, model), bfloat)]
        + [pltpu.SemaphoreType.DMA((3, pieces)), pltpu.SemaphoreType.DMA((4 + 2 * count + pieces,))],
        compiler_params=pltpu.CompilerParams(vmem_limit_bytes=56 << 20),
        cost_estimate=pl.CostEstimate(flops=0, bytes_accessed=0, transcendentals=0),
    )(*operands)
    return out[0], out[1:]


def expert_back_kernel(
    arrays, results, tok, pieces, capacity, experts, group, first, waits, *refs
):
    refs = list(refs)
    me_ref = refs.pop(0)
    blocks = views([refs.pop(0) for _ in range(arrays)], tok)
    count = len(blocks)
    all_cots = refs.pop(0)
    weights = [[refs.pop(0) for _ in range(pieces)] for _ in range(3)]
    gate_all, up_all, out_all = (refs.pop(0) for _ in range(3))
    refs = refs[waits:]
    if not first:
        refs = refs[2 + 2 * pieces :]
    backs = views([refs.pop(0) for _ in range(results)], tok)
    grads_all, cot_all = refs.pop(0), refs.pop(0)
    acts = [[refs.pop(0) for _ in range(pieces)] for _ in range(2)]
    full = [refs.pop(0) for _ in range(3)]
    grads, gate_scr, up_scr, out_scr, cot_scr, mark_scr = (refs.pop(0) for _ in range(6))
    act_scr = [[refs.pop(0) for _ in range(pieces)] for _ in range(2)]
    sem_w, sem_i, sem_c, sem_o = refs
    model = grads.shape[1]
    width = weights[0][0].shape[0]
    n = count * capacity
    mine = pl.ds(group * n, n)

    def fetch(src, dst, sem):
        c = pltpu.make_async_copy(src, dst, sem)
        c.start()
        return c

    cots = []
    for i in range(count):
        source = pl.multiple_of(me_ref[1 + group * count + i] * tok, tok)
        cots.append(fetch(all_cots.at[pl.ds(source, tok)], cot_scr.at[i], sem_c.at[0, i]))
        marks = blocks[i][0].at[pl.ds(blocks[i][1], tok), pl.ds(model, 128)]
        cots.append(fetch(marks, mark_scr.at[i], sem_c.at[1, i]))
    loads = {}
    for k in (2, 0, 1):
        loads[k] = [
            fetch(weights[k][j], full[k].at[pl.ds(j * width, width)], sem_w.at[k, j])
            for j in range(pieces)
        ]
    saved = [
        fetch(gate_all.at[mine], gate_scr, sem_i.at[0]),
        fetch(up_all.at[mine], up_scr, sem_i.at[1]),
        fetch(out_all.at[mine], out_scr, sem_i.at[2]),
    ]
    stores = []

    def store(src, dst):
        stores.append(fetch(src, dst, sem_o.at[len(stores)]))

    me = me_ref[0]
    for c in cots:
        c.wait()
    picks = []
    for i in range(count):
        pick, weight, lane = expert_marks(mark_scr[i], me, experts, capacity)
        picks.append(pick)
        scaled = (weight * cot_scr[i].astype(single)).astype(bfloat)
        grads[pl.ds(i * capacity, capacity)] = t_dot(pick, scaled).astype(bfloat)
        store(cot_scr.at[i], cot_all.at[pl.ds((group * count + i) * tok, tok)])
    store(grads, grads_all.at[mine])
    for c in loads[2]:
        c.wait()
    grad_hidden = dot_t(grads[...], full[2][...])
    for c in saved:
        c.wait()
    pre_gate, pre_up = gate_scr[...], up_scr[...]
    sigma = jax.nn.sigmoid(pre_gate)
    grad_gate = grad_hidden * pre_up * sigma * (1.0 + pre_gate * (1.0 - sigma))
    grad_gate = grad_gate.astype(bfloat)
    grad_up = (grad_hidden * pre_gate * sigma).astype(bfloat)
    for k, v in enumerate((grad_gate, grad_up)):
        for j in range(pieces):
            act_scr[k][j][...] = v[:, j * width : (j + 1) * width]
            store(act_scr[k][j], acts[k][j].at[mine])
    for c in loads[0] + loads[1]:
        c.wait()
    back = (dot(grad_gate, full[0][...]) + dot(grad_up, full[1][...])).astype(bfloat)
    for i in range(count):
        here = slice(i * capacity, (i + 1) * capacity)
        got = dot(picks[i], out_scr[here])
        dots = jnp.sum(got * cot_scr[i].astype(single), axis=1, keepdims=True)
        ref, at = backs[i]
        ref[at : at + tok, :model] = dot(picks[i], back[here]).astype(bfloat)
        high = dots.astype(bfloat).astype(single)
        tail = jnp.where(lane == me, high, 0.0) + jnp.where(lane == me + experts, dots - high, 0.0)
        ref[at : at + tok, model : model + 128] = tail.astype(bfloat)
    for c in stores:
        c.wait()


def run_experts_back(
    me, blocks, all_cots, weights, saved, capacity, experts, group, groups, apart, carried, others
):
    pieces, model = len(weights[0]), weights[0][0].shape[1]
    count = saved[0].shape[0] // groups // capacity
    tok = sum(v.shape[0] for v in blocks) // count
    results = [tok] * count if apart else [v.shape[0] for v in blocks]
    width = weights[0][0].shape[0]
    n = count * capacity
    shape = jax.ShapeDtypeStruct
    kept = [shape((groups * n, model), bfloat), shape((groups * count * tok, model), bfloat)]
    kept += [shape((groups * n, width), bfloat)] * (2 * pieces)
    hbm = pl.BlockSpec(memory_space=pl.ANY)
    flat = [w for ws in weights for w in ws]
    operands = [me, *blocks, all_cots, *flat, *saved, *others]
    in_specs = [pl.BlockSpec(memory_space=pltpu.SMEM)] + [hbm] * (len(operands) - 1)
    alias = {}
    if carried is not None:
        alias = {len(operands) + i: len(results) + i for i in range(len(kept))}
        operands += list(carried)
        in_specs += [hbm] * len(kept)
    out = pl.pallas_call(
        functools.partial(
            expert_back_kernel,
            len(blocks),
            len(results),
            tok,
            pieces,
            capacity,
            experts,
            group,
            carried is None,
            len(others),
        ),
        out_shape=[shape((v, model + 128), bfloat) for v in results] + kept,
        in_specs=in_specs,
        out_specs=[pl.BlockSpec(memory_space=pltpu.VMEM)] * len(results) + [hbm] * len(kept),
        input_output_aliases=alias,
        scratch_shapes=[pltpu.VMEM((pieces * width, model), bfloat)] * 3
        + [pltpu.VMEM((n, model), bfloat)]
        + [pltpu.VMEM((n, pieces * width), single)] * 2
        + [
            pltpu.VMEM((n, model), bfloat),
            pltpu.VMEM((count, tok, model), bfloat),
            pltpu.VMEM((count, tok, 128), bfloat),
        ]
        + [pltpu.VMEM((n, width), bfloat)] * (2 * pieces)
        + [
            pltpu.SemaphoreType.DMA((3, pieces)),
            pltpu.SemaphoreType.DMA((3,)),
            pltpu.SemaphoreType.DMA((2, count)),
            pltpu.SemaphoreType.DMA((1 + count + 2 * pieces,)),
        ],
        compiler_params=pltpu.CompilerParams(vmem_limit_bytes=56 << 20),
        cost_estimate=pl.CostEstimate(flops=0, bytes_accessed=0, transcendentals=0),
    )(*operands)
    return out[: len(results)], out[len(results) :]


def shared_kernel(parts, tiles, start, width, first, waits, *refs):
    refs = list(refs)
    xs = [refs.pop(0) for _ in range(parts)]
    cs = [refs.pop(0) for _ in range(parts)]
    weights = [refs.pop(0) for _ in range(3)]
    refs = refs[waits:]
    if not first:
        refs = refs[3:]
    outs = [refs.pop(0) for _ in range(3)]
    wgu, wd = (refs.pop(0) for _ in range(2))
    accs = [refs.pop(0) for _ in range(2)]
    sem_w, sem_o = refs
    step = pl.program_id(0)
    cols = pl.ds(start, width)
    loads = [
        pltpu.make_async_copy(weights[0].at[:, cols], wgu.at[:, pl.ds(0, width)], sem_w.at[0]),
        pltpu.make_async_copy(weights[1].at[:, cols], wgu.at[:, pl.ds(width, width)], sem_w.at[1]),
        pltpu.make_async_copy(weights[2].at[cols], wd, sem_w.at[2]),
    ]

    @pl.when(step == 0)
    def _():
        for c in loads:
            c.start()
        for a in accs:
            a[...] = jnp.zeros_like(a)
        for c in loads:
            c.wait()

    def work(x_ref, c_ref):
        x, c = x_ref[...], c_ref[...]
        pre = dot(x, wgu[...])
        pre_gate, pre_up = pre[:, :width], pre[:, width:]
        grad_hidden = dot_t(c, wd[...])
        sigma = jax.nn.sigmoid(pre_gate)
        silu = pre_gate * sigma
        hidden = (silu * pre_up).astype(bfloat)
        grad_gate = (grad_hidden * pre_up * sigma * (1.0 + pre_gate * (1.0 - sigma))).astype(bfloat)
        grad_up = (grad_hidden * silu).astype(bfloat)
        accs[0][...] += t_dot(x, jnp.concatenate([grad_gate, grad_up], axis=1))
        accs[1][...] += t_dot(hidden, c)

    if parts == 1:
        work(xs[0], cs[0])
    else:
        per = tiles // parts
        for p in range(parts):
            pl.when(step // per == p)(functools.partial(work, xs[p], cs[p]))

    @pl.when(step == tiles - 1)
    def _():
        puts = [
            pltpu.make_async_copy(accs[0].at[:, pl.ds(0, width)], outs[0].at[:, cols], sem_o.at[0]),
            pltpu.make_async_copy(accs[0].at[:, pl.ds(width, width)], outs[1].at[:, cols], sem_o.at[1]),
            pltpu.make_async_copy(accs[1], outs[2].at[cols], sem_o.at[2]),
        ]
        for c in puts:
            c.start()
        for c in puts:
            c.wait()

def run_shared(xs, cs, weights, start, width, carried, others=(), tile=512):
    parts = len(xs)
    rows, model = xs[0].shape
    per = rows // tile
    tiles = per * parts
    shape = jax.ShapeDtypeStruct
    hbm = pl.BlockSpec(memory_space=pl.ANY)
    specs = [
        pl.BlockSpec((tile, model), lambda i, p=p: (jnp.clip(i - p * per, 0, per - 1), 0))
        for p in range(parts)
    ]
    outs = [shape(w.shape, single) for w in weights]
    operands = [*xs, *cs, *weights, *others]
    in_specs = specs + specs + [hbm] * (3 + len(others))
    alias = {}
    if carried is not None:
        alias = {len(operands) + i: i for i in range(3)}
        operands += list(carried)
        in_specs += [hbm] * 3
    return pl.pallas_call(
        functools.partial(shared_kernel, parts, tiles, start, width, carried is None, len(others)),
        grid=(tiles,),
        out_shape=outs,
        in_specs=in_specs,
        out_specs=[hbm] * 3,
        input_output_aliases=alias,
        scratch_shapes=[
            pltpu.VMEM((model, 2 * width), bfloat),
            pltpu.VMEM((width, model), bfloat),
            pltpu.VMEM((model, 2 * width), single),
            pltpu.VMEM((width, model), single),
            pltpu.SemaphoreType.DMA((3,)),
            pltpu.SemaphoreType.DMA((3,)),
        ],
        compiler_params=pltpu.CompilerParams(vmem_limit_bytes=60 << 20),
        cost_estimate=pl.CostEstimate(flops=0, bytes_accessed=0, transcendentals=0),
    )(*operands)


def turned(values, cosine, sine, way):
    half = values.shape[-1] // 2
    first, second = values[:, :half], values[:, half:]
    return jnp.concatenate(
        [first * cosine - way * second * sine, second * cosine + way * first * sine], axis=1
    )


def heads_kernel(pieces, score_scale, *refs):
    refs = list(refs)
    q_ref = refs.pop(0)
    kvbs = [refs.pop(0) for _ in range(pieces)]
    latent, rope, shown, cosine, sine = (refs.pop(0) for _ in range(5))
    heads_ref, nope_ref, qrope_ref, abs_ref, probs_ref, lat_ref = refs
    latents, ropes = latent[...], rope[...]
    visible = shown[...] > 0
    q = q_ref[...]
    rank = latents.shape[1]
    for h in range(2):
        nope = q[:, h * (DN + DR) : h * (DN + DR) + DN].astype(bfloat)
        tail = q[:, h * (DN + DR) + DN : (h + 1) * (DN + DR)]
        qrope = turned(tail, cosine[...], sine[...], 1.0).astype(bfloat)
        at = h * (DN + DV)
        w_uk = jnp.concatenate([w[:, at : at + DN] for w in kvbs], axis=0)
        w_uv = jnp.concatenate([w[:, at + DN : at + DN + DV] for w in kvbs], axis=0)
        query = dot_t(nope, w_uk).astype(bfloat)
        raw = dot_t(query, latents) + dot_t(qrope, ropes)
        scores = jnp.where(visible, raw * score_scale, masked_score)
        expd = jnp.exp(scores - jnp.max(scores, axis=1, keepdims=True))
        probs = expd / jnp.sum(expd, axis=1, keepdims=True)
        lat = dot(probs.astype(bfloat), latents).astype(bfloat)
        heads_ref[:, h * DV : (h + 1) * DV] = dot(lat, w_uv).astype(bfloat)
        nope_ref[:, h * DN : (h + 1) * DN] = nope
        qrope_ref[:, h * DR : (h + 1) * DR] = qrope
        abs_ref[:, h * rank : (h + 1) * rank] = query
        keys = probs.shape[1]
        probs_ref[:, h * keys : (h + 1) * keys] = probs
        lat_ref[:, h * rank : (h + 1) * rank] = lat


def heads_back_kernel(pieces, score_scale, *refs):
    refs = list(refs)
    g_ref = refs.pop(0)
    kvbs = [refs.pop(0) for _ in range(pieces)]
    latent, rope, cosine, sine = (refs.pop(0) for _ in range(4))
    nope_ref, qrope_ref, abs_ref, probs_ref, lat_ref = (refs.pop(0) for _ in range(5))
    gq_ref = refs.pop(0)
    gkvbs = [refs.pop(0) for _ in range(pieces)]
    key_ref, rope_out = refs
    latents, ropes = latent[...], rope[...]
    rank, keys = latents.shape[1], latents.shape[0]

    @pl.when(pl.program_id(0) == 0)
    def _():
        key_ref[...] = jnp.zeros_like(key_ref)
        rope_out[...] = jnp.zeros_like(rope_out)

    parts = []
    key_sum = key_ref[...]
    rope_sum = rope_out[...]
    for h in range(2):
        at = h * (DN + DV)
        w_uk = jnp.concatenate([w[:, at : at + DN] for w in kvbs], axis=0)
        w_uv = jnp.concatenate([w[:, at + DN : at + DN + DV] for w in kvbs], axis=0)
        grad = g_ref[:, h * DV : (h + 1) * DV]
        lat = lat_ref[:, h * rank : (h + 1) * rank]
        query = abs_ref[:, h * rank : (h + 1) * rank]
        nope = nope_ref[:, h * DN : (h + 1) * DN]
        qrope = qrope_ref[:, h * DR : (h + 1) * DR]
        probs = probs_ref[:, h * keys : (h + 1) * keys]
        grad_uv = t_dot(lat, grad).astype(bfloat)
        grad_lat = dot_t(grad, w_uv).astype(bfloat)
        grad_probs = dot_t(grad_lat, latents)
        delta = jnp.sum(probs * grad_probs, axis=1, keepdims=True)
        grad_scores = (probs * (grad_probs - delta)).astype(bfloat)
        grad_abs = (dot(grad_scores, latents) * score_scale).astype(bfloat)
        grad_rope = dot(grad_scores, ropes) * score_scale
        key_sum = key_sum + t_dot(grad_scores, query) * score_scale
        key_sum = key_sum + t_dot(probs.astype(bfloat), grad_lat)
        rope_sum = rope_sum + t_dot(grad_scores, qrope) * score_scale
        grad_uk = t_dot(grad_abs, nope).astype(bfloat)
        rows = rank // pieces
        for j in range(pieces):
            gkvbs[j][:, at : at + DN] = grad_uk[j * rows : (j + 1) * rows]
            gkvbs[j][:, at + DN : at + DN + DV] = grad_uv[j * rows : (j + 1) * rows]
        parts.append(dot(grad_abs, w_uk))
        parts.append(turned(grad_rope, cosine[...], sine[...], -1.0))
    gq_ref[...] = jnp.concatenate(parts, axis=1).astype(bfloat)
    key_ref[...] = key_sum
    rope_out[...] = rope_sum


def run_heads(q, kvbs, latent, rope, shown, cosine, sine, heads, score_scale):
    rows, pieces = q.shape[0], len(kvbs)
    keys, rank = latent.shape
    shape = jax.ShapeDtypeStruct
    own = lambda width: pl.BlockSpec((rows, width), lambda g: (0, g))
    still = lambda v: pl.BlockSpec(v.shape, lambda g: (0, 0))
    kvb = [pl.BlockSpec((w.shape[0], 2 * (DN + DV)), lambda g: (0, g)) for w in kvbs]
    widths = (DV, DN, DR, rank, keys, rank)
    kinds = (bfloat, bfloat, bfloat, bfloat, single, bfloat)
    return pl.pallas_call(
        functools.partial(heads_kernel, pieces, score_scale),
        grid=(heads // 2,),
        out_shape=[shape((rows, heads * w), k) for w, k in zip(widths, kinds)],
        in_specs=[own(2 * (DN + DR)), *kvb] + [still(v) for v in (latent, rope, shown, cosine, sine)],
        out_specs=[own(2 * w) for w in widths],
        compiler_params=pltpu.CompilerParams(vmem_limit_bytes=40 << 20),
        cost_estimate=pl.CostEstimate(flops=0, bytes_accessed=0, transcendentals=0),
    )(q, *kvbs, latent, rope, shown, cosine, sine)


def run_heads_back(grad, kvbs, latent, rope, cosine, sine, saved, heads, score_scale, others):
    rows, pieces = grad.shape[0], len(kvbs)
    keys, rank = latent.shape
    shape = jax.ShapeDtypeStruct
    own = lambda width: pl.BlockSpec((rows, width), lambda g: (0, g))
    still = lambda v: pl.BlockSpec(v.shape, lambda g: (0, 0))
    kvb = [pl.BlockSpec((w.shape[0], 2 * (DN + DV)), lambda g: (0, g)) for w in kvbs]
    widths = (DN, DR, rank, keys, rank)

    def body(*refs):
        cut = 1 + pieces + 4 + 5
        heads_back_kernel(pieces, score_scale, *refs[:cut], *refs[cut + len(others) :])

    out = pl.pallas_call(
        body,
        grid=(heads // 2,),
        out_shape=[shape((rows, heads * (DN + DR)), bfloat)]
        + [shape(w.shape, bfloat) for w in kvbs]
        + [shape((keys, rank), single), shape((keys, DR), single)],
        in_specs=[own(2 * DV), *kvb]
        + [still(v) for v in (latent, rope, cosine, sine)]
        + [own(2 * w) for w in widths]
        + [pl.BlockSpec(memory_space=pl.ANY)] * len(others),
        out_specs=[own(2 * (DN + DR)), *kvb]
        + [pl.BlockSpec((keys, rank), lambda g: (0, 0)), pl.BlockSpec((keys, DR), lambda g: (0, 0))],
        compiler_params=pltpu.CompilerParams(vmem_limit_bytes=40 << 20),
        cost_estimate=pl.CostEstimate(flops=0, bytes_accessed=0, transcendentals=0),
    )(grad, *kvbs, latent, rope, cosine, sine, *saved, *others)
    return out[0], out[1 : 1 + pieces], out[1 + pieces], out[2 + pieces]


def assemble_kernel(parts, cuts, fold, *refs):
    where, one_0, one_1, two_0, two_1, *outs = refs
    step = pl.program_id(0)
    _, m = parts
    row = jnp.where(step // m == where[0], one_0[...], one_1[...])
    column = jnp.where(step % m == where[1], two_0[...], two_1[...])
    value = jnp.concatenate([row, column], axis=1).astype(single)
    start = 0
    for i, (width, out) in enumerate(zip(cuts, outs)):
        piece = value[:, start : start + width]
        start += width
        if i == 0 and fold > 1:
            rows = piece.shape[0] // fold
            piece = jnp.concatenate(
                [piece[k * rows : (k + 1) * rows] for k in range(fold)], axis=1
            )
        if out.shape[0] == width and out.shape[0] != piece.shape[0]:
            piece = piece.T
        out[...] = piece


def assemble(chips, lines, cuts, fold, turned):
    n, m = chips.dims[1:]
    parts = n * m
    rows = lines[0][0].shape[0] * n // parts
    where = jnp.stack([chips.own(1), chips.own(2)]).astype(jnp.int32)
    one = pl.BlockSpec((rows, lines[0][0].shape[1]), lambda p: (p % m, 0))
    two = pl.BlockSpec((rows, lines[1][0].shape[1]), lambda p: (p // m, 0))
    shapes, specs = [], []
    for i, width in enumerate(cuts):
        if i == 0 and fold > 1:
            shapes.append((rows * parts // fold, width * fold))
            specs.append(pl.BlockSpec((rows // fold, width * fold), lambda p: (p, 0)))
        elif i in turned:
            shapes.append((width, rows * parts))
            specs.append(pl.BlockSpec((width, rows), lambda p: (0, p)))
        else:
            shapes.append((rows * parts, width))
            specs.append(pl.BlockSpec((rows, width), lambda p: (p, 0)))
    return pl.pallas_call(
        functools.partial(assemble_kernel, (n, m), cuts, fold),
        grid=(parts,),
        out_shape=[jax.ShapeDtypeStruct(v, single) for v in shapes],
        in_specs=[pl.BlockSpec(memory_space=pltpu.SMEM), one, one, two, two],
        out_specs=specs,
        compiler_params=pltpu.CompilerParams(vmem_limit_bytes=56 << 20),
        cost_estimate=pl.CostEstimate(flops=0, bytes_accessed=0, transcendentals=0),
    )(where, *lines[0], *lines[1])


def plane_kernel(count, rows, start, widths, fold, *refs):
    refs = list(refs)
    lefts = [refs.pop(0) for _ in range(count)]
    rights = [[refs.pop(0) for _ in range(rows)] for _ in widths]
    extra = refs[:-1]
    out = refs[-1]
    tok = lefts[0].shape[0] // rows
    cols = out.shape[0]
    at = 0
    if extra:
        kvb, small = extra
        size = kvb.shape[1] // fold
        for k in range(fold):
            here = pl.ds(k * kvb.shape[0], kvb.shape[0])
            out[here, :size] = kvb[:, k * size : (k + 1) * size]
        at = size
    for width, parts in zip(widths, rights):
        total = None
        for c in range(rows):
            for o in range(count):
                left = lefts[o][c * tok : (c + 1) * tok, start : start + cols]
                term = t_dot(left, parts[c][o * tok : (o + 1) * tok, :width])
                total = term if total is None else total + term
        value = total.astype(bfloat)
        if extra:
            value = jnp.concatenate([value, small[...]], axis=1)
        out[:, at : at + value.shape[1]] = value
        at += value.shape[1]


def plane_dot(lefts, start, cols, rights, widths, fold=1, extra=()):
    total = sum(widths)
    if extra:
        total += extra[0].shape[1] // fold + extra[1].shape[1]
    flat = [v for parts in rights for v in parts]
    vm = pl.BlockSpec(memory_space=pltpu.VMEM)
    return pl.pallas_call(
        functools.partial(plane_kernel, len(lefts), len(rights[0]), start, widths, fold),
        out_shape=jax.ShapeDtypeStruct((cols, total), bfloat),
        in_specs=[vm] * (len(lefts) + len(flat) + len(extra)),
        out_specs=vm,
        compiler_params=pltpu.CompilerParams(vmem_limit_bytes=48 << 20),
        cost_estimate=pl.CostEstimate(flops=0, bytes_accessed=0, transcendentals=0),
    )(*lefts, *flat, *extra)


def rows_kernel(value, out):
    lines, rows = value.shape[0], value.shape[2]
    for i in range(lines):
        out[i * rows : (i + 1) * rows] = value[i, 0].astype(single)


def in_rows(chips, value):
    lines, parts = chips.dims[0], chips.plane
    rows = value.shape[0] // (lines * parts)
    value = value.reshape(lines, parts, rows, -1)
    if rows % 16:
        return value.swapaxes(0, 1).reshape(lines * parts * rows, -1).astype(single)
    width = value.shape[3]
    return pl.pallas_call(
        rows_kernel,
        grid=(parts,),
        out_shape=jax.ShapeDtypeStruct((lines * parts * rows, width), single),
        in_specs=[pl.BlockSpec((lines, 1, rows, width), lambda p: (0, p, 0, 0))],
        out_specs=pl.BlockSpec((lines * rows, width), lambda p: (p, 0)),
        compiler_params=pltpu.CompilerParams(vmem_limit_bytes=48 << 20),
        cost_estimate=pl.CostEstimate(flops=0, bytes_accessed=0, transcendentals=0),
    )(value)


def widths_of(total):
    if total % 128:
        return [total]
    out = []
    while total > 0:
        out.append(min(384, total))
        total -= out[-1]
    return out


def tie(value, *others):
    hbm = pl.BlockSpec(memory_space=pl.ANY)
    return pl.pallas_call(
        lambda *refs: None,
        out_shape=jax.ShapeDtypeStruct(value.shape, value.dtype),
        in_specs=[hbm] * (1 + len(others)),
        out_specs=hbm,
        input_output_aliases={0: 0},
    )(value, *others)


def grid_of(experts, shards):
    if shards == 2 and experts % 4 == 0:
        return (experts // 4, 2, 2)
    side = math.isqrt(experts)
    return (side, side) if side * side == experts else (experts,)


class Chips:
    def __init__(self, dims, names):
        self.dims = dims
        self.names = names
        self.size = int(np.prod(dims))
        self.plane = self.size // dims[0]
        self.places = [tuple(int(v) for v in np.unravel_index(i, dims)) for i in range(self.size)]
        self.offsets = [
            tuple(int(v) for v in np.unravel_index(i, dims[1:])) for i in range(self.plane)
        ]

    def index(self, place):
        return int(np.ravel_multi_index(place, self.dims))

    def own(self, axis):
        return lax.axis_index(self.names[axis])

    def me(self):
        return lax.axis_index(self.names)

    def pairs(self, axis_of, by):
        out = []
        for i, place in enumerate(self.places):
            axis = axis_of(place)
            to = list(place)
            to[axis] = (to[axis] + by) % self.dims[axis]
            out.append((i, self.index(to)))
        return out

    def along(self, value, axis, by):
        n = self.dims[axis]
        return lax.ppermute(value, self.names[axis], [(i, (i + by) % n) for i in range(n)])

    def offset_by(self, value, offset):
        out = []
        for i, place in enumerate(self.places):
            to = [place[0]] + [
                (p + o) % d for p, o, d in zip(place[1:], offset, self.dims[1:])
            ]
            out.append((i, self.index(to)))
        return lax.ppermute(value, self.names, out)

    def first(self, block):
        return [block] + [self.along(block, 0, j) for j in range(1, self.dims[0])]

    def axes(self, j):
        if len(self.dims) < 3:
            return (0, len(self.dims) - 1)
        return (1, 2) if j % 2 == 0 else (2, 1)

    def hop_one(self, block, j):
        axis, _ = self.axes(j)
        return self.hop_line(block, axis) if axis else [block]

    def hop_two(self, blocks, j):
        _, axis = self.axes(j)
        both = jnp.concatenate(blocks, axis=0) if len(blocks) > 1 else blocks[0]
        return self.hop_line(both, axis) if axis else [both]

    def places_of(self, j):
        one, two = self.axes(j)
        if not one:
            return list(range(self.plane))
        out = []
        for t in range(self.dims[two]):
            for h in range(self.dims[one]):
                out.append(self.offsets.index((h, t) if one == 1 else (t, h)))
        return out

    def hop_line(self, block, axis):
        return [block] + [self.along(block, axis, s) for s in range(1, self.dims[axis])]

    def straight(self, block):
        return [self.offset_by(block, o) if any(o) else block for o in self.offsets]

    def straight_back(self, blocks):
        return [
            self.offset_by(b, [-v for v in o]) if any(o) else b
            for b, o in zip(blocks, self.offsets)
        ]

    def pack_of(self, j, p):
        if len(self.dims) != 3:
            return (p, j)
        half = self.dims[0] // 2
        y, x = self.offsets[p]
        part, rest = (x, y) if j < half else (y, x)
        return (j // half * 2 + part, rest * half + j % half)

    def packs_one(self, packs):
        if len(self.dims) != 3:
            return [self.straight_back(packs)]
        return [
            [packs[0], self.along(packs[1], 2, -1)],
            [packs[2], self.along(packs[3], 1, -1)],
        ]

    def packs_two(self, totals):
        if len(self.dims) != 3:
            return [[v] for v in totals]
        out = []
        for v, axis in zip(totals, (1, 2)):
            rows = v.shape[0] // 2
            out.append([v[:rows], self.along(v[rows:], axis, -1)])
        return out

    def sources(self, at_once):
        table = []
        for place in self.places:
            row = []
            for j in range(self.dims[0]):
                for p in range(self.plane) if j in at_once else self.places_of(j):
                    offset = (j, *self.offsets[p])
                    row.append(self.index([(q - o) % d for q, o, d in zip(place, offset, self.dims)]))
            table.append(row)
        return jnp.asarray(np.array(table, np.int32))[self.me()]

    def back_first(self, total, j):
        return self.along(total.astype(bfloat), 0, -j) if j else total

    def own_part(self):
        part = 0
        for axis in range(1, len(self.dims)):
            part = part * self.dims[axis] + self.own(axis)
        return part

    def swap_columns(self, *values):
        out = []
        for offset in self.offsets:
            part = 0
            for axis, by in enumerate(offset):
                n = self.dims[axis + 1]
                part = part * n + (self.own(axis + 1) + by) % n
            pieces = []
            for v in values:
                size = v.shape[1] // self.plane
                pieces.append(lax.dynamic_slice_in_dim(v, part * size, size, 1))
            piece = jnp.concatenate(pieces, axis=1)
            out.append(self.offset_by(piece, offset) if any(offset) else piece)
        return out

    def orders(self):
        return ((2, 1), (1, 2)) if len(self.dims) == 3 else ((1,),)

    def halves(self, value):
        if len(self.dims) != 3:
            return [value]
        cut = value.shape[1] // 256 * 128
        return [value[:, :cut], value[:, cut:]]

    def stack_one(self, value):
        return [self.hop_line(v, o[0]) for v, o in zip(self.halves(value), self.orders())]

    def stack_two(self, lines, mark):
        out = []
        for line, order in zip(lines, self.orders()):
            both = jnp.concatenate(hold(line, mark), axis=0)
            out.append(self.hop_line(both, order[1]) if len(order) > 1 else [both])
        return out

    def stack_done(self, lines, mark):
        out = []
        for line, order in zip(lines, self.orders()):
            line = hold(line, mark)
            if order == (1, 2):
                n = self.dims[1]
                rows = line[0].shape[0] // n
                line = [v[s * rows : (s + 1) * rows] for s in range(n) for v in line]
            out.append(jnp.concatenate(line, axis=0))
        return out

    def send_rows(self, value):
        size = value.shape[0] // self.plane
        out = []
        for offset in self.offsets:
            part = 0
            for axis, by in enumerate(offset):
                n = self.dims[axis + 1]
                part = part * n + (self.own(axis + 1) + by) % n
            piece = lax.dynamic_slice_in_dim(value, part * size, size, 0)
            out.append(self.offset_by(piece, offset) if any(offset) else piece)
        return out

    def line_send(self, value):
        n = self.dims[0]
        rows = value.shape[0] // n
        own = self.own(0)
        out = [lax.dynamic_slice_in_dim(value, own * rows, rows, 0)]
        for j in range(1, n):
            piece = lax.dynamic_slice_in_dim(value, ((own + j) % n) * rows, rows, 0)
            out.append(self.along(piece, 0, j))
        return out

    def gather_one(self, halves):
        return [self.hop_line(v, o[0]) for v, o in zip(halves, self.orders())]

    def gather_two(self, lines, mark):
        out = []
        for line, order in zip(lines, self.orders()):
            line = hold(line, mark)
            own = self.own(order[0])
            if len(order) == 1:
                out.append([in_order(line, own, 0)])
            else:
                both = in_order(line, own, 0)
                out.append(self.hop_line(both, order[1]))
        return out

    def gather_done(self, lines, mark):
        out = []
        for line, order in zip(lines, self.orders()):
            line = hold(line, mark)
            if len(order) == 1:
                out.append(line[0])
            elif order == (1, 2):
                n = self.dims[1]
                rows = line[0].shape[0] // n
                cut = [[v[i * rows : (i + 1) * rows] for v in line] for i in range(n)]
                out += [jnp.concatenate([in_order(v, self.own(2), 0) for v in cut], axis=0)]
            else:
                out.append(in_order(line, self.own(order[1]), 0))
        return jnp.concatenate(out, axis=1)


def hold(values, *others):
    return [values[0]] + [tie(v, *others) for v in values[1:]]


def visit(mark, lines, singles=()):
    lines = [[v[0]] + [tie(x, mark) for x in v[1:]] for v in lines]
    singles = [tie(v, mark) for v in singles]
    mark = tie(lines[0][0], mark, *[x for v in lines for x in v[1:]], *singles)
    lines = [[mark] + lines[0][1:]] + [[tie(v[0], mark)] + v[1:] for v in lines[1:]]
    return mark, lines, [tie(v, mark) for v in singles]


def add_up(values):
    return sum([v.astype(single) for v in values[1:]], values[0].astype(single)).astype(bfloat)


def split(value, widths):
    out, start = [], 0
    for width in widths:
        out.append(value[:, start : start + width])
        start += width
    return out


def in_order(pieces, own, axis):
    n = len(pieces)
    if n == 1:
        return pieces[0]
    if n == 2:
        return jnp.where(
            own == 0,
            jnp.concatenate(pieces, axis=axis),
            jnp.concatenate([pieces[1], pieces[0]], axis=axis),
        )
    turned = pieces[::-1]
    line = jnp.concatenate(turned + turned[:-1], axis=axis)
    extent = pieces[0].shape[axis]
    return lax.dynamic_slice_in_dim(line, (n - 1 - own) * extent, n * extent, axis)


class Cores:
    def __init__(self, count):
        self.count = count
        self.own = lax.axis_index("shard")

    def along(self, value, by):
        n = self.count
        return lax.ppermute(value, "shard", [(i, (i + by) % n) for i in range(n)])

    def spread(self, value):
        return [value] + [self.along(value, j) for j in range(1, self.count)]

    def whole(self, value, axis):
        return in_order(self.spread(value), self.own, axis)

    def chunk(self, value, j, axis):
        size = value.shape[axis] // self.count
        place = (self.own + j + self.count) % self.count
        return lax.dynamic_slice_in_dim(value, place * size, size, axis)

    def rows_times(self, left, pieces):
        out = None
        for j, piece in enumerate(pieces):
            term = dot(self.chunk(left, -j, 1), piece)
            out = term if out is None else out + term
        return out

    def times_rows_t(self, left, pieces):
        return in_order([dot_t(left, piece) for piece in pieces], self.own, 1)

    def swap_columns(self, *values):
        out = []
        for j in range(self.count):
            piece = jnp.concatenate([self.chunk(v, j, 1) for v in values], axis=1)
            out.append(self.along(piece, j) if j else piece)
        return split(jnp.concatenate(out, axis=0), [v.shape[1] // self.count for v in values])

    def stack(self, value):
        return jnp.concatenate(self.spread(value), axis=0)

    def give_back(self, value):
        rows = value.shape[0] // self.count
        total = value[:rows]
        for j in range(1, self.count):
            total = total + self.along(value[j * rows : (j + 1) * rows], -j)
        return total

    def scatter(self, value, axis):
        total = self.chunk(value, 0, axis).astype(single)
        for j in range(1, self.count):
            total = total + self.along(self.chunk(value, j, axis).astype(bfloat), j).astype(single)
        return total


def per_device(
    chips,
    shards,
    tokens,
    segment_ids,
    routes,
    cotangent,
    gain_attn,
    gain_query,
    gain_latent,
    gain_ffn,
    w_qa,
    w_qb,
    w_kva,
    w_kvb,
    w_out,
    w_router,
    shared_gate,
    shared_up,
    shared_down,
    expert_gate,
    expert_up,
    expert_down,
):
    cores = Cores(shards)
    me = chips.me()
    shard_pos = cores.own
    tok_rows = tokens.shape[0]
    model = tokens.shape[1]
    group_rows = tok_rows * shards
    score_scale = 1.0 / (DN + DR) ** 0.5
    query_rank = w_qa.shape[1]

    gains = jnp.concatenate([gain_attn, gain_query, gain_latent, gain_ffn])
    gain_pieces = cores.spread(gains)
    sizes = [v.shape[0] for v in (gain_attn, gain_query, gain_latent, gain_ffn)]
    full_gains = []
    start = 0
    for size in sizes:
        full_gains.append(
            in_order([g[start : start + size] for g in gain_pieces], shard_pos, 0).astype(single)
        )
        start += size
    gain_attn_f, gain_query_f, gain_latent_f, gain_ffn_f = full_gains
    qa_pieces = cores.spread(w_qa)
    kva_pieces = cores.spread(w_kva)
    qb_pieces = cores.spread(w_qb)
    kvb_pieces = cores.spread(w_kvb)
    out_pieces = cores.spread(w_out)
    router_full = cores.whole(w_router, 0)
    expert_weights = [
        cores.spread(expert_gate[0].T),
        cores.spread(expert_up[0].T),
        cores.spread(expert_down[0]),
    ]
    turns = chips.dims[0]
    order = [0] + list(range(1, turns, 2)) + list(range(2, turns, 2))
    order_back = [0] + list(range(2, turns, 2)) + list(range(1, turns, 2))
    all_cots = lax.all_gather(cotangent, chips.names, axis=0, tiled=True)

    resid = tokens.astype(single)
    attn_scale = row_scale(resid)
    attn_normed = resid * attn_scale
    attn_in = (attn_normed * gain_attn_f).astype(bfloat)
    query_lat = cores.rows_times(attn_in, qa_pieces)
    query_scale = row_scale(query_lat)
    query_normed = query_lat * query_scale
    query_in = (query_normed * gain_query_f).astype(bfloat)
    query_all = cores.rows_times(query_in, qb_pieces)
    group_pos = seq_positions(segment_ids)
    own_start = shard_pos * tok_rows
    own_pos = lax.dynamic_slice_in_dim(group_pos, own_start, tok_rows, 0)
    own_seg = lax.dynamic_slice_in_dim(segment_ids, own_start, tok_rows, 0)
    cosine, sine = rope_tables(own_pos, DR // 2)
    latent_raw = cores.rows_times(attn_in, kva_pieces)
    latent_part = latent_raw[:, :KR]
    latent_scale = row_scale(latent_part)
    latent_normed = latent_part * latent_scale
    latent = (latent_normed * gain_latent_f).astype(bfloat)
    key_rope = rotate(latent_raw[:, KR:], cosine, sine).astype(bfloat)
    keys = cores.whole(jnp.concatenate([latent, key_rope], axis=1), 0)
    keys_latent, keys_rope = keys[:, :KR], keys[:, KR:]
    keys_turned = jnp.concatenate(
        [cores.chunk(keys_latent, -j, 1) for j in range(shards)], axis=1
    )
    group_index = jnp.arange(group_rows, dtype=jnp.int32)
    own_index = own_start + jnp.arange(tok_rows, dtype=jnp.int32)
    visible = (own_seg[:, None] == segment_ids[None, :]) & (
        group_index[None, :] <= own_index[:, None]
    )

    attn_heads, *saved = run_heads(
        query_all,
        kvb_pieces,
        keys_turned,
        keys_rope,
        visible.astype(single),
        cosine,
        sine,
        H,
        score_scale,
    )
    mid = resid + cores.rows_times(attn_heads, out_pieces)
    ffn_scale = row_scale(mid)
    ffn_normed = mid * ffn_scale
    ffn_in = (ffn_normed * gain_ffn_f).astype(bfloat)

    experts_all = router_full.shape[1]
    lanes = -(-4 * experts_all // 128) * 128
    logits = dot(ffn_in, router_full)
    chosen = jnp.sum(
        (routes[:, :, None] == jnp.arange(experts_all, dtype=jnp.int32)[None, None, :]).astype(
            single
        ),
        axis=1,
    )
    sig = jax.nn.sigmoid(logits)
    denom = jnp.sum(chosen * sig, axis=-1, keepdims=True)
    routing_weights = route_scale * chosen * sig / denom
    capacity = min(tok_rows, 4 * tok_rows * TOP // (3 * experts_all))
    earlier = (jnp.arange(tok_rows)[:, None] > jnp.arange(tok_rows)[None, :]).astype(bfloat)
    slot = dot(earlier, chosen.astype(bfloat))
    code = jnp.where(chosen > 0, slot, -1.0)
    weight_high = routing_weights.astype(bfloat)
    weight_rest = (routing_weights - weight_high.astype(single)).astype(bfloat)
    marks = jnp.concatenate(
        [
            code.astype(bfloat),
            weight_high,
            weight_rest,
            jnp.zeros((tok_rows, lanes - 3 * experts_all), bfloat),
        ],
        axis=1,
    )
    payload = jnp.concatenate([ffn_in, marks], axis=1)
    first = chips.first(payload)
    one, two = [None] * turns, [None] * turns
    two[0] = chips.straight(payload)

    stack_ffn = cores.stack(ffn_in)
    stack_cot = cores.stack(cotangent)

    def feed_forward(rows, grads, gate, up, down):
        pre_gate = dot(rows, gate)
        pre_up = dot(rows, up)
        hidden = (jax.nn.silu(pre_gate) * pre_up).astype(bfloat)
        grad_gate, grad_up = silu_grads(dot_t(grads, down), pre_gate, pre_up)
        return hidden, grad_gate, grad_up

    sh_hidden, sh_gate, sh_up = feed_forward(
        stack_ffn, stack_cot, shared_gate, shared_up, shared_down
    )
    sh_back = dot_t(sh_gate, shared_gate) + dot_t(sh_up, shared_up)
    shared_out = cores.give_back(dot(sh_hidden, shared_down))
    shared_back = cores.give_back(sh_back)

    at_once = order[:2]
    who = jnp.concatenate([me.astype(jnp.int32).reshape(1), chips.sources(at_once)])
    kept, kept_back = None, None
    sent, grads_of = [], []

    def parts_of(i):
        if i == 2:
            return kept[5 : 5 + shards], kept_back[0]
        return kept_back[2 + i * shards : 2 + (i + 1) * shards], kept[0]

    def others_part(i, waits):
        left, right = parts_of(i)
        out = [t_dot(tie(v, *waits), right).astype(bfloat) for v in left[1:]]
        sent.append([cores.along(v, -j - 1) for j, v in enumerate(out)])
        return out[-1]

    def own_part(i, waits):
        left, right = parts_of(i)
        got = [tie(v, *waits).astype(single) for v in sent[i]]
        grads_of.append(sum(got, t_dot(tie(left[0], *waits), right)))
        return grads_of[-1]

    fillers = [
        lambda waits: others_part(1, [others_part(0, waits)]),
        lambda waits: others_part(2, waits),
        lambda waits: own_part(1, [own_part(0, waits)]),
    ]
    mark = sh_back
    backs = [None] * turns

    def places_of(j):
        return list(range(chips.plane)) if j in at_once else chips.places_of(j)

    def forward_step(step):
        nonlocal kept, mark
        waits = [mark]
        if step + 1 < turns:
            k = order[step + 1]
            if k in at_once:
                first[k] = tie(first[k], mark)
                two[k] = chips.straight(first[k])
                waits.append(first[k])
            else:
                one[k] = hold(one[k], mark)
                two[k] = chips.hop_two(one[k], k)
                waits.append(one[k][0])
        if step + 2 < turns:
            k = order[step + 2]
            first[k] = tie(first[k], mark)
            one[k] = chips.hop_one(first[k], k)
            waits.append(first[k])
        j = order[step]
        mark, kept = run_experts(
            who,
            two[j],
            expert_weights,
            capacity,
            experts_all,
            j,
            turns,
            [chips.pack_of(j, p) for p in places_of(j)],
            kept,
            waits,
        )

    def backward_step(step):
        nonlocal kept_back, mark
        waits = [mark]
        if 2 <= step:
            k = order_back[step - 2]
            total = add_up(hold(backs[k], mark))
            backs[k] = chips.back_first(total, k)
            waits.append(total)
        if step >= turns:
            mark = fillers[step - turns](waits)
            return
        j = order_back[step]
        back_blocks, kept_back = run_experts_back(
            who,
            two[j],
            all_cots,
            expert_weights,
            kept[2:5],
            capacity,
            experts_all,
            j,
            turns,
            True,
            kept_back,
            waits,
        )
        places = places_of(j)
        back_blocks = [back_blocks[places.index(p)] for p in range(chips.plane)]
        backs[j] = chips.straight_back(back_blocks)
        mark = back_blocks[0]

    ahead = min(2, turns)
    for step in range(ahead):
        forward_step(step)
    backward_step(0)
    for step in range(ahead, turns):
        forward_step(step)
    for step in range(1, turns + 2):
        backward_step(step)
    out_packs = kept[5 + shards :]
    routed_back = backs[0].astype(single)
    for j in order[1:]:
        routed_back = routed_back + tie(backs[j], mark).astype(single)
    chip_ffn, chip_cot = kept[1], kept_back[1]

    grad_out = cotangent.astype(single)
    grad_weights = (
        routed_back[:, model : model + experts_all]
        + routed_back[:, model + experts_all : model + 2 * experts_all]
    )
    grad_sig = chosen * (
        route_scale * grad_weights / denom
        - jnp.sum(grad_weights * routing_weights, axis=-1, keepdims=True) / denom
    )
    grad_logits = grad_sig * sig * (1.0 - sig)
    grad_router = jnp.einsum("te,td->ed", grad_logits, ffn_in.astype(single), precision=highest)
    grad_ffn_in = (
        routed_back[:, :model]
        + shared_back
        + jnp.einsum("te,de->td", grad_logits, router_full.astype(single), precision=highest)
    )
    grad_mid, grad_gffn = norm_back(grad_ffn_in, ffn_normed, ffn_scale, gain_ffn_f)
    grad_mid = grad_mid + grad_out

    grad_attn_out = grad_mid.astype(bfloat)
    heads_line = chips.stack_one(grad_attn_out)
    lefts = cores.swap_columns(attn_in, query_in, tie(attn_heads, sh_back))
    lefts = chips.swap_columns(*[tie(v, mark) for v in lefts])
    sent[:] = [[tie(v, grad_attn_out) for v in line] for line in sent]
    grad_attn_out = tie(grad_attn_out, *[v for line in sent for v in line])
    grad_heads = cores.times_rows_t(grad_attn_out, out_pieces).astype(bfloat)
    heads_line = chips.stack_two(heads_line, grad_heads)
    grad_query, kvb_parts, key_terms, rope_terms = run_heads_back(
        grad_heads,
        kvb_pieces,
        keys_turned,
        keys_rope,
        cosine,
        sine,
        saved,
        H,
        score_scale,
        [v[0] for v in heads_line],
    )
    heads_line = [hold(v, grad_query) for v in heads_line]
    lefts = hold(lefts, grad_query)
    there = [v for line in [*heads_line, lefts] for v in line[1:]]
    grad_query = tie(grad_query, *there)
    heads_all = [cores.spread(v) for v in chips.stack_done(heads_line, grad_query)]
    query_line = chips.stack_one(grad_query)
    kvb_terms = add_up(
        [kvb_parts[0]] + [cores.along(v, -j - 1) for j, v in enumerate(kvb_parts[1:])]
    )
    kvb_part = lax.psum_scatter(kvb_terms, chips.names[1:], scatter_dimension=0, tiled=True)
    size = KR // shards
    key_terms = in_order(
        [key_terms[:, j * size : (j + 1) * size] for j in range(shards)], shard_pos, 1
    )
    grad_keys = cores.scatter(jnp.concatenate([key_terms, rope_terms], axis=1), 0)
    grad_latent, grad_krope = grad_keys[:, :KR], grad_keys[:, KR:]
    grad_query_in = cores.times_rows_t(grad_query, qb_pieces)
    grad_qlat, grad_gquery = norm_back(grad_query_in, query_normed, query_scale, gain_query_f)
    grad_kvpart, grad_glatent = norm_back(grad_latent, latent_normed, latent_scale, gain_latent_f)
    grad_kvrope = rotate_back(grad_krope, cosine, sine)
    grad_low = jnp.concatenate([grad_qlat, grad_kvpart, grad_kvrope], axis=-1).astype(bfloat)
    shared_weights = (shared_gate, shared_up, shared_down)
    xs, cs = cores.spread(tie(chip_ffn, routed_back)), cores.spread(tie(chip_cot, routed_back))
    widths = widths_of(shared_gate.shape[1]) if shards == 2 else []
    shared_grads = None
    start = 0

    def shared_step(waits):
        nonlocal shared_grads, start
        if not widths:
            return waits[0]
        width = widths.pop(0)
        shared_grads = run_shared(xs, cs, shared_weights, start, width, shared_grads, waits)
        start += width
        return shared_grads[0]

    low_wide = jnp.pad(grad_low, ((0, 0), (0, -grad_low.shape[1] % 128)))
    low_line = chips.straight(low_wide)
    mark = fillers[2]([grad_low, kvb_terms, *[v[0] for v in query_line]])
    query_line = chips.stack_two(query_line, mark)
    sizes = [v.shape[1] // (shards * chips.plane) for v in (attn_in, query_in, attn_heads)]
    part = plane_dot(
        lefts, sizes[0] + sizes[1], sizes[2], heads_all, [v[0].shape[1] for v in heads_all]
    )
    part_sums = lax.psum_scatter(part, chips.names[0], scatter_dimension=0, tiled=True)
    mark = shared_step([part, low_line[0]] + [v[0] for v in query_line])
    mark, lines, (part_sums, kvb_part) = visit(
        mark, [low_line, *query_line], [part_sums, kvb_part]
    )
    low_line, *query_line = lines
    part_all = lax.all_gather(part_sums, chips.names, axis=0, tiled=True)
    mark = tie(grad_low, mark)
    grad_low = mark
    grad_attn_in = in_order(
        [
            dot_t(grad_low[:, :query_rank], qa) + dot_t(grad_low[:, query_rank:], kva)
            for qa, kva in zip(qa_pieces, kva_pieces)
        ],
        shard_pos,
        1,
    )
    grad_resid, grad_gattn = norm_back(grad_attn_in, attn_normed, attn_scale, gain_attn_f)
    grad_tokens = grad_mid + grad_resid
    mixed = jnp.concatenate(
        [grad_gquery.reshape(shards, -1), grad_glatent.reshape(shards, -1)], axis=1
    ).reshape(-1)
    small = jnp.concatenate(
        [grad_gattn[None], grad_gffn[None], mixed[None], grad_router], axis=0
    )
    small_line = chips.send_rows(cores.scatter(small, 1).T.astype(bfloat))
    query_all = [cores.spread(v) for v in chips.stack_done(query_line, mark)]
    query_part = plane_dot(
        lefts, sizes[0], sizes[1], query_all, [v[0].shape[1] for v in query_all]
    )
    query_sums = lax.psum_scatter(query_part, chips.names[0], scatter_dimension=0, tiled=True)
    low_all = cores.spread(jnp.concatenate(low_line, axis=0))
    small_part = add_up(hold(small_line, query_part))
    low_cols = grad_low.shape[1]
    spare = low_wide.shape[1] - low_cols - small_part.shape[1]
    fold = sizes[2] // kvb_part.shape[0]
    kvb_cols = kvb_part.shape[1] // fold
    small_wide = jnp.pad(small_part, ((0, 0), (0, spare)))
    low_part = plane_dot(
        lefts, 0, sizes[0], [low_all], [low_cols], fold, (kvb_part, small_wide)
    )
    low_line = chips.line_send(low_part)
    out_lines = chips.packs_one([tie(v, small_part) for v in out_packs])
    mark = shared_step([query_part, low_line[0]])
    mark, lines, (query_sums,) = visit(mark, [low_line, *out_lines], [query_sums])
    low_line, *out_lines = lines
    query_all = lax.all_gather(query_sums, chips.names, axis=0, tiled=True)
    low_line = chips.hop_line(add_up(low_line), 0)
    out_lines = chips.packs_two([add_up(v) for v in out_lines])
    waits = [v[0] for v in out_lines]
    mark = shared_step(waits + [low_line[0]])
    mark, lines, (part_all,) = visit(mark, [low_line, *out_lines], [part_all])
    low_line, *out_lines = lines
    low_all = in_order(low_line, chips.own(0), 0)
    low_line = chips.gather_one(chips.halves(low_all))
    totals = jnp.concatenate([add_up(v) for v in out_lines], axis=0)
    back_sums = [
        chips.back_first(totals[j * tok_rows : (j + 1) * tok_rows], j) for j in range(turns)
    ]
    mark = shared_step([v[0] for v in low_line] + back_sums[:1])
    mark, low_line, back_sums[1:] = visit(mark, low_line, back_sums[1:])
    low_line = chips.gather_two(low_line, mark)
    routed_out = back_sums[0].astype(single)
    for j in range(1, turns):
        routed_out = routed_out + tie(back_sums[j], mark).astype(single)
    result = mid + shared_out + routed_out
    mark = own_part(2, [mark])
    grad_egate = grads_of[0].T[None]
    grad_eup = grads_of[1].T[None]
    grad_edown = grads_of[2][None]
    grad_wout = in_rows(chips, tie(part_all, result))
    grad_wqb = in_rows(chips, tie(query_all, grad_wout))
    low_cuts = [kvb_cols, query_rank, low_cols - query_rank, small_part.shape[1] + spare]
    if len(chips.dims) == 3:
        low_line = [hold(v, grad_wqb, mark) for v in low_line]
        grad_wkvb, grad_wqa, grad_wkva, small = assemble(chips, low_line, low_cuts, fold, (2,))
        grad_wkva = grad_wkva.T
    else:
        low_all = chips.gather_done(low_line, mark).astype(single)
        kvb_all, grad_wqa, grad_wkva, small = split(low_all, low_cuts)
        kvb_all = kvb_all.reshape(chips.plane, fold, -1, kvb_cols)
        grad_wkvb = kvb_all.swapaxes(1, 2).reshape(-1, fold * kvb_cols)

    if shards == 2:
        grad_sgate, grad_sup, grad_sdown = shared_grads
    else:
        grad_sgate = grad_sup = grad_sdown = 0.0
        all_ffn, all_cot = chip_ffn, chip_cot
        for turn in range(shards):
            if turn > 0:
                tied = lax.optimization_barrier(
                    (all_ffn, all_cot, grad_sgate, grad_sup, grad_sdown)
                )
                grad_sgate, grad_sup, grad_sdown = tied[2:]
                all_ffn, all_cot = cores.along(tied[0], 1), cores.along(tied[1], 1)
            all_hidden, all_gate, all_up = feed_forward(
                all_ffn, all_cot, shared_gate, shared_up, shared_down
            )
            grad_sgate = grad_sgate + t_dot(all_ffn, all_gate)
            grad_sup = grad_sup + t_dot(all_ffn, all_up)
            grad_sdown = grad_sdown + t_dot(all_hidden, all_cot)
    query_part = gain_query.shape[0]
    return (
        result,
        grad_tokens,
        small[:, 0],
        small[:query_part, 2],
        small[query_part:, 2],
        small[:, 1],
        grad_wqa,
        grad_wqb,
        grad_wkva,
        grad_wkvb,
        grad_wout,
        small[:, 3 : 3 + experts_all],
        grad_sgate,
        grad_sup,
        grad_sdown,
        grad_egate,
        grad_eup,
        grad_edown,
    )


def solution(mesh):
    shards = mesh.shape["shard"]
    dims = grid_of(mesh.shape["expert"], shards)
    names = tuple(f"line{i}" for i in range(len(dims)))
    grid = jax.sharding.Mesh(mesh.devices.reshape(dims + (shards,)), names + ("shard",))
    chips = Chips(dims, names)
    both = names + ("shard",)
    in_specs = (
        P(both, None),
        P(names),
        P(both, None),
        P(both, None),
        P("shard"),
        P("shard"),
        P("shard"),
        P("shard"),
        P("shard", None),
        P("shard", None),
        P("shard", None),
        P("shard", None),
        P("shard", None),
        P("shard", None),
        P(None, "shard"),
        P(None, "shard"),
        P("shard", None),
        P(names, None, "shard"),
        P(names, None, "shard"),
        P(names, "shard", None),
    )
    out_specs = (
        P(both, None),
        P(both, None),
        P("shard"),
        P("shard"),
        P("shard"),
        P("shard"),
        P("shard", None),
        P("shard", None),
        P("shard", None),
        P("shard", None),
        P("shard", None),
        P("shard", None),
        P(None, "shard"),
        P(None, "shard"),
        P("shard", None),
        P(names, None, "shard"),
        P(names, None, "shard"),
        P(names, "shard", None),
    )

    def body(*args):
        return per_device(chips, shards, *args)

    return jax.shard_map(
        body, mesh=grid, in_specs=in_specs, out_specs=out_specs, check_vma=False
    )
```

```python
import functools
import math

import jax
import jax.numpy as jnp
import numpy as np
from jax import lax
from jax.experimental import pallas as pl
from jax.experimental.pallas import tpu as pltpu
from jax.sharding import PartitionSpec as P

H = 16
DN = 128
DR = 64
DV = 128
KR = 512
TOP = 6


norm_eps = 1e-06
rope_base = 50000.0
route_scale = 2.446
masked_score = -1e30
highest = lax.Precision.HIGHEST
bfloat = jnp.bfloat16
single = jnp.float32


def row_scale(values):
    return lax.rsqrt(jnp.mean(values * values, axis=-1, keepdims=True) + norm_eps)


def norm_back(grad_out, normed_rows, scale_rows, gain):
    grad_normed = grad_out * gain
    grad_input = scale_rows * (
        grad_normed - normed_rows * jnp.mean(grad_normed * normed_rows, axis=-1, keepdims=True)
    )
    return (grad_input, jnp.sum(grad_out * normed_rows, axis=0))


def seq_positions(segments):
    token_count = segments.shape[0]
    index = jnp.arange(token_count, dtype=jnp.int32)
    change = jnp.concatenate([jnp.ones((1,), bool), segments[1:] != segments[:-1]])
    starts = lax.cummax(jnp.where(change, index, 0), axis=0)
    return index - starts


def rope_tables(positions, half):
    freq = rope_base ** (-jnp.arange(half, dtype=jnp.float32) / half)
    angles = positions.astype(jnp.float32)[:, None] * freq[None, :]
    return (jnp.cos(angles), jnp.sin(angles))


def rotate(values, cosine, sine):
    half = values.shape[-1] // 2
    first = values[..., :half]
    second = values[..., half:]
    return jnp.concatenate(
        [first * cosine - second * sine, second * cosine + first * sine], axis=-1
    )


def rotate_back(grads, cosine, sine):
    half = grads.shape[-1] // 2
    first = grads[..., :half]
    second = grads[..., half:]
    return jnp.concatenate(
        [first * cosine + second * sine, second * cosine - first * sine], axis=-1
    )


def silu_grads(grad_hidden, pre_gate, pre_up):
    sigma = jax.nn.sigmoid(pre_gate)
    grad_gate = grad_hidden * pre_up * sigma * (1.0 + pre_gate * (1.0 - sigma))
    grad_up = grad_hidden * pre_gate * sigma
    return (grad_gate.astype(bfloat), grad_up.astype(bfloat))


def dot(left, right):
    return jnp.dot(left, right, preferred_element_type=single)


def dot_t(left, right):
    return lax.dot_general(left, right, (((1,), (1,)), ((), ())), preferred_element_type=single)


def t_dot(left, right):
    return lax.dot_general(left, right, (((0,), (0,)), ((), ())), preferred_element_type=single)


def expert_marks(marks, me, experts, capacity):
    marks = marks.astype(single)
    lane = lax.broadcasted_iota(jnp.int32, marks.shape, 1)
    place = lax.broadcasted_iota(jnp.int32, (marks.shape[0], capacity), 1).astype(single)
    code = jnp.sum(jnp.where(lane == me, marks, 0.0), axis=1, keepdims=True)
    weight = (lane == me + experts) | (lane == me + 2 * experts)
    weight = jnp.sum(jnp.where(weight, marks, 0.0), axis=1, keepdims=True)
    return (code == place).astype(single).astype(bfloat), weight, lane


def views(arrays, tok):
    return [(v, at) for v in arrays for at in range(0, v.shape[0], tok)]


def expert_kernel(arrays, tok, pieces, capacity, experts, group, places, first, waits, *refs):
    refs = list(refs)
    me_ref = refs.pop(0)
    count = len(places)
    blocks = views([refs.pop(0) for _ in range(arrays)], tok)
    weights = [[refs.pop(0) for _ in range(pieces)] for _ in range(3)]
    refs = refs[waits:]
    if not first:
        refs = refs[5 + pieces + count :]
    mark = refs.pop(0)
    rows_all, ffn_all, gate_all, up_all, out_all = (refs.pop(0) for _ in range(5))
    hidden_all = [refs.pop(0) for _ in range(pieces)]
    packs = [refs.pop(0) for _ in range(count)]
    full = [refs.pop(0) for _ in range(3)]
    rows, gate_scr, up_scr, out_scr = (refs.pop(0) for _ in range(4))
    hidden_scr = [refs.pop(0) for _ in range(pieces)]
    outs = refs.pop(0)
    sem_w, sem_o = refs
    model = rows.shape[1]
    width = weights[0][0].shape[0]
    loads = [[], [], []]
    for k in range(3):
        for j in range(pieces):
            c = pltpu.make_async_copy(
                weights[k][j], full[k].at[pl.ds(j * width, width)], sem_w.at[k, j]
            )
            c.start()
            loads[k].append(c)
    stores = []

    def store(src, dst):
        c = pltpu.make_async_copy(src, dst, sem_o.at[len(stores)])
        c.start()
        stores.append(c)

    me = me_ref[0]
    n = count * capacity
    mine = pl.ds(group * n, n)
    picks = []
    for i in range(count):
        ref, at = blocks[i]
        pick, weight, _ = expert_marks(
            ref[at : at + tok, model : model + 128], me, experts, capacity
        )
        picks.append((pick, weight))
        rows[pl.ds(i * capacity, capacity)] = t_dot(pick, ref[at : at + tok, :model]).astype(bfloat)
    store(rows, rows_all.at[mine])
    for i in range(count):
        store(
            blocks[i][0].at[pl.ds(blocks[i][1], tok), pl.ds(0, model)],
            ffn_all.at[pl.ds((group * count + i) * tok, tok)],
        )
    for c in loads[0]:
        c.wait()
    pre_gate = dot_t(rows[...], full[0][...])
    gate_scr[...] = pre_gate
    store(gate_scr, gate_all.at[mine])
    for c in loads[1]:
        c.wait()
    pre_up = dot_t(rows[...], full[1][...])
    up_scr[...] = pre_up
    store(up_scr, up_all.at[mine])
    hidden = (pre_gate * jax.nn.sigmoid(pre_gate) * pre_up).astype(bfloat)
    for j in range(pieces):
        hidden_scr[j][...] = hidden[:, j * width : (j + 1) * width]
        store(hidden_scr[j], hidden_all[j].at[mine])
    for c in loads[2]:
        c.wait()
    out = dot(hidden, full[2][...]).astype(bfloat)
    out_scr[...] = out
    store(out_scr, out_all.at[mine])
    for i, (pick, weight) in enumerate(picks):
        got = dot(pick, out[i * capacity : (i + 1) * capacity])
        outs[i] = (weight * got).astype(bfloat)
        pack, at = places[i]
        store(outs.at[i], packs[pack].at[pl.ds(at * tok, tok)])
    mark[...] = jnp.zeros_like(mark)
    for c in stores:
        c.wait()


def run_experts(me, blocks, weights, capacity, experts, group, groups, places, carried, others):
    count, pieces = len(places), len(weights[0])
    tok, model = sum(v.shape[0] for v in blocks) // count, weights[0][0].shape[1]
    width = weights[0][0].shape[0]
    n = count * capacity
    shape = jax.ShapeDtypeStruct
    kept = [
        shape((groups * n, model), bfloat),
        shape((groups * count * tok, model), bfloat),
        shape((groups * n, pieces * width), single),
        shape((groups * n, pieces * width), single),
        shape((groups * n, model), bfloat),
    ] + [shape((groups * n, width), bfloat)] * pieces
    kept += [shape((groups * tok, model), bfloat)] * count
    vm = pl.BlockSpec(memory_space=pltpu.VMEM)
    hbm = pl.BlockSpec(memory_space=pl.ANY)
    flat = [w for ws in weights for w in ws]
    operands = [me, *blocks, *flat, *others]
    in_specs = [pl.BlockSpec(memory_space=pltpu.SMEM)] + [vm] * len(blocks)
    in_specs += [hbm] * (len(flat) + len(others))
    alias = {}
    if carried is not None:
        alias = {len(operands) + i: 1 + i for i in range(len(kept))}
        operands += list(carried)
        in_specs += [hbm] * len(kept)
    out = pl.pallas_call(
        functools.partial(
            expert_kernel,
            len(blocks),
            tok,
            pieces,
            capacity,
            experts,
            group,
            places,
            carried is None,
            len(others),
        ),
        out_shape=[shape((16, 128), bfloat)] + kept,
        in_specs=in_specs,
        out_specs=[vm] + [hbm] * len(kept),
        input_output_aliases=alias,
        scratch_shapes=[pltpu.VMEM((pieces * width, model), bfloat)] * 3
        + [pltpu.VMEM((n, model), bfloat)]
        + [pltpu.VMEM((n, pieces * width), single)] * 2
        + [pltpu.VMEM((n, model), bfloat)]
        + [pltpu.VMEM((n, width), bfloat)] * pieces
        + [pltpu.VMEM((count, tok, model), bfloat)]
        + [pltpu.SemaphoreType.DMA((3, pieces)), pltpu.SemaphoreType.DMA((4 + 2 * count + pieces,))],
        compiler_params=pltpu.CompilerParams(vmem_limit_bytes=56 << 20),
        cost_estimate=pl.CostEstimate(flops=0, bytes_accessed=0, transcendentals=0),
    )(*operands)
    return out[0], out[1:]


def expert_back_kernel(
    arrays, results, tok, pieces, capacity, experts, group, first, waits, *refs
):
    refs = list(refs)
    me_ref = refs.pop(0)
    blocks = views([refs.pop(0) for _ in range(arrays)], tok)
    count = len(blocks)
    all_cots = refs.pop(0)
    weights = [[refs.pop(0) for _ in range(pieces)] for _ in range(3)]
    gate_all, up_all, out_all = (refs.pop(0) for _ in range(3))
    refs = refs[waits:]
    if not first:
        refs = refs[2 + 2 * pieces :]
    backs = views([refs.pop(0) for _ in range(results)], tok)
    grads_all, cot_all = refs.pop(0), refs.pop(0)
    acts = [[refs.pop(0) for _ in range(pieces)] for _ in range(2)]
    full = [refs.pop(0) for _ in range(3)]
    grads, gate_scr, up_scr, out_scr, cot_scr, mark_scr = (refs.pop(0) for _ in range(6))
    act_scr = [[refs.pop(0) for _ in range(pieces)] for _ in range(2)]
    sem_w, sem_i, sem_c, sem_o = refs
    model = grads.shape[1]
    width = weights[0][0].shape[0]
    n = count * capacity
    mine = pl.ds(group * n, n)

    def fetch(src, dst, sem):
        c = pltpu.make_async_copy(src, dst, sem)
        c.start()
        return c

    cots = []
    for i in range(count):
        source = pl.multiple_of(me_ref[1 + group * count + i] * tok, tok)
        cots.append(fetch(all_cots.at[pl.ds(source, tok)], cot_scr.at[i], sem_c.at[0, i]))
        marks = blocks[i][0].at[pl.ds(blocks[i][1], tok), pl.ds(model, 128)]
        cots.append(fetch(marks, mark_scr.at[i], sem_c.at[1, i]))
    loads = {}
    for k in (2, 0, 1):
        loads[k] = [
            fetch(weights[k][j], full[k].at[pl.ds(j * width, width)], sem_w.at[k, j])
            for j in range(pieces)
        ]
    saved = [
        fetch(gate_all.at[mine], gate_scr, sem_i.at[0]),
        fetch(up_all.at[mine], up_scr, sem_i.at[1]),
        fetch(out_all.at[mine], out_scr, sem_i.at[2]),
    ]
    stores = []

    def store(src, dst):
        stores.append(fetch(src, dst, sem_o.at[len(stores)]))

    me = me_ref[0]
    for c in cots:
        c.wait()
    picks = []
    for i in range(count):
        pick, weight, lane = expert_marks(mark_scr[i], me, experts, capacity)
        picks.append(pick)
        scaled = (weight * cot_scr[i].astype(single)).astype(bfloat)
        grads[pl.ds(i * capacity, capacity)] = t_dot(pick, scaled).astype(bfloat)
        store(cot_scr.at[i], cot_all.at[pl.ds((group * count + i) * tok, tok)])
    store(grads, grads_all.at[mine])
    for c in loads[2]:
        c.wait()
    grad_hidden = dot_t(grads[...], full[2][...])
    for c in saved:
        c.wait()
    pre_gate, pre_up = gate_scr[...], up_scr[...]
    sigma = jax.nn.sigmoid(pre_gate)
    grad_gate = grad_hidden * pre_up * sigma * (1.0 + pre_gate * (1.0 - sigma))
    grad_gate = grad_gate.astype(bfloat)
    grad_up = (grad_hidden * pre_gate * sigma).astype(bfloat)
    for k, v in enumerate((grad_gate, grad_up)):
        for j in range(pieces):
            act_scr[k][j][...] = v[:, j * width : (j + 1) * width]
            store(act_scr[k][j], acts[k][j].at[mine])
    for c in loads[0] + loads[1]:
        c.wait()
    back = (dot(grad_gate, full[0][...]) + dot(grad_up, full[1][...])).astype(bfloat)
    for i in range(count):
        here = slice(i * capacity, (i + 1) * capacity)
        got = dot(picks[i], out_scr[here])
        dots = jnp.sum(got * cot_scr[i].astype(single), axis=1, keepdims=True)
        ref, at = backs[i]
        ref[at : at + tok, :model] = dot(picks[i], back[here]).astype(bfloat)
        high = dots.astype(bfloat).astype(single)
        tail = jnp.where(lane == me, high, 0.0) + jnp.where(lane == me + experts, dots - high, 0.0)
        ref[at : at + tok, model : model + 128] = tail.astype(bfloat)
    for c in stores:
        c.wait()


def run_experts_back(
    me, blocks, all_cots, weights, saved, capacity, experts, group, groups, apart, carried, others
):
    pieces, model = len(weights[0]), weights[0][0].shape[1]
    count = saved[0].shape[0] // groups // capacity
    tok = sum(v.shape[0] for v in blocks) // count
    results = [tok] * count if apart else [v.shape[0] for v in blocks]
    width = weights[0][0].shape[0]
    n = count * capacity
    shape = jax.ShapeDtypeStruct
    kept = [shape((groups * n, model), bfloat), shape((groups * count * tok, model), bfloat)]
    kept += [shape((groups * n, width), bfloat)] * (2 * pieces)
    hbm = pl.BlockSpec(memory_space=pl.ANY)
    flat = [w for ws in weights for w in ws]
    operands = [me, *blocks, all_cots, *flat, *saved, *others]
    in_specs = [pl.BlockSpec(memory_space=pltpu.SMEM)] + [hbm] * (len(operands) - 1)
    alias = {}
    if carried is not None:
        alias = {len(operands) + i: len(results) + i for i in range(len(kept))}
        operands += list(carried)
        in_specs += [hbm] * len(kept)
    out = pl.pallas_call(
        functools.partial(
            expert_back_kernel,
            len(blocks),
            len(results),
            tok,
            pieces,
            capacity,
            experts,
            group,
            carried is None,
            len(others),
        ),
        out_shape=[shape((v, model + 128), bfloat) for v in results] + kept,
        in_specs=in_specs,
        out_specs=[pl.BlockSpec(memory_space=pltpu.VMEM)] * len(results) + [hbm] * len(kept),
        input_output_aliases=alias,
        scratch_shapes=[pltpu.VMEM((pieces * width, model), bfloat)] * 3
        + [pltpu.VMEM((n, model), bfloat)]
        + [pltpu.VMEM((n, pieces * width), single)] * 2
        + [
            pltpu.VMEM((n, model), bfloat),
            pltpu.VMEM((count, tok, model), bfloat),
            pltpu.VMEM((count, tok, 128), bfloat),
        ]
        + [pltpu.VMEM((n, width), bfloat)] * (2 * pieces)
        + [
            pltpu.SemaphoreType.DMA((3, pieces)),
            pltpu.SemaphoreType.DMA((3,)),
            pltpu.SemaphoreType.DMA((2, count)),
            pltpu.SemaphoreType.DMA((1 + count + 2 * pieces,)),
        ],
        compiler_params=pltpu.CompilerParams(vmem_limit_bytes=56 << 20),
        cost_estimate=pl.CostEstimate(flops=0, bytes_accessed=0, transcendentals=0),
    )(*operands)
    return out[: len(results)], out[len(results) :]


def shared_kernel(parts, tiles, start, width, first, waits, *refs):
    refs = list(refs)
    xs = [refs.pop(0) for _ in range(parts)]
    cs = [refs.pop(0) for _ in range(parts)]
    weights = [refs.pop(0) for _ in range(3)]
    refs = refs[waits:]
    if not first:
        refs = refs[3:]
    outs = [refs.pop(0) for _ in range(3)]
    wgu, wd = (refs.pop(0) for _ in range(2))
    accs = [refs.pop(0) for _ in range(2)]
    sem_w, sem_o = refs
    step = pl.program_id(0)
    cols = pl.ds(start, width)
    loads = [
        pltpu.make_async_copy(weights[0].at[:, cols], wgu.at[:, pl.ds(0, width)], sem_w.at[0]),
        pltpu.make_async_copy(weights[1].at[:, cols], wgu.at[:, pl.ds(width, width)], sem_w.at[1]),
        pltpu.make_async_copy(weights[2].at[cols], wd, sem_w.at[2]),
    ]

    @pl.when(step == 0)
    def _():
        for c in loads:
            c.start()
        for a in accs:
            a[...] = jnp.zeros_like(a)
        for c in loads:
            c.wait()

    def work(x_ref, c_ref):
        x, c = x_ref[...], c_ref[...]
        pre = dot(x, wgu[...])
        pre_gate, pre_up = pre[:, :width], pre[:, width:]
        grad_hidden = dot_t(c, wd[...])
        sigma = jax.nn.sigmoid(pre_gate)
        silu = pre_gate * sigma
        hidden = (silu * pre_up).astype(bfloat)
        grad_gate = (grad_hidden * pre_up * sigma * (1.0 + pre_gate * (1.0 - sigma))).astype(bfloat)
        grad_up = (grad_hidden * silu).astype(bfloat)
        accs[0][...] += t_dot(x, jnp.concatenate([grad_gate, grad_up], axis=1))
        accs[1][...] += t_dot(hidden, c)

    if parts == 1:
        work(xs[0], cs[0])
    else:
        per = tiles // parts
        for p in range(parts):
            pl.when(step // per == p)(functools.partial(work, xs[p], cs[p]))

    @pl.when(step == tiles - 1)
    def _():
        puts = [
            pltpu.make_async_copy(accs[0].at[:, pl.ds(0, width)], outs[0].at[:, cols], sem_o.at[0]),
            pltpu.make_async_copy(accs[0].at[:, pl.ds(width, width)], outs[1].at[:, cols], sem_o.at[1]),
            pltpu.make_async_copy(accs[1], outs[2].at[cols], sem_o.at[2]),
        ]
        for c in puts:
            c.start()
        for c in puts:
            c.wait()

def run_shared(xs, cs, weights, start, width, carried, others=(), tile=512):
    parts = len(xs)
    rows, model = xs[0].shape
    per = rows // tile
    tiles = per * parts
    shape = jax.ShapeDtypeStruct
    hbm = pl.BlockSpec(memory_space=pl.ANY)
    specs = [
        pl.BlockSpec((tile, model), lambda i, p=p: (jnp.clip(i - p * per, 0, per - 1), 0))
        for p in range(parts)
    ]
    outs = [shape(w.shape, single) for w in weights]
    operands = [*xs, *cs, *weights, *others]
    in_specs = specs + specs + [hbm] * (3 + len(others))
    alias = {}
    if carried is not None:
        alias = {len(operands) + i: i for i in range(3)}
        operands += list(carried)
        in_specs += [hbm] * 3
    return pl.pallas_call(
        functools.partial(shared_kernel, parts, tiles, start, width, carried is None, len(others)),
        grid=(tiles,),
        out_shape=outs,
        in_specs=in_specs,
        out_specs=[hbm] * 3,
        input_output_aliases=alias,
        scratch_shapes=[
            pltpu.VMEM((model, 2 * width), bfloat),
            pltpu.VMEM((width, model), bfloat),
            pltpu.VMEM((model, 2 * width), single),
            pltpu.VMEM((width, model), single),
            pltpu.SemaphoreType.DMA((3,)),
            pltpu.SemaphoreType.DMA((3,)),
        ],
        compiler_params=pltpu.CompilerParams(vmem_limit_bytes=60 << 20),
        cost_estimate=pl.CostEstimate(flops=0, bytes_accessed=0, transcendentals=0),
    )(*operands)


def turned(values, cosine, sine, way):
    half = values.shape[-1] // 2
    first, second = values[:, :half], values[:, half:]
    return jnp.concatenate(
        [first * cosine - way * second * sine, second * cosine + way * first * sine], axis=1
    )


def heads_kernel(pieces, score_scale, *refs):
    refs = list(refs)
    q_ref = refs.pop(0)
    kvbs = [refs.pop(0) for _ in range(pieces)]
    latent, rope, shown, cosine, sine = (refs.pop(0) for _ in range(5))
    heads_ref, nope_ref, qrope_ref, abs_ref, probs_ref, lat_ref = refs
    latents, ropes = latent[...], rope[...]
    visible = shown[...] > 0
    q = q_ref[...]
    rank = latents.shape[1]
    for h in range(2):
        nope = q[:, h * (DN + DR) : h * (DN + DR) + DN].astype(bfloat)
        tail = q[:, h * (DN + DR) + DN : (h + 1) * (DN + DR)]
        qrope = turned(tail, cosine[...], sine[...], 1.0).astype(bfloat)
        at = h * (DN + DV)
        w_uk = jnp.concatenate([w[:, at : at + DN] for w in kvbs], axis=0)
        w_uv = jnp.concatenate([w[:, at + DN : at + DN + DV] for w in kvbs], axis=0)
        query = dot_t(nope, w_uk).astype(bfloat)
        raw = dot_t(query, latents) + dot_t(qrope, ropes)
        scores = jnp.where(visible, raw * score_scale, masked_score)
        expd = jnp.exp(scores - jnp.max(scores, axis=1, keepdims=True))
        probs = expd / jnp.sum(expd, axis=1, keepdims=True)
        lat = dot(probs.astype(bfloat), latents).astype(bfloat)
        heads_ref[:, h * DV : (h + 1) * DV] = dot(lat, w_uv).astype(bfloat)
        nope_ref[:, h * DN : (h + 1) * DN] = nope
        qrope_ref[:, h * DR : (h + 1) * DR] = qrope
        abs_ref[:, h * rank : (h + 1) * rank] = query
        keys = probs.shape[1]
        probs_ref[:, h * keys : (h + 1) * keys] = probs
        lat_ref[:, h * rank : (h + 1) * rank] = lat


def heads_back_kernel(pieces, score_scale, *refs):
    refs = list(refs)
    g_ref = refs.pop(0)
    kvbs = [refs.pop(0) for _ in range(pieces)]
    latent, rope, cosine, sine = (refs.pop(0) for _ in range(4))
    nope_ref, qrope_ref, abs_ref, probs_ref, lat_ref = (refs.pop(0) for _ in range(5))
    gq_ref = refs.pop(0)
    gkvbs = [refs.pop(0) for _ in range(pieces)]
    key_ref, rope_out = refs
    latents, ropes = latent[...], rope[...]
    rank, keys = latents.shape[1], latents.shape[0]

    @pl.when(pl.program_id(0) == 0)
    def _():
        key_ref[...] = jnp.zeros_like(key_ref)
        rope_out[...] = jnp.zeros_like(rope_out)

    parts = []
    key_sum = key_ref[...]
    rope_sum = rope_out[...]
    for h in range(2):
        at = h * (DN + DV)
        w_uk = jnp.concatenate([w[:, at : at + DN] for w in kvbs], axis=0)
        w_uv = jnp.concatenate([w[:, at + DN : at + DN + DV] for w in kvbs], axis=0)
        grad = g_ref[:, h * DV : (h + 1) * DV]
        lat = lat_ref[:, h * rank : (h + 1) * rank]
        query = abs_ref[:, h * rank : (h + 1) * rank]
        nope = nope_ref[:, h * DN : (h + 1) * DN]
        qrope = qrope_ref[:, h * DR : (h + 1) * DR]
        probs = probs_ref[:, h * keys : (h + 1) * keys]
        grad_uv = t_dot(lat, grad).astype(bfloat)
        grad_lat = dot_t(grad, w_uv).astype(bfloat)
        grad_probs = dot_t(grad_lat, latents)
        delta = jnp.sum(probs * grad_probs, axis=1, keepdims=True)
        grad_scores = (probs * (grad_probs - delta)).astype(bfloat)
        grad_abs = (dot(grad_scores, latents) * score_scale).astype(bfloat)
        grad_rope = dot(grad_scores, ropes) * score_scale
        key_sum = key_sum + t_dot(grad_scores, query) * score_scale
        key_sum = key_sum + t_dot(probs.astype(bfloat), grad_lat)
        rope_sum = rope_sum + t_dot(grad_scores, qrope) * score_scale
        grad_uk = t_dot(grad_abs, nope).astype(bfloat)
        rows = rank // pieces
        for j in range(pieces):
            gkvbs[j][:, at : at + DN] = grad_uk[j * rows : (j + 1) * rows]
            gkvbs[j][:, at + DN : at + DN + DV] = grad_uv[j * rows : (j + 1) * rows]
        parts.append(dot(grad_abs, w_uk))
        parts.append(turned(grad_rope, cosine[...], sine[...], -1.0))
    gq_ref[...] = jnp.concatenate(parts, axis=1).astype(bfloat)
    key_ref[...] = key_sum
    rope_out[...] = rope_sum


def run_heads(q, kvbs, latent, rope, shown, cosine, sine, heads, score_scale):
    rows, pieces = q.shape[0], len(kvbs)
    keys, rank = latent.shape
    shape = jax.ShapeDtypeStruct
    own = lambda width: pl.BlockSpec((rows, width), lambda g: (0, g))
    still = lambda v: pl.BlockSpec(v.shape, lambda g: (0, 0))
    kvb = [pl.BlockSpec((w.shape[0], 2 * (DN + DV)), lambda g: (0, g)) for w in kvbs]
    widths = (DV, DN, DR, rank, keys, rank)
    kinds = (bfloat, bfloat, bfloat, bfloat, single, bfloat)
    return pl.pallas_call(
        functools.partial(heads_kernel, pieces, score_scale),
        grid=(heads // 2,),
        out_shape=[shape((rows, heads * w), k) for w, k in zip(widths, kinds)],
        in_specs=[own(2 * (DN + DR)), *kvb] + [still(v) for v in (latent, rope, shown, cosine, sine)],
        out_specs=[own(2 * w) for w in widths],
        compiler_params=pltpu.CompilerParams(vmem_limit_bytes=40 << 20),
        cost_estimate=pl.CostEstimate(flops=0, bytes_accessed=0, transcendentals=0),
    )(q, *kvbs, latent, rope, shown, cosine, sine)


def run_heads_back(grad, kvbs, latent, rope, cosine, sine, saved, heads, score_scale, others):
    rows, pieces = grad.shape[0], len(kvbs)
    keys, rank = latent.shape
    shape = jax.ShapeDtypeStruct
    own = lambda width: pl.BlockSpec((rows, width), lambda g: (0, g))
    still = lambda v: pl.BlockSpec(v.shape, lambda g: (0, 0))
    kvb = [pl.BlockSpec((w.shape[0], 2 * (DN + DV)), lambda g: (0, g)) for w in kvbs]
    widths = (DN, DR, rank, keys, rank)

    def body(*refs):
        cut = 1 + pieces + 4 + 5
        heads_back_kernel(pieces, score_scale, *refs[:cut], *refs[cut + len(others) :])

    out = pl.pallas_call(
        body,
        grid=(heads // 2,),
        out_shape=[shape((rows, heads * (DN + DR)), bfloat)]
        + [shape(w.shape, bfloat) for w in kvbs]
        + [shape((keys, rank), single), shape((keys, DR), single)],
        in_specs=[own(2 * DV), *kvb]
        + [still(v) for v in (latent, rope, cosine, sine)]
        + [own(2 * w) for w in widths]
        + [pl.BlockSpec(memory_space=pl.ANY)] * len(others),
        out_specs=[own(2 * (DN + DR)), *kvb]
        + [pl.BlockSpec((keys, rank), lambda g: (0, 0)), pl.BlockSpec((keys, DR), lambda g: (0, 0))],
        compiler_params=pltpu.CompilerParams(vmem_limit_bytes=40 << 20),
        cost_estimate=pl.CostEstimate(flops=0, bytes_accessed=0, transcendentals=0),
    )(grad, *kvbs, latent, rope, cosine, sine, *saved, *others)
    return out[0], out[1 : 1 + pieces], out[1 + pieces], out[2 + pieces]


def assemble_kernel(parts, cuts, fold, *refs):
    where, one_0, one_1, two_0, two_1, *outs = refs
    step = pl.program_id(0)
    _, m = parts
    row = jnp.where(step // m == where[0], one_0[...], one_1[...])
    column = jnp.where(step % m == where[1], two_0[...], two_1[...])
    value = jnp.concatenate([row, column], axis=1).astype(single)
    start = 0
    for i, (width, out) in enumerate(zip(cuts, outs)):
        piece = value[:, start : start + width]
        start += width
        if i == 0 and fold > 1:
            rows = piece.shape[0] // fold
            piece = jnp.concatenate(
                [piece[k * rows : (k + 1) * rows] for k in range(fold)], axis=1
            )
        if out.shape[0] == width and out.shape[0] != piece.shape[0]:
            piece = piece.T
        out[...] = piece


def assemble(chips, lines, cuts, fold, turned):
    n, m = chips.dims[1:]
    parts = n * m
    rows = lines[0][0].shape[0] * n // parts
    where = jnp.stack([chips.own(1), chips.own(2)]).astype(jnp.int32)
    one = pl.BlockSpec((rows, lines[0][0].shape[1]), lambda p: (p % m, 0))
    two = pl.BlockSpec((rows, lines[1][0].shape[1]), lambda p: (p // m, 0))
    shapes, specs = [], []
    for i, width in enumerate(cuts):
        if i == 0 and fold > 1:
            shapes.append((rows * parts // fold, width * fold))
            specs.append(pl.BlockSpec((rows // fold, width * fold), lambda p: (p, 0)))
        elif i in turned:
            shapes.append((width, rows * parts))
            specs.append(pl.BlockSpec((width, rows), lambda p: (0, p)))
        else:
            shapes.append((rows * parts, width))
            specs.append(pl.BlockSpec((rows, width), lambda p: (p, 0)))
    return pl.pallas_call(
        functools.partial(assemble_kernel, (n, m), cuts, fold),
        grid=(parts,),
        out_shape=[jax.ShapeDtypeStruct(v, single) for v in shapes],
        in_specs=[pl.BlockSpec(memory_space=pltpu.SMEM), one, one, two, two],
        out_specs=specs,
        compiler_params=pltpu.CompilerParams(vmem_limit_bytes=56 << 20),
        cost_estimate=pl.CostEstimate(flops=0, bytes_accessed=0, transcendentals=0),
    )(where, *lines[0], *lines[1])


def plane_kernel(count, rows, start, widths, fold, *refs):
    refs = list(refs)
    lefts = [refs.pop(0) for _ in range(count)]
    rights = [[refs.pop(0) for _ in range(rows)] for _ in widths]
    extra = refs[:-1]
    out = refs[-1]
    tok = lefts[0].shape[0] // rows
    cols = out.shape[0]
    at = 0
    if extra:
        kvb, small = extra
        size = kvb.shape[1] // fold
        for k in range(fold):
            here = pl.ds(k * kvb.shape[0], kvb.shape[0])
            out[here, :size] = kvb[:, k * size : (k + 1) * size]
        at = size
    for width, parts in zip(widths, rights):
        total = None
        for c in range(rows):
            for o in range(count):
                left = lefts[o][c * tok : (c + 1) * tok, start : start + cols]
                term = t_dot(left, parts[c][o * tok : (o + 1) * tok, :width])
                total = term if total is None else total + term
        value = total.astype(bfloat)
        if extra:
            value = jnp.concatenate([value, small[...]], axis=1)
        out[:, at : at + value.shape[1]] = value
        at += value.shape[1]


def plane_dot(lefts, start, cols, rights, widths, fold=1, extra=()):
    total = sum(widths)
    if extra:
        total += extra[0].shape[1] // fold + extra[1].shape[1]
    flat = [v for parts in rights for v in parts]
    vm = pl.BlockSpec(memory_space=pltpu.VMEM)
    return pl.pallas_call(
        functools.partial(plane_kernel, len(lefts), len(rights[0]), start, widths, fold),
        out_shape=jax.ShapeDtypeStruct((cols, total), bfloat),
        in_specs=[vm] * (len(lefts) + len(flat) + len(extra)),
        out_specs=vm,
        compiler_params=pltpu.CompilerParams(vmem_limit_bytes=48 << 20),
        cost_estimate=pl.CostEstimate(flops=0, bytes_accessed=0, transcendentals=0),
    )(*lefts, *flat, *extra)


def rows_kernel(value, out):
    lines, rows = value.shape[0], value.shape[2]
    for i in range(lines):
        out[i * rows : (i + 1) * rows] = value[i, 0].astype(single)


def in_rows(chips, value):
    lines, parts = chips.dims[0], chips.plane
    rows = value.shape[0] // (lines * parts)
    value = value.reshape(lines, parts, rows, -1)
    if rows % 16:
        return value.swapaxes(0, 1).reshape(lines * parts * rows, -1).astype(single)
    width = value.shape[3]
    return pl.pallas_call(
        rows_kernel,
        grid=(parts,),
        out_shape=jax.ShapeDtypeStruct((lines * parts * rows, width), single),
        in_specs=[pl.BlockSpec((lines, 1, rows, width), lambda p: (0, p, 0, 0))],
        out_specs=pl.BlockSpec((lines * rows, width), lambda p: (p, 0)),
        compiler_params=pltpu.CompilerParams(vmem_limit_bytes=48 << 20),
        cost_estimate=pl.CostEstimate(flops=0, bytes_accessed=0, transcendentals=0),
    )(value)


def widths_of(total):
    if total % 128:
        return [total]
    out = []
    while total > 0:
        out.append(min(384, total))
        total -= out[-1]
    return out


def tie(value, *others):
    hbm = pl.BlockSpec(memory_space=pl.ANY)
    return pl.pallas_call(
        lambda *refs: None,
        out_shape=jax.ShapeDtypeStruct(value.shape, value.dtype),
        in_specs=[hbm] * (1 + len(others)),
        out_specs=hbm,
        input_output_aliases={0: 0},
    )(value, *others)


def grid_of(experts, shards):
    if shards == 2 and experts % 4 == 0:
        return (experts // 4, 2, 2)
    side = math.isqrt(experts)
    return (side, side) if side * side == experts else (experts,)


class Chips:
    def __init__(self, dims, names):
        self.dims = dims
        self.names = names
        self.size = int(np.prod(dims))
        self.plane = self.size // dims[0]
        self.places = [tuple(int(v) for v in np.unravel_index(i, dims)) for i in range(self.size)]
        self.offsets = [
            tuple(int(v) for v in np.unravel_index(i, dims[1:])) for i in range(self.plane)
        ]

    def index(self, place):
        return int(np.ravel_multi_index(place, self.dims))

    def own(self, axis):
        return lax.axis_index(self.names[axis])

    def me(self):
        return lax.axis_index(self.names)

    def pairs(self, axis_of, by):
        out = []
        for i, place in enumerate(self.places):
            axis = axis_of(place)
            to = list(place)
            to[axis] = (to[axis] + by) % self.dims[axis]
            out.append((i, self.index(to)))
        return out

    def along(self, value, axis, by):
        n = self.dims[axis]
        return lax.ppermute(value, self.names[axis], [(i, (i + by) % n) for i in range(n)])

    def offset_by(self, value, offset):
        out = []
        for i, place in enumerate(self.places):
            to = [place[0]] + [
                (p + o) % d for p, o, d in zip(place[1:], offset, self.dims[1:])
            ]
            out.append((i, self.index(to)))
        return lax.ppermute(value, self.names, out)

    def first(self, block):
        return [block] + [self.along(block, 0, j) for j in range(1, self.dims[0])]

    def axes(self, j):
        if len(self.dims) < 3:
            return (0, len(self.dims) - 1)
        return (1, 2) if j % 2 == 0 else (2, 1)

    def hop_one(self, block, j):
        axis, _ = self.axes(j)
        return self.hop_line(block, axis) if axis else [block]

    def hop_two(self, blocks, j):
        _, axis = self.axes(j)
        both = jnp.concatenate(blocks, axis=0) if len(blocks) > 1 else blocks[0]
        return self.hop_line(both, axis) if axis else [both]

    def places_of(self, j):
        one, two = self.axes(j)
        if not one:
            return list(range(self.plane))
        out = []
        for t in range(self.dims[two]):
            for h in range(self.dims[one]):
                out.append(self.offsets.index((h, t) if one == 1 else (t, h)))
        return out

    def hop_line(self, block, axis):
        return [block] + [self.along(block, axis, s) for s in range(1, self.dims[axis])]

    def straight(self, block):
        return [self.offset_by(block, o) if any(o) else block for o in self.offsets]

    def straight_back(self, blocks):
        return [
            self.offset_by(b, [-v for v in o]) if any(o) else b
            for b, o in zip(blocks, self.offsets)
        ]

    def pack_of(self, j, p):
        if len(self.dims) != 3:
            return (p, j)
        half = self.dims[0] // 2
        y, x = self.offsets[p]
        part, rest = (x, y) if j < half else (y, x)
        return (j // half * 2 + part, rest * half + j % half)

    def packs_one(self, packs):
        if len(self.dims) != 3:
            return [self.straight_back(packs)]
        return [
            [packs[0], self.along(packs[1], 2, -1)],
            [packs[2], self.along(packs[3], 1, -1)],
        ]

    def packs_two(self, totals):
        if len(self.dims) != 3:
            return [[v] for v in totals]
        out = []
        for v, axis in zip(totals, (1, 2)):
            rows = v.shape[0] // 2
            out.append([v[:rows], self.along(v[rows:], axis, -1)])
        return out

    def sources(self, at_once):
        table = []
        for place in self.places:
            row = []
            for j in range(self.dims[0]):
                for p in range(self.plane) if j in at_once else self.places_of(j):
                    offset = (j, *self.offsets[p])
                    row.append(self.index([(q - o) % d for q, o, d in zip(place, offset, self.dims)]))
            table.append(row)
        return jnp.asarray(np.array(table, np.int32))[self.me()]

    def back_first(self, total, j):
        return self.along(total.astype(bfloat), 0, -j) if j else total

    def own_part(self):
        part = 0
        for axis in range(1, len(self.dims)):
            part = part * self.dims[axis] + self.own(axis)
        return part

    def swap_columns(self, *values):
        out = []
        for offset in self.offsets:
            part = 0
            for axis, by in enumerate(offset):
                n = self.dims[axis + 1]
                part = part * n + (self.own(axis + 1) + by) % n
            pieces = []
            for v in values:
                size = v.shape[1] // self.plane
                pieces.append(lax.dynamic_slice_in_dim(v, part * size, size, 1))
            piece = jnp.concatenate(pieces, axis=1)
            out.append(self.offset_by(piece, offset) if any(offset) else piece)
        return out

    def orders(self):
        return ((2, 1), (1, 2)) if len(self.dims) == 3 else ((1,),)

    def halves(self, value):
        if len(self.dims) != 3:
            return [value]
        cut = value.shape[1] // 256 * 128
        return [value[:, :cut], value[:, cut:]]

    def stack_one(self, value):
        return [self.hop_line(v, o[0]) for v, o in zip(self.halves(value), self.orders())]

    def stack_two(self, lines, mark):
        out = []
        for line, order in zip(lines, self.orders()):
            both = jnp.concatenate(hold(line, mark), axis=0)
            out.append(self.hop_line(both, order[1]) if len(order) > 1 else [both])
        return out

    def stack_done(self, lines, mark):
        out = []
        for line, order in zip(lines, self.orders()):
            line = hold(line, mark)
            if order == (1, 2):
                n = self.dims[1]
                rows = line[0].shape[0] // n
                line = [v[s * rows : (s + 1) * rows] for s in range(n) for v in line]
            out.append(jnp.concatenate(line, axis=0))
        return out

    def send_rows(self, value):
        size = value.shape[0] // self.plane
        out = []
        for offset in self.offsets:
            part = 0
            for axis, by in enumerate(offset):
                n = self.dims[axis + 1]
                part = part * n + (self.own(axis + 1) + by) % n
            piece = lax.dynamic_slice_in_dim(value, part * size, size, 0)
            out.append(self.offset_by(piece, offset) if any(offset) else piece)
        return out

    def line_send(self, value):
        n = self.dims[0]
        rows = value.shape[0] // n
        own = self.own(0)
        out = [lax.dynamic_slice_in_dim(value, own * rows, rows, 0)]
        for j in range(1, n):
            piece = lax.dynamic_slice_in_dim(value, ((own + j) % n) * rows, rows, 0)
            out.append(self.along(piece, 0, j))
        return out

    def gather_one(self, halves):
        return [self.hop_line(v, o[0]) for v, o in zip(halves, self.orders())]

    def gather_two(self, lines, mark):
        out = []
        for line, order in zip(lines, self.orders()):
            line = hold(line, mark)
            own = self.own(order[0])
            if len(order) == 1:
                out.append([in_order(line, own, 0)])
            else:
                both = in_order(line, own, 0)
                out.append(self.hop_line(both, order[1]))
        return out

    def gather_done(self, lines, mark):
        out = []
        for line, order in zip(lines, self.orders()):
            line = hold(line, mark)
            if len(order) == 1:
                out.append(line[0])
            elif order == (1, 2):
                n = self.dims[1]
                rows = line[0].shape[0] // n
                cut = [[v[i * rows : (i + 1) * rows] for v in line] for i in range(n)]
                out += [jnp.concatenate([in_order(v, self.own(2), 0) for v in cut], axis=0)]
            else:
                out.append(in_order(line, self.own(order[1]), 0))
        return jnp.concatenate(out, axis=1)


def hold(values, *others):
    return [values[0]] + [tie(v, *others) for v in values[1:]]


def visit(mark, lines, singles=()):
    lines = [[v[0]] + [tie(x, mark) for x in v[1:]] for v in lines]
    singles = [tie(v, mark) for v in singles]
    mark = tie(lines[0][0], mark, *[x for v in lines for x in v[1:]], *singles)
    lines = [[mark] + lines[0][1:]] + [[tie(v[0], mark)] + v[1:] for v in lines[1:]]
    return mark, lines, [tie(v, mark) for v in singles]


def add_up(values):
    return sum([v.astype(single) for v in values[1:]], values[0].astype(single)).astype(bfloat)


def split(value, widths):
    out, start = [], 0
    for width in widths:
        out.append(value[:, start : start + width])
        start += width
    return out


def in_order(pieces, own, axis):
    n = len(pieces)
    if n == 1:
        return pieces[0]
    if n == 2:
        return jnp.where(
            own == 0,
            jnp.concatenate(pieces, axis=axis),
            jnp.concatenate([pieces[1], pieces[0]], axis=axis),
        )
    turned = pieces[::-1]
    line = jnp.concatenate(turned + turned[:-1], axis=axis)
    extent = pieces[0].shape[axis]
    return lax.dynamic_slice_in_dim(line, (n - 1 - own) * extent, n * extent, axis)


class Cores:
    def __init__(self, count):
        self.count = count
        self.own = lax.axis_index("shard")

    def along(self, value, by):
        n = self.count
        return lax.ppermute(value, "shard", [(i, (i + by) % n) for i in range(n)])

    def spread(self, value):
        return [value] + [self.along(value, j) for j in range(1, self.count)]

    def whole(self, value, axis):
        return in_order(self.spread(value), self.own, axis)

    def chunk(self, value, j, axis):
        size = value.shape[axis] // self.count
        place = (self.own + j + self.count) % self.count
        return lax.dynamic_slice_in_dim(value, place * size, size, axis)

    def rows_times(self, left, pieces):
        out = None
        for j, piece in enumerate(pieces):
            term = dot(self.chunk(left, -j, 1), piece)
            out = term if out is None else out + term
        return out

    def times_rows_t(self, left, pieces):
        return in_order([dot_t(left, piece) for piece in pieces], self.own, 1)

    def swap_columns(self, *values):
        out = []
        for j in range(self.count):
            piece = jnp.concatenate([self.chunk(v, j, 1) for v in values], axis=1)
            out.append(self.along(piece, j) if j else piece)
        return split(jnp.concatenate(out, axis=0), [v.shape[1] // self.count for v in values])

    def stack(self, value):
        return jnp.concatenate(self.spread(value), axis=0)

    def give_back(self, value):
        rows = value.shape[0] // self.count
        total = value[:rows]
        for j in range(1, self.count):
            total = total + self.along(value[j * rows : (j + 1) * rows], -j)
        return total

    def scatter(self, value, axis):
        total = self.chunk(value, 0, axis).astype(single)
        for j in range(1, self.count):
            total = total + self.along(self.chunk(value, j, axis).astype(bfloat), j).astype(single)
        return total


def per_device(
    chips,
    shards,
    tokens,
    segment_ids,
    routes,
    cotangent,
    gain_attn,
    gain_query,
    gain_latent,
    gain_ffn,
    w_qa,
    w_qb,
    w_kva,
    w_kvb,
    w_out,
    w_router,
    shared_gate,
    shared_up,
    shared_down,
    expert_gate,
    expert_up,
    expert_down,
):
    cores = Cores(shards)
    me = chips.me()
    shard_pos = cores.own
    tok_rows = tokens.shape[0]
    model = tokens.shape[1]
    group_rows = tok_rows * shards
    score_scale = 1.0 / (DN + DR) ** 0.5
    query_rank = w_qa.shape[1]

    gains = jnp.concatenate([gain_attn, gain_query, gain_latent, gain_ffn])
    gain_pieces = cores.spread(gains)
    sizes = [v.shape[0] for v in (gain_attn, gain_query, gain_latent, gain_ffn)]
    full_gains = []
    start = 0
    for size in sizes:
        full_gains.append(
            in_order([g[start : start + size] for g in gain_pieces], shard_pos, 0).astype(single)
        )
        start += size
    gain_attn_f, gain_query_f, gain_latent_f, gain_ffn_f = full_gains
    qa_pieces = cores.spread(w_qa)
    kva_pieces = cores.spread(w_kva)
    qb_pieces = cores.spread(w_qb)
    kvb_pieces = cores.spread(w_kvb)
    out_pieces = cores.spread(w_out)
    router_full = cores.whole(w_router, 0)
    expert_weights = [
        cores.spread(expert_gate[0].T),
        cores.spread(expert_up[0].T),
        cores.spread(expert_down[0]),
    ]
    turns = chips.dims[0]
    order = [0] + list(range(1, turns, 2)) + list(range(2, turns, 2))
    order_back = [0] + list(range(2, turns, 2)) + list(range(1, turns, 2))
    all_cots = lax.all_gather(cotangent, chips.names, axis=0, tiled=True)

    resid = tokens.astype(single)
    attn_scale = row_scale(resid)
    attn_normed = resid * attn_scale
    attn_in = (attn_normed * gain_attn_f).astype(bfloat)
    query_lat = cores.rows_times(attn_in, qa_pieces)
    query_scale = row_scale(query_lat)
    query_normed = query_lat * query_scale
    query_in = (query_normed * gain_query_f).astype(bfloat)
    query_all = cores.rows_times(query_in, qb_pieces)
    group_pos = seq_positions(segment_ids)
    own_start = shard_pos * tok_rows
    own_pos = lax.dynamic_slice_in_dim(group_pos, own_start, tok_rows, 0)
    own_seg = lax.dynamic_slice_in_dim(segment_ids, own_start, tok_rows, 0)
    cosine, sine = rope_tables(own_pos, DR // 2)
    latent_raw = cores.rows_times(attn_in, kva_pieces)
    latent_part = latent_raw[:, :KR]
    latent_scale = row_scale(latent_part)
    latent_normed = latent_part * latent_scale
    latent = (latent_normed * gain_latent_f).astype(bfloat)
    key_rope = rotate(latent_raw[:, KR:], cosine, sine).astype(bfloat)
    keys = cores.whole(jnp.concatenate([latent, key_rope], axis=1), 0)
    keys_latent, keys_rope = keys[:, :KR], keys[:, KR:]
    keys_turned = jnp.concatenate(
        [cores.chunk(keys_latent, -j, 1) for j in range(shards)], axis=1
    )
    group_index = jnp.arange(group_rows, dtype=jnp.int32)
    own_index = own_start + jnp.arange(tok_rows, dtype=jnp.int32)
    visible = (own_seg[:, None] == segment_ids[None, :]) & (
        group_index[None, :] <= own_index[:, None]
    )

    attn_heads, *saved = run_heads(
        query_all,
        kvb_pieces,
        keys_turned,
        keys_rope,
        visible.astype(single),
        cosine,
        sine,
        H,
        score_scale,
    )
    mid = resid + cores.rows_times(attn_heads, out_pieces)
    ffn_scale = row_scale(mid)
    ffn_normed = mid * ffn_scale
    ffn_in = (ffn_normed * gain_ffn_f).astype(bfloat)

    experts_all = router_full.shape[1]
    lanes = -(-4 * experts_all // 128) * 128
    logits = dot(ffn_in, router_full)
    chosen = jnp.sum(
        (routes[:, :, None] == jnp.arange(experts_all, dtype=jnp.int32)[None, None, :]).astype(
            single
        ),
        axis=1,
    )
    sig = jax.nn.sigmoid(logits)
    denom = jnp.sum(chosen * sig, axis=-1, keepdims=True)
    routing_weights = route_scale * chosen * sig / denom
    capacity = min(tok_rows, 4 * tok_rows * TOP // (3 * experts_all))
    earlier = (jnp.arange(tok_rows)[:, None] > jnp.arange(tok_rows)[None, :]).astype(bfloat)
    slot = dot(earlier, chosen.astype(bfloat))
    code = jnp.where(chosen > 0, slot, -1.0)
    weight_high = routing_weights.astype(bfloat)
    weight_rest = (routing_weights - weight_high.astype(single)).astype(bfloat)
    marks = jnp.concatenate(
        [
            code.astype(bfloat),
            weight_high,
            weight_rest,
            jnp.zeros((tok_rows, lanes - 3 * experts_all), bfloat),
        ],
        axis=1,
    )
    payload = jnp.concatenate([ffn_in, marks], axis=1)
    first = chips.first(payload)
    one, two = [None] * turns, [None] * turns
    two[0] = chips.straight(payload)

    stack_ffn = cores.stack(ffn_in)
    stack_cot = cores.stack(cotangent)

    def feed_forward(rows, grads, gate, up, down):
        pre_gate = dot(rows, gate)
        pre_up = dot(rows, up)
        hidden = (jax.nn.silu(pre_gate) * pre_up).astype(bfloat)
        grad_gate, grad_up = silu_grads(dot_t(grads, down), pre_gate, pre_up)
        return hidden, grad_gate, grad_up

    sh_hidden, sh_gate, sh_up = feed_forward(
        stack_ffn, stack_cot, shared_gate, shared_up, shared_down
    )
    sh_back = dot_t(sh_gate, shared_gate) + dot_t(sh_up, shared_up)
    shared_out = cores.give_back(dot(sh_hidden, shared_down))
    shared_back = cores.give_back(sh_back)

    at_once = order[:2]
    who = jnp.concatenate([me.astype(jnp.int32).reshape(1), chips.sources(at_once)])
    kept, kept_back = None, None
    sent, grads_of = [], []

    def parts_of(i):
        if i == 2:
            return kept[5 : 5 + shards], kept_back[0]
        return kept_back[2 + i * shards : 2 + (i + 1) * shards], kept[0]

    def others_part(i, waits):
        left, right = parts_of(i)
        out = [t_dot(tie(v, *waits), right).astype(bfloat) for v in left[1:]]
        sent.append([cores.along(v, -j - 1) for j, v in enumerate(out)])
        return out[-1]

    def own_part(i, waits):
        left, right = parts_of(i)
        got = [tie(v, *waits).astype(single) for v in sent[i]]
        grads_of.append(sum(got, t_dot(tie(left[0], *waits), right)))
        return grads_of[-1]

    fillers = [
        lambda waits: others_part(1, [others_part(0, waits)]),
        lambda waits: others_part(2, waits),
        lambda waits: own_part(1, waits),
    ]
    mark = sh_back
    backs = [None] * turns

    def places_of(j):
        return list(range(chips.plane)) if j in at_once else chips.places_of(j)

    def forward_step(step):
        nonlocal kept, mark
        waits = [mark]
        if step + 1 < turns:
            k = order[step + 1]
            if k in at_once:
                first[k] = tie(first[k], mark)
                two[k] = chips.straight(first[k])
                waits.append(first[k])
            else:
                one[k] = hold(one[k], mark)
                two[k] = chips.hop_two(one[k], k)
                waits.append(one[k][0])
        if step + 2 < turns:
            k = order[step + 2]
            first[k] = tie(first[k], mark)
            one[k] = chips.hop_one(first[k], k)
            waits.append(first[k])
        j = order[step]
        mark, kept = run_experts(
            who,
            two[j],
            expert_weights,
            capacity,
            experts_all,
            j,
            turns,
            [chips.pack_of(j, p) for p in places_of(j)],
            kept,
            waits,
        )

    def backward_step(step):
        nonlocal kept_back, mark
        waits = [mark]
        if 2 <= step:
            k = order_back[step - 2]
            total = add_up(hold(backs[k], mark))
            backs[k] = chips.back_first(total, k)
            waits.append(total)
        if step >= turns:
            mark = fillers[step - turns](waits)
            return
        j = order_back[step]
        back_blocks, kept_back = run_experts_back(
            who,
            two[j],
            all_cots,
            expert_weights,
            kept[2:5],
            capacity,
            experts_all,
            j,
            turns,
            True,
            kept_back,
            waits,
        )
        places = places_of(j)
        back_blocks = [back_blocks[places.index(p)] for p in range(chips.plane)]
        backs[j] = chips.straight_back(back_blocks)
        mark = back_blocks[0]

    ahead = min(2, turns)
    for step in range(ahead):
        forward_step(step)
    backward_step(0)
    for step in range(ahead, turns):
        forward_step(step)
    for step in range(1, turns + 2):
        backward_step(step)
    out_packs = kept[5 + shards :]
    routed_back = backs[0].astype(single)
    for j in order[1:]:
        routed_back = routed_back + tie(backs[j], mark).astype(single)
    chip_ffn, chip_cot = kept[1], kept_back[1]

    grad_out = cotangent.astype(single)
    grad_weights = (
        routed_back[:, model : model + experts_all]
        + routed_back[:, model + experts_all : model + 2 * experts_all]
    )
    grad_sig = chosen * (
        route_scale * grad_weights / denom
        - jnp.sum(grad_weights * routing_weights, axis=-1, keepdims=True) / denom
    )
    grad_logits = grad_sig * sig * (1.0 - sig)
    grad_router = jnp.einsum("te,td->ed", grad_logits, ffn_in.astype(single), precision=highest)
    grad_ffn_in = (
        routed_back[:, :model]
        + shared_back
        + jnp.einsum("te,de->td", grad_logits, router_full.astype(single), precision=highest)
    )
    grad_mid, grad_gffn = norm_back(grad_ffn_in, ffn_normed, ffn_scale, gain_ffn_f)
    grad_mid = grad_mid + grad_out

    grad_attn_out = grad_mid.astype(bfloat)
    heads_line = chips.stack_one(grad_attn_out)
    lefts = cores.swap_columns(attn_in, query_in, tie(attn_heads, sh_back))
    lefts = chips.swap_columns(*[tie(v, mark) for v in lefts])
    sent[:] = [[tie(v, grad_attn_out) for v in line] for line in sent]
    grad_attn_out = tie(grad_attn_out, *[v for line in sent for v in line])
    grad_heads = cores.times_rows_t(grad_attn_out, out_pieces).astype(bfloat)
    heads_line = chips.stack_two(heads_line, grad_heads)
    grad_query, kvb_parts, key_terms, rope_terms = run_heads_back(
        grad_heads,
        kvb_pieces,
        keys_turned,
        keys_rope,
        cosine,
        sine,
        saved,
        H,
        score_scale,
        [v[0] for v in heads_line],
    )
    mark = own_part(0, [grad_query])
    heads_line = [hold(v, mark) for v in heads_line]
    lefts = hold(lefts, mark)
    there = [v for line in [*heads_line, lefts] for v in line[1:]]
    grad_query = tie(grad_query, *there)
    heads_all = [cores.spread(v) for v in chips.stack_done(heads_line, grad_query)]
    query_line = chips.stack_one(grad_query)
    kvb_terms = add_up(
        [kvb_parts[0]] + [cores.along(v, -j - 1) for j, v in enumerate(kvb_parts[1:])]
    )
    kvb_part = lax.psum_scatter(kvb_terms, chips.names[1:], scatter_dimension=0, tiled=True)
    size = KR // shards
    key_terms = in_order(
        [key_terms[:, j * size : (j + 1) * size] for j in range(shards)], shard_pos, 1
    )
    grad_keys = cores.scatter(jnp.concatenate([key_terms, rope_terms], axis=1), 0)
    grad_latent, grad_krope = grad_keys[:, :KR], grad_keys[:, KR:]
    grad_query_in = cores.times_rows_t(grad_query, qb_pieces)
    grad_qlat, grad_gquery = norm_back(grad_query_in, query_normed, query_scale, gain_query_f)
    grad_kvpart, grad_glatent = norm_back(grad_latent, latent_normed, latent_scale, gain_latent_f)
    grad_kvrope = rotate_back(grad_krope, cosine, sine)
    grad_low = jnp.concatenate([grad_qlat, grad_kvpart, grad_kvrope], axis=-1).astype(bfloat)
    shared_weights = (shared_gate, shared_up, shared_down)
    xs, cs = cores.spread(tie(chip_ffn, routed_back)), cores.spread(tie(chip_cot, routed_back))
    widths = widths_of(shared_gate.shape[1]) if shards == 2 else []
    shared_grads = None
    start = 0

    def shared_step(waits):
        nonlocal shared_grads, start
        if not widths:
            return waits[0]
        width = widths.pop(0)
        shared_grads = run_shared(xs, cs, shared_weights, start, width, shared_grads, waits)
        start += width
        return shared_grads[0]

    low_wide = jnp.pad(grad_low, ((0, 0), (0, -grad_low.shape[1] % 128)))
    low_line = chips.straight(low_wide)
    mark = fillers[2]([grad_low, kvb_terms, *[v[0] for v in query_line]])
    query_line = chips.stack_two(query_line, mark)
    sizes = [v.shape[1] // (shards * chips.plane) for v in (attn_in, query_in, attn_heads)]
    part = plane_dot(
        lefts, sizes[0] + sizes[1], sizes[2], heads_all, [v[0].shape[1] for v in heads_all]
    )
    part_sums = lax.psum_scatter(part, chips.names[0], scatter_dimension=0, tiled=True)
    mark = shared_step([part, low_line[0]] + [v[0] for v in query_line])
    mark, lines, (part_sums, kvb_part) = visit(
        mark, [low_line, *query_line], [part_sums, kvb_part]
    )
    low_line, *query_line = lines
    part_all = lax.all_gather(part_sums, chips.names, axis=0, tiled=True)
    mark = tie(grad_low, mark)
    grad_low = mark
    grad_attn_in = in_order(
        [
            dot_t(grad_low[:, :query_rank], qa) + dot_t(grad_low[:, query_rank:], kva)
            for qa, kva in zip(qa_pieces, kva_pieces)
        ],
        shard_pos,
        1,
    )
    grad_resid, grad_gattn = norm_back(grad_attn_in, attn_normed, attn_scale, gain_attn_f)
    grad_tokens = grad_mid + grad_resid
    mixed = jnp.concatenate(
        [grad_gquery.reshape(shards, -1), grad_glatent.reshape(shards, -1)], axis=1
    ).reshape(-1)
    small = jnp.concatenate(
        [grad_gattn[None], grad_gffn[None], mixed[None], grad_router], axis=0
    )
    small_line = chips.send_rows(cores.scatter(small, 1).T.astype(bfloat))
    query_all = [cores.spread(v) for v in chips.stack_done(query_line, mark)]
    query_part = plane_dot(
        lefts, sizes[0], sizes[1], query_all, [v[0].shape[1] for v in query_all]
    )
    query_sums = lax.psum_scatter(query_part, chips.names[0], scatter_dimension=0, tiled=True)
    low_all = cores.spread(jnp.concatenate(low_line, axis=0))
    small_part = add_up(hold(small_line, query_part))
    low_cols = grad_low.shape[1]
    spare = low_wide.shape[1] - low_cols - small_part.shape[1]
    fold = sizes[2] // kvb_part.shape[0]
    kvb_cols = kvb_part.shape[1] // fold
    small_wide = jnp.pad(small_part, ((0, 0), (0, spare)))
    low_part = plane_dot(
        lefts, 0, sizes[0], [low_all], [low_cols], fold, (kvb_part, small_wide)
    )
    low_line = chips.line_send(low_part)
    out_lines = chips.packs_one([tie(v, small_part) for v in out_packs])
    mark = shared_step([query_part, low_line[0]])
    mark, lines, (query_sums,) = visit(mark, [low_line, *out_lines], [query_sums])
    low_line, *out_lines = lines
    query_all = lax.all_gather(query_sums, chips.names, axis=0, tiled=True)
    low_line = chips.hop_line(add_up(low_line), 0)
    out_lines = chips.packs_two([add_up(v) for v in out_lines])
    waits = [v[0] for v in out_lines]
    mark = shared_step(waits + [low_line[0]])
    mark, lines, (part_all,) = visit(mark, [low_line, *out_lines], [part_all])
    low_line, *out_lines = lines
    low_all = in_order(low_line, chips.own(0), 0)
    low_line = chips.gather_one(chips.halves(low_all))
    totals = jnp.concatenate([add_up(v) for v in out_lines], axis=0)
    back_sums = [
        chips.back_first(totals[j * tok_rows : (j + 1) * tok_rows], j) for j in range(turns)
    ]
    mark = shared_step([v[0] for v in low_line] + back_sums[:1])
    mark, low_line, back_sums[1:] = visit(mark, low_line, back_sums[1:])
    low_line = chips.gather_two(low_line, mark)
    routed_out = back_sums[0].astype(single)
    for j in range(1, turns):
        routed_out = routed_out + tie(back_sums[j], mark).astype(single)
    result = mid + shared_out + routed_out
    mark = own_part(2, [mark])
    grad_egate = grads_of[0].T[None]
    grad_eup = grads_of[1].T[None]
    grad_edown = grads_of[2][None]
    grad_wout = in_rows(chips, tie(part_all, result))
    grad_wqb = in_rows(chips, tie(query_all, grad_wout))
    low_cuts = [kvb_cols, query_rank, low_cols - query_rank, small_part.shape[1] + spare]
    if len(chips.dims) == 3:
        low_line = [hold(v, grad_wqb, mark) for v in low_line]
        grad_wkvb, grad_wqa, grad_wkva, small = assemble(chips, low_line, low_cuts, fold, (2,))
        grad_wkva = grad_wkva.T
    else:
        low_all = chips.gather_done(low_line, mark).astype(single)
        kvb_all, grad_wqa, grad_wkva, small = split(low_all, low_cuts)
        kvb_all = kvb_all.reshape(chips.plane, fold, -1, kvb_cols)
        grad_wkvb = kvb_all.swapaxes(1, 2).reshape(-1, fold * kvb_cols)

    if shards == 2:
        grad_sgate, grad_sup, grad_sdown = shared_grads
    else:
        grad_sgate = grad_sup = grad_sdown = 0.0
        all_ffn, all_cot = chip_ffn, chip_cot
        for turn in range(shards):
            if turn > 0:
                tied = lax.optimization_barrier(
                    (all_ffn, all_cot, grad_sgate, grad_sup, grad_sdown)
                )
                grad_sgate, grad_sup, grad_sdown = tied[2:]
                all_ffn, all_cot = cores.along(tied[0], 1), cores.along(tied[1], 1)
            all_hidden, all_gate, all_up = feed_forward(
                all_ffn, all_cot, shared_gate, shared_up, shared_down
            )
            grad_sgate = grad_sgate + t_dot(all_ffn, all_gate)
            grad_sup = grad_sup + t_dot(all_ffn, all_up)
            grad_sdown = grad_sdown + t_dot(all_hidden, all_cot)
    query_part = gain_query.shape[0]
    return (
        result,
        grad_tokens,
        small[:, 0],
        small[:query_part, 2],
        small[query_part:, 2],
        small[:, 1],
        grad_wqa,
        grad_wqb,
        grad_wkva,
        grad_wkvb,
        grad_wout,
        small[:, 3 : 3 + experts_all],
        grad_sgate,
        grad_sup,
        grad_sdown,
        grad_egate,
        grad_eup,
        grad_edown,
    )


def solution(mesh):
    shards = mesh.shape["shard"]
    dims = grid_of(mesh.shape["expert"], shards)
    names = tuple(f"line{i}" for i in range(len(dims)))
    grid = jax.sharding.Mesh(mesh.devices.reshape(dims + (shards,)), names + ("shard",))
    chips = Chips(dims, names)
    both = names + ("shard",)
    in_specs = (
        P(both, None),
        P(names),
        P(both, None),
        P(both, None),
        P("shard"),
        P("shard"),
        P("shard"),
        P("shard"),
        P("shard", None),
        P("shard", None),
        P("shard", None),
        P("shard", None),
        P("shard", None),
        P("shard", None),
        P(None, "shard"),
        P(None, "shard"),
        P("shard", None),
        P(names, None, "shard"),
        P(names, None, "shard"),
        P(names, "shard", None),
    )
    out_specs = (
        P(both, None),
        P(both, None),
        P("shard"),
        P("shard"),
        P("shard"),
        P("shard"),
        P("shard", None),
        P("shard", None),
        P("shard", None),
        P("shard", None),
        P("shard", None),
        P("shard", None),
        P(None, "shard"),
        P(None, "shard"),
        P("shard", None),
        P(names, None, "shard"),
        P(names, None, "shard"),
        P(names, "shard", None),
    )

    def body(*args):
        return per_device(chips, shards, *args)

    return jax.shard_map(
        body, mesh=grid, in_specs=in_specs, out_specs=out_specs, check_vma=False
    )
```
